256 devices in a mesh: slab: 8 (over x, core), dir: 32 (over z, y).
Axes of the slice: x: 4, y: 4, z: 8, core: 2. Of those that a mesh axis runs over, the one named last changes fastest.
Arguments:
- currents: float32 [2, 512, 128, 256], P(None, ('slab', 'dir')), may hold values from -6 to 6
- near_blocks: float32 [2, 512, 9, 128, 128], P(None, ('slab', 'dir')), may hold values from -0.1875 to 0.1875
- near_index: int32 [512, 9], P(('slab', 'dir')), may hold values from 0 to 5
- aggregate: float32 [2, 256, 128], replicated, may hold values from -0.5 to 0.5
- translations: float32 [2, 64, 256], P(None, None, 'dir'), may hold values from -1 to 1
- inter_source: int32 [512, 32], P('slab'), may hold values from 0 to 191
- inter_shift: int32 [512, 32], P('slab'), may hold values from 0 to 63
- disaggregate: float32 [2, 128, 256], replicated, may hold values from -0.375 to 0.375
Outputs:
- product: float32 [2, 512, 128, 256], P(None, ('slab', 'dir'))
The draws below stay inside these ranges and needn't reach their ends.
All inputs are finite; a program needn't handle non-finite values.
Results may differ from the reference program's by a relative error of at most 0.0003.
Values sent between devices are 32-bit elements; how exact they have to be, the bound alone decides.
No kernel may reach another device: no remote copies, remote signals or barrier semaphores. Data moves between devices by JAX's collectives and lax.ppermute only.
A program may use at most 64 MiB of HBM per device.

```python
import jax
import jax.numpy as jnp
from jax import lax

P_SIZE = 128
K = 256
R = 256
BOX_DEV = 2
NN = 9
NI = 32
NT = 64
SLAB_BOXES = 64
BOXES = 512
N_SLAB = 8


def set_ends(drawn, stream_key, low, top_value):
    place = [jax.random.randint(jax.random.fold_in(stream_key, axis), (), 0, length) for axis, length in enumerate(drawn.shape)]
    widest = drawn.shape.index(max(drawn.shape))
    beside = place[:widest] + [(place[widest] + 1) % drawn.shape[widest]] + place[widest + 1:]
    return drawn.at[tuple(place)].set(low).at[tuple(beside)].set(top_value)


def block_scale(stream_key, extent, cuts, least, top_value):
    factor_of = 1.0
    for dim, blocks in cuts:
        steps = jax.random.uniform(jax.random.fold_in(jax.random.fold_in(stream_key, 6), dim), (blocks,), jnp.float32, least / len(cuts), top_value / len(cuts))
        factor_of = factor_of * jnp.repeat(jnp.exp(steps), extent[dim] // blocks).reshape((-1,) + (1,) * (len(extent) - 1 - dim))
    return factor_of


def centred(rng, dims, scale, reach, cuts=(), kind=jnp.bfloat16):
    entries = scale * jax.random.normal(rng, dims, jnp.float32)
    if cuts:
        entries = entries * block_scale(rng, dims, cuts, -0.22, 0.18)
    return jnp.clip(entries, -reach, reach).astype(kind)


def setup_inputs(seed: int = 0) -> dict:
    streams_of = jax.random.split(jax.random.key(seed), 9)
    return {
        "currents": centred(streams_of[0], (2, BOXES, P_SIZE, R), 1.0, 6.0, ((1, 256),), jnp.float32),
        "near_blocks": centred(streams_of[1], (2, BOXES, NN, P_SIZE, P_SIZE), (NN * P_SIZE) ** -0.5, 0.1875, ((1, 256),), jnp.float32),
        "near_index": set_ends(jax.random.randint(streams_of[2], (BOXES, NN), 0, 3 * BOX_DEV), jax.random.fold_in(streams_of[2], 1), 0, (3 * BOX_DEV) - 1).astype(jnp.int32),
        "aggregate": centred(streams_of[3], (2, K, P_SIZE), P_SIZE ** -0.5, 0.5, (), jnp.float32),
        "translations": centred(streams_of[4], (2, NT, K), 0.18, 1.0, ((2, 32),), jnp.float32),
        "inter_source": set_ends(jax.random.randint(streams_of[5], (BOXES, NI), 0, 3 * SLAB_BOXES), jax.random.fold_in(streams_of[5], 1), 0, (3 * SLAB_BOXES) - 1).astype(jnp.int32),
        "inter_shift": set_ends(jax.random.randint(streams_of[6], (BOXES, NI), 0, NT), jax.random.fold_in(streams_of[6], 1), 0, NT - 1).astype(jnp.int32),
        "disaggregate": centred(streams_of[7], (2, P_SIZE, K), K ** -0.5, 0.375, (), jnp.float32),
    }


def cein(form, left, right):
    def single(u, v):
        return jnp.einsum(form, u, v, precision=lax.Precision.HIGHEST)
    real = single(left[0], right[0]) - single(left[1], right[1])
    imag = single(left[0], right[1]) + single(left[1], right[0])
    return jnp.stack([real, imag])


def reference(currents, near_blocks, near_index, aggregate, translations, inter_source, inter_shift, disaggregate):
    def near_one(box):
        slab_id = box // SLAB_BOXES
        within = box % SLAB_BOXES
        device = within // BOX_DEV
        source = slab_id * SLAB_BOXES + (device * BOX_DEV - BOX_DEV + near_index[box] + SLAB_BOXES) % SLAB_BOXES
        pieces = jnp.take(currents, source.astype(jnp.int32), axis=1)
        blocks = jnp.take(near_blocks, box, axis=1)
        return cein('jpq,jqr->pr', blocks, pieces)

    near = lax.map(near_one, jnp.arange(BOXES, dtype=jnp.int32))
    near = jnp.transpose(near, (1, 0, 2, 3))
    radiated = cein('kp,bpr->bkr', aggregate, currents)
    zeros_rim = jnp.zeros((2, SLAB_BOXES, K, R), jnp.float32)
    padded = jnp.concatenate([zeros_rim, radiated, zeros_rim], axis=1)

    def far_slab(slab_id):
        start = (slab_id * SLAB_BOXES).astype(jnp.int32)
        local = lax.dynamic_slice_in_dim(padded, start, 3 * SLAB_BOXES, 1)
        sources = lax.dynamic_slice_in_dim(inter_source, start, SLAB_BOXES, 0)
        shifts = lax.dynamic_slice_in_dim(inter_shift, start, SLAB_BOXES, 0)

        def add_entry(entry, total):
            rows = jnp.take(local, sources[:, entry], axis=1)
            factor = jnp.take(translations, shifts[:, entry], axis=1)[:, :, :, None]
            real = factor[0] * rows[0] - factor[1] * rows[1]
            imag = factor[0] * rows[1] + factor[1] * rows[0]
            return total + jnp.stack([real, imag])

        incoming = lax.fori_loop(0, NI, add_entry, jnp.zeros((2, SLAB_BOXES, K, R), jnp.float32))
        return cein('pk,bkr->bpr', disaggregate, incoming)

    far = lax.map(far_slab, jnp.arange(N_SLAB, dtype=jnp.int32))
    far = jnp.transpose(far, (1, 0, 2, 3, 4)).reshape(2, BOXES, P_SIZE, R)
    return near + far
```

```python
import functools

import jax
import jax.numpy as jnp
from jax import lax
from jax.experimental import pallas as pl
from jax.experimental.pallas import tpu as pltpu
from jax.sharding import PartitionSpec as P

F32, BF16 = jnp.float32, jnp.bfloat16
VMEM = pltpu.MemorySpace.VMEM
SMEM = pltpu.MemorySpace.SMEM
MIB = 1 << 20


def split(x):
    high = x.astype(BF16)
    return high, (x - high.astype(F32)).astype(BF16)


def dot3(left, right, contract):
    def one(a, b):
        return lax.dot_general(a, b, (contract, ((), ())), preferred_element_type=F32)

    return one(left[0], right[0]) + (one(left[0], right[1]) + one(left[1], right[0]))


NN_FORM = ((1,), (0,))
NT_FORM = ((1,), (1,))


def pack_kernel(currents_ref, translations_ref, out_ref):
    devices, rows, lanes = out_ref.shape
    parts, boxes, _, illum = currents_ref.shape
    own = illum // devices
    for c in range(parts):
        for b in range(boxes):
            turned = currents_ref[c, b].T.reshape(devices, own, lanes)
            out_ref[:, pl.ds((c * boxes + b) * own, own), :] = turned
    table = jnp.concatenate([translations_ref[0], translations_ref[1]], axis=1)
    first = parts * boxes * own
    out_ref[:, first:, :] = jnp.broadcast_to(table[None], (devices, rows - first, lanes))


def near_kernel(index_ref, blocks_ref, own_ref, left_ref, right_ref, out_ref, high_ref, low_ref):
    boxes, entries = blocks_ref.shape[1], blocks_ref.shape[2]
    width = own_ref.shape[3]
    for place, ref in enumerate((left_ref, own_ref, right_ref)):
        for b in range(boxes):
            slot = place * boxes + b
            real, imag = split(ref[0, b]), split(ref[1, b])
            for store, x, y in ((high_ref, real[0], imag[0]), (low_ref, real[1], imag[1])):
                store[slot] = jnp.concatenate(
                    [jnp.concatenate([x, y], axis=1), jnp.concatenate([-y, x], axis=1)], axis=0
                )
    for b in range(boxes):

        def step(j, total):
            source = index_ref[b, j]
            block = split(jnp.concatenate([blocks_ref[0, b, j], blocks_ref[1, b, j]], axis=1))
            return total + dot3(block, (high_ref[source], low_ref[source]), NN_FORM)

        total = lax.fori_loop(0, entries, step, jnp.zeros((blocks_ref.shape[3], 2 * width), F32))
        out_ref[0, b] = total[:, :width]
        out_ref[1, b] = total[:, width:]


def radiate(block_ref, weights):
    devices, _, lanes = block_ref.shape
    real = block_ref[:, :16, :].reshape(devices * 16, lanes)
    imag = block_ref[:, 16:32, :].reshape(devices * 16, lanes)
    rows = jnp.concatenate([real, imag], axis=1)
    return dot3(split(rows), weights, NT_FORM)


def complex_rows(ref):
    real, imag = ref[0], ref[1]
    return jnp.concatenate(
        [jnp.concatenate([real, -imag], axis=1), jnp.concatenate([imag, real], axis=1)], axis=0
    )


def own_kernel(own_ref, aggregate_ref, radiated_ref, table_ref):
    boxes, sub, width = radiated_ref.shape
    radiated_ref[...] = radiate(own_ref, split(complex_rows(aggregate_ref))).reshape(boxes, sub, width)
    devices, rows, lanes = own_ref.shape
    table = own_ref[:, 32:, :].reshape(devices * (rows - 32), lanes).T
    half = lanes // 2
    wide = jnp.concatenate([table[:half], table[half:]], axis=1)
    table_ref[...] = jnp.broadcast_to(wide[:, None, :], table_ref.shape)


def far_kernel(
    source_ref, shift_ref, own_ref, table_ref, before_ref, after_ref, aggregate_ref, incoming_ref, radiated_ref
):
    boxes, sub, width = own_ref.shape
    entries = source_ref.shape[0]
    half = width // 2
    weights = split(complex_rows(aggregate_ref))
    radiated_ref[:boxes] = radiate(before_ref, weights).reshape(boxes, sub, width)
    radiated_ref[boxes : 2 * boxes] = own_ref[...]
    radiated_ref[2 * boxes :] = radiate(after_ref, weights).reshape(boxes, sub, width)

    def one_box(g, carry):
        real = jnp.zeros((sub, half), F32)
        imag = jnp.zeros((sub, half), F32)
        for i in range(entries):
            q, t = source_ref[i, g], shift_ref[i, g]
            xr, xi = radiated_ref[q, :, :half], radiated_ref[q, :, half:]
            tr, ti = table_ref[t, :, :half], table_ref[t, :, half:]
            real += tr * xr - ti * xi
            imag += tr * xi + ti * xr
        incoming_ref[g, :, :half] = real
        incoming_ref[g, :, half:] = imag
        return carry

    lax.fori_loop(0, boxes, one_box, 0)


def down_kernel(incoming_ref, disaggregate_ref, left_ref, right_ref, out_ref):
    boxes, sub, width = incoming_ref.shape
    far = dot3(
        split(incoming_ref[...].reshape(boxes * sub, width)), split(complex_rows(disaggregate_ref)), NT_FORM
    )
    devices, rows, lanes = out_ref.shape
    out_ref[:, : rows // 2, :] = far[:, :lanes].reshape(devices, rows // 2, lanes)
    out_ref[:, rows // 2 :, :] = far[:, lanes:].reshape(devices, rows // 2, lanes)


def join_kernel(far_ref, near_ref, out_ref):
    parts, boxes, lanes, illum = out_ref.shape
    devices = far_ref.shape[0]
    own = illum // devices
    for c in range(parts):
        for b in range(boxes):
            turned = far_ref[:, pl.ds((c * boxes + b) * own, own), :].reshape(illum, lanes)
            out_ref[c, b] = near_ref[c, b] + turned.T


def call(kernel, outs, kinds, scratch=(), limit=16, flops=0, name=None):
    specs = [pl.BlockSpec(memory_space=kind) for kind in kinds]

    def run(*args):
        moved = sum(a.size * 4 for a in args) + sum(o.size * 4 for o in jax.tree.leaves(outs))
        return pl.pallas_call(
            kernel,
            out_shape=outs,
            in_specs=specs,
            out_specs=jax.tree.map(lambda _: pl.BlockSpec(memory_space=VMEM), outs),
            scratch_shapes=list(scratch),
            compiler_params=pltpu.CompilerParams(vmem_limit_bytes=limit * MIB),
            cost_estimate=pl.CostEstimate(flops=flops, bytes_accessed=moved, transcendentals=0),
            name=name,
        )(*args)

    return run


def body(currents, near_blocks, near_index, aggregate, translations, inter_source, inter_shift, disaggregate):
    devices = lax.axis_size("dir")
    slabs = lax.axis_size("slab")
    parts, box_dev, unknowns, illum = currents.shape
    own = illum // devices
    directions = aggregate.shape[1]
    boxes = inter_source.shape[0]
    ops = translations.shape[1]
    ring = [(i, (i + 1) % devices) for i in range(devices)]
    line = [(i, i + 1) for i in range(slabs - 1)]
    rows = parts * box_dev * own
    packed = call(
        pack_kernel, jax.ShapeDtypeStruct((devices, rows + translations.shape[2], unknowns), F32), (VMEM, VMEM), name="pack"
    )(currents, jnp.transpose(translations, (0, 2, 1)))
    mine = lax.all_to_all(packed, "dir", 0, 0, tiled=True)
    before = lax.ppermute(mine, "slab", line)
    after = lax.ppermute(mine, "slab", [(j, i) for i, j in line])

    radiated, table = call(
        own_kernel,
        (
            jax.ShapeDtypeStruct((boxes, own, 2 * directions), F32),
            jax.ShapeDtypeStruct((ops, own, 2 * directions), F32),
        ),
        (VMEM, VMEM),
        flops=2 * 3 * 67_000_000,
        name="own",
    )(mine, aggregate)
    radiated, beside = lax.optimization_barrier((radiated, currents))
    left = lax.ppermute(beside, "dir", ring)
    right = lax.ppermute(beside, "dir", [(j, i) for i, j in ring])
    incoming = call(
        far_kernel,
        jax.ShapeDtypeStruct((boxes, own, 2 * directions), F32),
        (SMEM, SMEM) + (VMEM,) * 5,
        scratch=(pltpu.VMEM((3 * boxes, own, 2 * directions), F32),),
        limit=24,
        flops=2 * 3 * 200_000_000,
        name="far",
    )(inter_source.T, inter_shift.T, radiated, table, before, after, aggregate)
    far = call(
        down_kernel,
        jax.ShapeDtypeStruct((devices, rows, unknowns), F32),
        (VMEM, VMEM, pl.ANY, pl.ANY),
        flops=2 * 3 * 67_000_000,
        name="down",
    )(incoming, disaggregate, left, right)
    back = lax.all_to_all(far, "dir", 0, 0, tiled=True)

    near = call(
        near_kernel,
        jax.ShapeDtypeStruct(currents.shape, F32),
        (SMEM,) + (VMEM,) * 4,
        scratch=(
            pltpu.VMEM((3 * box_dev, 2 * unknowns, 2 * illum), BF16),
            pltpu.VMEM((3 * box_dev, 2 * unknowns, 2 * illum), BF16),
        ),
        limit=24,
        flops=2 * 3 * 302_000_000,
        name="near",
    )(near_index, near_blocks, currents, left, right)
    return call(join_kernel, jax.ShapeDtypeStruct(currents.shape, F32), (VMEM, VMEM), name="join")(back, near)


def solution(mesh):
    in_specs = (
        P(None, ("slab", "dir"), None, None),
        P(None, ("slab", "dir"), None, None, None),
        P(("slab", "dir"), None),
        P(),
        P(None, None, "dir"),
        P("slab", None),
        P("slab", None),
        P(),
    )
    out_specs = P(None, ("slab", "dir"), None, None)
    return jax.shard_map(body, mesh=mesh, in_specs=in_specs, out_specs=out_specs, check_vma=False)
```

```python
import functools

import jax
import jax.numpy as jnp
from jax import lax
from jax.experimental import pallas as pl
from jax.experimental.pallas import tpu as pltpu
from jax.sharding import PartitionSpec as P

F32, BF16 = jnp.float32, jnp.bfloat16
VMEM = pltpu.MemorySpace.VMEM
SMEM = pltpu.MemorySpace.SMEM
MIB = 1 << 20
RE_IM_ROWS = 32
GROUP = 4


def split(x):
    high = x.astype(BF16)
    return high, (x - high.astype(F32)).astype(BF16)


def dot3(left, right, contract):
    def one(a, b):
        return lax.dot_general(a, b, (contract, ((), ())), preferred_element_type=F32)

    return one(left[0], right[0]) + (one(left[0], right[1]) + one(left[1], right[0]))


NN_FORM = ((1,), (0,))
NT_FORM = ((1,), (1,))


def pack_kernel(currents_ref, translations_ref, out_ref):
    devices, rows, lanes = out_ref.shape
    parts, boxes, _, illum = currents_ref.shape
    own = illum // devices
    for c in range(parts):
        for b in range(boxes):
            turned = currents_ref[c, b].T.reshape(devices, own, lanes)
            out_ref[:, pl.ds((c * boxes + b) * own, own), :] = turned
    table = jnp.concatenate([translations_ref[0], translations_ref[1]], axis=1)
    first = parts * boxes * own
    out_ref[:, first:, :] = jnp.broadcast_to(table[None], (devices, rows - first, lanes))


def near_kernel(index_ref, blocks_ref, own_ref, left_ref, right_ref, out_ref, high_ref, low_ref):
    boxes, entries = blocks_ref.shape[1], blocks_ref.shape[2]
    width = own_ref.shape[3]
    for place, ref in enumerate((left_ref, own_ref, right_ref)):
        for b in range(boxes):
            slot = place * boxes + b
            real, imag = split(ref[0, b]), split(ref[1, b])
            for store, x, y in ((high_ref, real[0], imag[0]), (low_ref, real[1], imag[1])):
                store[slot] = jnp.concatenate(
                    [jnp.concatenate([x, y], axis=1), jnp.concatenate([-y, x], axis=1)], axis=0
                )
    for b in range(boxes):

        def step(j, total):
            source = index_ref[b, j]
            block = split(jnp.concatenate([blocks_ref[0, b, j], blocks_ref[1, b, j]], axis=1))
            return total + dot3(block, (high_ref[source], low_ref[source]), NN_FORM)

        total = lax.fori_loop(0, entries, step, jnp.zeros((blocks_ref.shape[3], 2 * width), F32))
        out_ref[0, b] = total[:, :width]
        out_ref[1, b] = total[:, width:]


def radiate(block_ref, weights):
    devices, rows, lanes = block_ref.shape
    half = RE_IM_ROWS // 2
    real = block_ref[:, :half, :].reshape(devices * half, lanes)
    imag = block_ref[:, half : 2 * half, :].reshape(devices * half, lanes)
    return dot3(split(jnp.concatenate([real, imag], axis=1)), weights, NT_FORM)


def complex_rows(ref):
    real, imag = ref[0], ref[1]
    return jnp.concatenate(
        [jnp.concatenate([real, -imag], axis=1), jnp.concatenate([imag, real], axis=1)], axis=0
    )


def plan_kernel(source_ref, shift_ref, first_ref, source2_ref, shift2_ref, count_ref):
    entries, boxes = source_ref.shape
    odd = lax.axis_index("slab") % 2
    source, shift = source_ref[...], shift_ref[...]
    part, place = source // boxes, source % boxes
    away = part == 2 * odd
    first_ref[...] = jnp.where(part == 1, place, jnp.where(away, 2 * boxes, boxes + place))
    one = away.astype(jnp.int32)
    position = jnp.zeros((1, boxes), jnp.int32)
    row = lax.broadcasted_iota(jnp.int32, (entries, boxes), 0)
    moved_source = jnp.zeros((entries, boxes), jnp.int32)
    moved_shift = jnp.zeros((entries, boxes), jnp.int32)
    for i in range(entries):
        here = (row == position) & (one[i : i + 1] == 1)
        moved_source = jnp.where(here, place[i : i + 1], moved_source)
        moved_shift = jnp.where(here, shift[i : i + 1], moved_shift)
        position = position + one[i : i + 1]
    source2_ref[...] = jnp.where(row < position, moved_source, boxes)
    shift2_ref[...] = moved_shift
    count_ref[...] = jnp.broadcast_to((position + (GROUP - 1)) // GROUP, count_ref.shape)


def own_kernel(own_ref, aggregate_ref, disaggregate_ref, radiated_ref, table_ref, up0_ref, up1_ref, down0_ref, down1_ref):
    boxes, sub, width = radiated_ref.shape
    up = split(complex_rows(aggregate_ref))
    up0_ref[...], up1_ref[...] = up
    down0_ref[...], down1_ref[...] = split(complex_rows(disaggregate_ref))
    radiated_ref[...] = radiate(own_ref, up).reshape(boxes, sub, width)
    devices, rows, lanes = own_ref.shape
    table = own_ref[:, RE_IM_ROWS:, :].reshape(devices * (rows - RE_IM_ROWS), lanes).T
    half = lanes // 2
    wide = jnp.concatenate([table[:half], table[half:]], axis=1)
    table_ref[...] = jnp.broadcast_to(wide[:, None, :], table_ref.shape)


def add_entry(total, radiated_ref, q, table_ref, t):
    half = table_ref.shape[2] // 2
    xr, xi = radiated_ref[q, :, :half], radiated_ref[q, :, half:]
    tr, ti = table_ref[t, :, :half], table_ref[t, :, half:]
    return total[0] + (tr * xr - ti * xi), total[1] + (tr * xi + ti * xr)


def mid_kernel(
    source_ref, shift_ref, own_ref, table_ref, block_ref, up0_ref, up1_ref, out_ref, radiated_ref
):
    boxes, sub, width = own_ref.shape
    half = width // 2
    radiated_ref[:boxes] = own_ref[...]
    radiated_ref[boxes : 2 * boxes] = radiate(block_ref, (up0_ref[...], up1_ref[...])).reshape(boxes, sub, width)
    radiated_ref[2 * boxes] = jnp.zeros((sub, width), F32)

    def one_box(g, carry):
        total = (jnp.zeros((sub, half), F32), jnp.zeros((sub, half), F32))
        for i in range(source_ref.shape[0]):
            total = add_entry(total, radiated_ref, source_ref[i, g], table_ref, shift_ref[i, g])
        out_ref[g, :, :half], out_ref[g, :, half:] = total
        return carry

    lax.fori_loop(0, boxes, one_box, 0)


def far_kernel(
    source_ref, shift_ref, count_ref, mid_ref, table_ref, block_ref, up0_ref, up1_ref, down0_ref, down1_ref,
    out_ref, radiated_ref, incoming_ref,
):
    boxes, sub, width = mid_ref.shape
    half = width // 2
    radiated_ref[:boxes] = radiate(block_ref, (up0_ref[...], up1_ref[...])).reshape(boxes, sub, width)
    radiated_ref[boxes] = jnp.zeros((sub, width), F32)

    def one_box(g, carry):
        def group(n, total):
            for i in range(GROUP):
                e = n * GROUP + i
                total = add_entry(total, radiated_ref, source_ref[e, g], table_ref, shift_ref[e, g])
            return total

        total = lax.fori_loop(0, count_ref[0, g], group, (mid_ref[g, :, :half], mid_ref[g, :, half:]))
        incoming_ref[g, :, :half], incoming_ref[g, :, half:] = total
        return carry

    lax.fori_loop(0, boxes, one_box, 0)
    far = dot3(split(incoming_ref[...].reshape(boxes * sub, width)), (down0_ref[...], down1_ref[...]), NT_FORM)
    devices, rows, lanes = out_ref.shape
    out_ref[:, : rows // 2, :] = far[:, :lanes].reshape(devices, rows // 2, lanes)
    out_ref[:, rows // 2 :, :] = far[:, lanes:].reshape(devices, rows // 2, lanes)


def join_kernel(far_ref, near_ref, out_ref):
    parts, boxes, lanes, illum = out_ref.shape
    devices = far_ref.shape[0]
    own = illum // devices
    for c in range(parts):
        for b in range(boxes):
            turned = far_ref[:, pl.ds((c * boxes + b) * own, own), :].reshape(illum, lanes)
            out_ref[c, b] = near_ref[c, b] + turned.T


def call(kernel, outs, kinds, scratch=(), limit=16, micros=1, name=None):
    specs = [pl.BlockSpec(memory_space=kind) for kind in kinds]

    def run(*args):
        return pl.pallas_call(
            kernel,
            out_shape=outs,
            in_specs=specs,
            out_specs=jax.tree.map(lambda _: pl.BlockSpec(memory_space=VMEM), outs),
            scratch_shapes=list(scratch),
            compiler_params=pltpu.CompilerParams(vmem_limit_bytes=limit * MIB),
            cost_estimate=pl.CostEstimate(flops=micros * 1_000_000_000, bytes_accessed=0, transcendentals=0),
            name=name,
        )(*args)

    return run


def shape(*dims, kind=F32):
    return jax.ShapeDtypeStruct(dims, kind)


def body(currents, near_blocks, near_index, aggregate, translations, inter_source, inter_shift, disaggregate):
    devices = lax.axis_size("dir")
    slabs = lax.axis_size("slab")
    parts, box_dev, unknowns, illum = currents.shape
    own = illum // devices
    width = 2 * aggregate.shape[1]
    boxes, entries = inter_source.shape
    ops = translations.shape[1]
    rows = parts * box_dev * own
    ring = [(i, (i + 1) % devices) for i in range(devices)]
    pairs_of = [[(i, i + 1) for i in range(start, slabs - 1, 2)] for start in (0, 1)]
    same, cross = [p + [(j, i) for i, j in p] for p in pairs_of]

    packed = call(pack_kernel, shape(devices, rows + translations.shape[2], unknowns), (VMEM, VMEM), name="pack")(
        currents, jnp.transpose(translations, (0, 2, 1))
    )
    mine = lax.all_to_all(packed, "dir", 0, 0, tiled=True)
    index = shape(entries, boxes, kind=jnp.int32)
    first, source2, shift2, count = call(
        plan_kernel, (index, index, index, shape(8, boxes, kind=jnp.int32)), (VMEM, VMEM), name="plan"
    )(inter_source.T, inter_shift.T)
    mine, beside, first, source2, shift2, count = lax.optimization_barrier(
        (mine, currents, first, source2, shift2, count)
    )
    sent = mine[:, :rows]
    from_cross = lax.ppermute(sent, "slab", cross)
    from_same = lax.ppermute(sent, "slab", same)
    left = lax.ppermute(beside, "dir", ring)
    right = lax.ppermute(beside, "dir", [(j, i) for i, j in ring])
    field = shape(boxes, own, width)
    up, down = shape(width, 2 * unknowns, kind=BF16), shape(2 * unknowns, width, kind=BF16)
    radiated, table, up0, up1, down0, down1 = call(
        own_kernel, (field, shape(ops, own, width), up, up, down, down), (VMEM,) * 3, name="own"
    )(mine, aggregate, disaggregate)
    partial = call(
        mid_kernel,
        field,
        (SMEM, SMEM) + (VMEM,) * 5,
        scratch=(pltpu.VMEM((2 * boxes + 1, own, width), F32),),
        micros=6,
        name="mid",
    )(first, inter_shift.T, radiated, table, from_same, up0, up1)
    far = call(
        far_kernel,
        shape(devices, rows, unknowns),
        (SMEM,) * 3 + (VMEM,) * 7,
        scratch=(pltpu.VMEM((boxes + 1, own, width), F32), pltpu.VMEM((boxes, own, width), F32)),
        micros=5,
        name="far",
    )(source2, shift2, count, partial, table, from_cross, up0, up1, down0, down1)
    back = lax.all_to_all(far, "dir", 0, 0, tiled=True)

    stack = pltpu.VMEM((3 * box_dev, 2 * unknowns, 2 * illum), BF16)
    near = call(
        near_kernel, shape(*currents.shape), (SMEM,) + (VMEM,) * 4, scratch=(stack, stack), micros=20, name="near"
    )(near_index, near_blocks, currents, left, right)
    return call(join_kernel, shape(*currents.shape), (VMEM, VMEM), name="join")(back, near)


def solution(mesh):
    in_specs = (
        P(None, ("slab", "dir"), None, None),
        P(None, ("slab", "dir"), None, None, None),
        P(("slab", "dir"), None),
        P(),
        P(None, None, "dir"),
        P("slab", None),
        P("slab", None),
        P(),
    )
    out_specs = P(None, ("slab", "dir"), None, None)
    return jax.shard_map(body, mesh=mesh, in_specs=in_specs, out_specs=out_specs, check_vma=False)
```

```python
import functools

import jax
import jax.numpy as jnp
from jax import lax
from jax.experimental import pallas as pl
from jax.experimental.pallas import tpu as pltpu
from jax.sharding import PartitionSpec as P

F32, BF16 = jnp.float32, jnp.bfloat16
VMEM = pltpu.MemorySpace.VMEM
SMEM = pltpu.MemorySpace.SMEM
MIB = 1 << 20
RE_IM_ROWS = 32
EARLY, LATE = 24, 14
LIST_ROWS = 8


def split(x):
    high = x.astype(BF16)
    return high, (x - high.astype(F32)).astype(BF16)


def dot3(left, right, contract):
    def one(a, b):
        return lax.dot_general(a, b, (contract, ((), ())), preferred_element_type=F32)

    return one(left[0], right[0]) + (one(left[0], right[1]) + one(left[1], right[0]))


NN_FORM = ((1,), (0,))
NT_FORM = ((1,), (1,))


def pack_kernel(currents_ref, translations_ref, out_ref):
    devices, rows, lanes = out_ref.shape
    parts, boxes, _, illum = currents_ref.shape
    own = illum // devices
    for c in range(parts):
        for b in range(boxes):
            turned = currents_ref[c, b].T.reshape(devices, own, lanes)
            out_ref[:, pl.ds((c * boxes + b) * own, own), :] = turned
    table = jnp.concatenate([translations_ref[0], translations_ref[1]], axis=1)
    first = parts * boxes * own
    out_ref[:, first:, :] = jnp.broadcast_to(table[None], (devices, rows - first, lanes))


def near_kernel(index_ref, blocks_ref, own_ref, left_ref, right_ref, out_ref, high_ref, low_ref):
    boxes, entries = blocks_ref.shape[1], blocks_ref.shape[2]
    width = own_ref.shape[3]
    for place, ref in enumerate((left_ref, own_ref, right_ref)):
        for b in range(boxes):
            slot = place * boxes + b
            real, imag = split(ref[0, b]), split(ref[1, b])
            for store, x, y in ((high_ref, real[0], imag[0]), (low_ref, real[1], imag[1])):
                store[slot] = jnp.concatenate(
                    [jnp.concatenate([x, y], axis=1), jnp.concatenate([-y, x], axis=1)], axis=0
                )
    for b in range(boxes):

        def step(j, total):
            source = index_ref[b, j]
            block = split(jnp.concatenate([blocks_ref[0, b, j], blocks_ref[1, b, j]], axis=1))
            return total + dot3(block, (high_ref[source], low_ref[source]), NN_FORM)

        total = lax.fori_loop(0, entries, step, jnp.zeros((blocks_ref.shape[3], 2 * width), F32))
        out_ref[0, b] = total[:, :width]
        out_ref[1, b] = total[:, width:]


def radiate(block_ref, weights):
    devices, rows, lanes = block_ref.shape
    half = RE_IM_ROWS // 2
    real = block_ref[:, :half, :].reshape(devices * half, lanes)
    imag = block_ref[:, half : 2 * half, :].reshape(devices * half, lanes)
    return dot3(split(jnp.concatenate([real, imag], axis=1)), weights, NT_FORM)


def complex_rows(ref):
    real, imag = ref[0], ref[1]
    return jnp.concatenate(
        [jnp.concatenate([real, -imag], axis=1), jnp.concatenate([imag, real], axis=1)], axis=0
    )


def plan_kernel(source_ref, shift_ref, early_ref, late_ref):
    entries, boxes = source_ref.shape
    odd = lax.axis_index("slab") % 2
    source, shift = source_ref[...], shift_ref[...]
    part, place = source // boxes, source % boxes
    away = part == 2 * odd
    row = lax.broadcasted_iota(jnp.int32, (entries, boxes), 0)
    for ref, chosen, where, zeros in (
        (early_ref, jnp.logical_not(away), jnp.where(part == 1, place, boxes + place), 2 * boxes),
        (late_ref, away, place, boxes),
    ):
        one = chosen.astype(jnp.int32)
        count = jnp.zeros((1, boxes), jnp.int32)
        front_where = jnp.full((entries, boxes), zeros, jnp.int32)
        front_shift = jnp.zeros((entries, boxes), jnp.int32)
        for i in range(entries):
            here = (row == count) & (one[i : i + 1] == 1)
            front_where = jnp.where(here, where[i : i + 1], front_where)
            front_shift = jnp.where(here, shift[i : i + 1], front_shift)
            count = count + one[i : i + 1]
        ref[...] = jnp.zeros(ref.shape, jnp.int32)
        ref[:entries, :boxes] = front_where
        ref[entries : 2 * entries, :boxes] = front_shift
        ref[2 * entries :, :boxes] = jnp.broadcast_to(count, (ref.shape[0] - 2 * entries, boxes))


def own_kernel(own_ref, aggregate_ref, disaggregate_ref, radiated_ref, table_ref, up0_ref, up1_ref, down0_ref, down1_ref):
    boxes, sub, width = radiated_ref.shape
    up = split(complex_rows(aggregate_ref))
    up0_ref[...], up1_ref[...] = up
    down0_ref[...], down1_ref[...] = split(complex_rows(disaggregate_ref))
    radiated_ref[...] = radiate(own_ref, up).reshape(boxes, sub, width)
    devices, rows, lanes = own_ref.shape
    table = own_ref[:, RE_IM_ROWS:, :].reshape(devices * (rows - RE_IM_ROWS), lanes).T
    half = lanes // 2
    wide = jnp.concatenate([table[:half], table[half:]], axis=1)
    table_ref[...] = jnp.broadcast_to(wide[:, None, :], table_ref.shape)


def add_entries(list_ref, g, numbers, total, radiated_ref, table_ref):
    entries = list_ref.shape[0] // 2 - LIST_ROWS // 2
    half = table_ref.shape[2] // 2
    real, imag = total
    for n in numbers:
        q, t = list_ref[n, g], list_ref[entries + n, g]
        xr, xi = radiated_ref[q, :, :half], radiated_ref[q, :, half:]
        tr, ti = table_ref[t, :, :half], table_ref[t, :, half:]
        real, imag = real + (tr * xr - ti * xi), imag + (tr * xi + ti * xr)
    return real, imag


def add_all(list_ref, fixed, start, out_ref, radiated_ref, table_ref):
    entries = list_ref.shape[0] // 2 - LIST_ROWS // 2
    half = table_ref.shape[2] // 2

    def one_box(g, carry):
        total = add_entries(list_ref, g, range(fixed), start(g), radiated_ref, table_ref)
        out_ref[g, :, :half], out_ref[g, :, half:] = total
        count = list_ref[2 * entries, g]

        @pl.when(count > fixed)
        def _():
            def rest(n, total):
                return add_entries(list_ref, g, (n,), total, radiated_ref, table_ref)

            both = lax.fori_loop(fixed, count, rest, (out_ref[g, :, :half], out_ref[g, :, half:]))
            out_ref[g, :, :half], out_ref[g, :, half:] = both

        return carry

    lax.fori_loop(0, out_ref.shape[0], one_box, 0)


def mid_kernel(
    lists_ref, own_ref, table_ref, block_ref, up0_ref, up1_ref, out_ref, radiated_ref, list_ref, sem
):
    staged = pltpu.make_async_copy(lists_ref, list_ref, sem)
    staged.start()
    boxes, sub, width = own_ref.shape
    radiated_ref[:boxes] = own_ref[...]
    radiated_ref[boxes : 2 * boxes] = radiate(block_ref, (up0_ref[...], up1_ref[...])).reshape(boxes, sub, width)
    radiated_ref[2 * boxes] = jnp.zeros((sub, width), F32)
    staged.wait()
    nothing = jnp.zeros((sub, width // 2), F32)
    add_all(list_ref, EARLY, lambda g: (nothing, nothing), out_ref, radiated_ref, table_ref)


def far_kernel(
    lists_ref, mid_ref, table_ref, block_ref, up0_ref, up1_ref, down0_ref, down1_ref, out_ref, radiated_ref,
    incoming_ref, list_ref, sem,
):
    staged = pltpu.make_async_copy(lists_ref, list_ref, sem)
    staged.start()
    boxes, sub, width = mid_ref.shape
    half = width // 2
    radiated_ref[:boxes] = radiate(block_ref, (up0_ref[...], up1_ref[...])).reshape(boxes, sub, width)
    radiated_ref[boxes] = jnp.zeros((sub, width), F32)
    staged.wait()
    add_all(
        list_ref, LATE, lambda g: (mid_ref[g, :, :half], mid_ref[g, :, half:]), incoming_ref, radiated_ref, table_ref
    )
    far = dot3(split(incoming_ref[...].reshape(boxes * sub, width)), (down0_ref[...], down1_ref[...]), NT_FORM)
    devices, rows, lanes = out_ref.shape
    out_ref[:, : rows // 2, :] = far[:, :lanes].reshape(devices, rows // 2, lanes)
    out_ref[:, rows // 2 :, :] = far[:, lanes:].reshape(devices, rows // 2, lanes)


def join_kernel(far_ref, near_ref, out_ref):
    parts, boxes, lanes, illum = out_ref.shape
    devices = far_ref.shape[0]
    own = illum // devices
    for c in range(parts):
        for b in range(boxes):
            turned = far_ref[:, pl.ds((c * boxes + b) * own, own), :].reshape(illum, lanes)
            out_ref[c, b] = near_ref[c, b] + turned.T


def call(kernel, outs, kinds, scratch=(), limit=16, micros=1, name=None):
    specs = [pl.BlockSpec(memory_space=kind) for kind in kinds]

    def run(*args):
        return pl.pallas_call(
            kernel,
            out_shape=outs,
            in_specs=specs,
            out_specs=jax.tree.map(lambda _: pl.BlockSpec(memory_space=VMEM), outs),
            scratch_shapes=list(scratch),
            compiler_params=pltpu.CompilerParams(vmem_limit_bytes=limit * MIB),
            cost_estimate=pl.CostEstimate(flops=micros * 1_000_000_000, bytes_accessed=0, transcendentals=0),
            name=name,
        )(*args)

    return run


def shape(*dims, kind=F32):
    return jax.ShapeDtypeStruct(dims, kind)


def body(currents, near_blocks, near_index, aggregate, translations, inter_source, inter_shift, disaggregate):
    devices = lax.axis_size("dir")
    slabs = lax.axis_size("slab")
    parts, box_dev, unknowns, illum = currents.shape
    own = illum // devices
    width = 2 * aggregate.shape[1]
    boxes, entries = inter_source.shape
    ops = translations.shape[1]
    rows = parts * box_dev * own
    ring = [(i, (i + 1) % devices) for i in range(devices)]
    pairs_of = [[(i, i + 1) for i in range(start, slabs - 1, 2)] for start in (0, 1)]
    same, cross = [p + [(j, i) for i, j in p] for p in pairs_of]

    packed = call(pack_kernel, shape(devices, rows + translations.shape[2], unknowns), (VMEM, VMEM), name="pack")(
        currents, jnp.transpose(translations, (0, 2, 1))
    )
    mine = lax.all_to_all(packed, "dir", 0, 0, tiled=True)
    lists = shape(2 * entries + LIST_ROWS, 128, kind=jnp.int32)
    early, late = call(plan_kernel, (lists, lists), (VMEM, VMEM), name="plan")(inter_source.T, inter_shift.T)
    mine, beside, early, late = lax.optimization_barrier((mine, currents, early, late))
    sent = mine[:, :rows]
    from_cross = lax.ppermute(sent, "slab", cross)
    from_same = lax.ppermute(sent, "slab", same)
    left = lax.ppermute(beside, "dir", ring)
    right = lax.ppermute(beside, "dir", [(j, i) for i, j in ring])
    field = shape(boxes, own, width)
    up, down = shape(width, 2 * unknowns, kind=BF16), shape(2 * unknowns, width, kind=BF16)
    radiated, table, up0, up1, down0, down1 = call(
        own_kernel, (field, shape(ops, own, width), up, up, down, down), (VMEM,) * 3, name="own"
    )(mine, aggregate, disaggregate)
    staging = (pltpu.SMEM(lists.shape, jnp.int32), pltpu.SemaphoreType.DMA)
    partial = call(
        mid_kernel,
        field,
        (VMEM,) * 6,
        scratch=(pltpu.VMEM((2 * boxes + 1, own, width), F32), *staging),
        micros=6,
        name="mid",
    )(early, radiated, table, from_same, up0, up1)
    far = call(
        far_kernel,
        shape(devices, rows, unknowns),
        (VMEM,) * 8,
        scratch=(pltpu.VMEM((boxes + 1, own, width), F32), pltpu.VMEM((boxes, own, width), F32), *staging),
        micros=5,
        name="far",
    )(late, partial, table, from_cross, up0, up1, down0, down1)
    back = lax.all_to_all(far, "dir", 0, 0, tiled=True)

    stack = pltpu.VMEM((3 * box_dev, 2 * unknowns, 2 * illum), BF16)
    near = call(
        near_kernel, shape(*currents.shape), (SMEM,) + (VMEM,) * 4, scratch=(stack, stack), micros=20, name="near"
    )(near_index, near_blocks, currents, left, right)
    return call(join_kernel, shape(*currents.shape), (VMEM, VMEM), name="join")(back, near)


def solution(mesh):
    in_specs = (
        P(None, ("slab", "dir"), None, None),
        P(None, ("slab", "dir"), None, None, None),
        P(("slab", "dir"), None),
        P(),
        P(None, None, "dir"),
        P("slab", None),
        P("slab", None),
        P(),
    )
    out_specs = P(None, ("slab", "dir"), None, None)
    return jax.shard_map(body, mesh=mesh, in_specs=in_specs, out_specs=out_specs, check_vma=False)
```

```python
import functools

import jax
import jax.numpy as jnp
from jax import lax
from jax.experimental import pallas as pl
from jax.experimental.pallas import tpu as pltpu
from jax.sharding import PartitionSpec as P

F32, BF16 = jnp.float32, jnp.bfloat16
VMEM = pltpu.MemorySpace.VMEM
SMEM = pltpu.MemorySpace.SMEM
ANY = pl.ANY
MIB = 1 << 20
RE_IM_ROWS = 32
EARLY, LATE = 26, 14
LIST_ROWS = 8
FULL = 63


def split(x):
    high = x.astype(BF16)
    return high, (x - high.astype(F32)).astype(BF16)


def dot3(left, right, contract):
    def one(a, b):
        return lax.dot_general(a, b, (contract, ((), ())), preferred_element_type=F32)

    return one(left[0], right[0]) + (one(left[0], right[1]) + one(left[1], right[0]))


NN_FORM = ((1,), (0,))
NT_FORM = ((1,), (1,))


def pack_kernel(currents_ref, translations_ref, out_ref, block_ref, table_ref, packed_ref, in_sem, out_sem):
    devices, rows, lanes = out_ref.shape
    parts, boxes, _, illum = currents_ref.shape
    own = illum // devices
    pieces = [(c, b) for c in range(parts) for b in range(boxes)]
    last = len(pieces)
    loads = [pltpu.make_async_copy(currents_ref.at[c, b], block_ref.at[n], in_sem.at[n]) for n, (c, b) in enumerate(pieces)]
    loads.append(pltpu.make_async_copy(translations_ref, table_ref, in_sem.at[last]))
    stores = [
        pltpu.make_async_copy(packed_ref.at[:, pl.ds(n * own, own), :], out_ref.at[:, pl.ds(n * own, own), :], out_sem.at[n])
        for n in range(last + 1)
    ]
    for load in loads:
        load.start()
    for n in range(last):
        loads[n].wait()
        packed_ref[:, n * own : (n + 1) * own, :] = block_ref[n].T.reshape(devices, own, lanes)
        stores[n].start()
    loads[last].wait()
    table = jnp.concatenate([table_ref[0], table_ref[1]], axis=1)
    packed_ref[:, last * own :, :] = jnp.broadcast_to(table[None], (devices, own, lanes))
    stores[last].start()
    for store in stores:
        store.wait()


def near_kernel(index_ref, blocks_ref, own_ref, left_ref, right_ref, out_ref, high_ref, low_ref):
    boxes, entries = blocks_ref.shape[1], blocks_ref.shape[2]
    width = own_ref.shape[3]
    for place, ref in enumerate((left_ref, own_ref, right_ref)):
        for b in range(boxes):
            slot = place * boxes + b
            real, imag = split(ref[0, b]), split(ref[1, b])
            for store, x, y in ((high_ref, real[0], imag[0]), (low_ref, real[1], imag[1])):
                store[slot] = jnp.concatenate(
                    [jnp.concatenate([x, y], axis=1), jnp.concatenate([-y, x], axis=1)], axis=0
                )
    for b in range(boxes):

        def step(j, total):
            source = index_ref[b, j]
            block = split(jnp.concatenate([blocks_ref[0, b, j], blocks_ref[1, b, j]], axis=1))
            return total + dot3(block, (high_ref[source], low_ref[source]), NN_FORM)

        total = lax.fori_loop(0, entries, step, jnp.zeros((blocks_ref.shape[3], 2 * width), F32))
        out_ref[0, b] = total[:, :width]
        out_ref[1, b] = total[:, width:]


def radiate(block_ref, weights):
    devices, rows, lanes = block_ref.shape
    half = RE_IM_ROWS // 2
    real = block_ref[:, :half, :].reshape(devices * half, lanes)
    imag = block_ref[:, half : 2 * half, :].reshape(devices * half, lanes)
    return dot3(split(jnp.concatenate([real, imag], axis=1)), weights, NT_FORM)


def complex_rows(ref):
    real, imag = ref[0], ref[1]
    return jnp.concatenate(
        [jnp.concatenate([real, -imag], axis=1), jnp.concatenate([imag, real], axis=1)], axis=0
    )


def plan_kernel(source_ref, shift_ref, early_ref, late_ref):
    entries, boxes = source_ref.shape
    odd = lax.axis_index("slab") % 2
    source, shift = source_ref[...], shift_ref[...]
    part, place = source // boxes, source % boxes
    away = part == 2 * odd
    row = lax.broadcasted_iota(jnp.int32, (entries, boxes), 0)
    for ref, chosen, where, zeros in (
        (early_ref, jnp.logical_not(away), jnp.where(part == 1, place, boxes + place), 2 * boxes),
        (late_ref, away, place, boxes),
    ):
        one = chosen.astype(jnp.int32)
        count = jnp.zeros((1, boxes), jnp.int32)
        front_where = jnp.full((entries, boxes), zeros, jnp.int32)
        front_shift = jnp.zeros((entries, boxes), jnp.int32)
        for i in range(entries):
            here = (row == count) & (one[i : i + 1] == 1)
            front_where = jnp.where(here, where[i : i + 1], front_where)
            front_shift = jnp.where(here, shift[i : i + 1], front_shift)
            count = count + one[i : i + 1]
        ref[...] = jnp.zeros(ref.shape, jnp.int32)
        ref[:entries, :boxes] = front_where
        ref[entries : 2 * entries, :boxes] = front_shift
        ref[2 * entries :, :boxes] = jnp.broadcast_to(count, (ref.shape[0] - 2 * entries, boxes))


def own_kernel(own_ref, aggregate_ref, disaggregate_ref, radiated_ref, table_ref, up0_ref, up1_ref, down0_ref, down1_ref):
    boxes, sub, width = radiated_ref.shape
    up = split(complex_rows(aggregate_ref))
    up0_ref[...], up1_ref[...] = up
    down0_ref[...], down1_ref[...] = split(complex_rows(disaggregate_ref))
    radiated_ref[...] = radiate(own_ref, up).reshape(boxes, sub, width)
    devices, rows, lanes = own_ref.shape
    table = own_ref[:, RE_IM_ROWS:, :].reshape(devices * (rows - RE_IM_ROWS), lanes).T
    half = lanes // 2
    wide = jnp.concatenate([table[:half], table[half:]], axis=1)
    table_ref[...] = jnp.broadcast_to(wide[:, None, :], table_ref.shape)


def add_entries(list_ref, g, numbers, total, radiated_ref, table_ref):
    entries = list_ref.shape[0] // 2 - LIST_ROWS // 2
    half = table_ref.shape[2] // 2
    real, imag = total
    for n in numbers:
        q, t = list_ref[n, g], list_ref[entries + n, g]
        xr, xi = radiated_ref[q, :, :half], radiated_ref[q, :, half:]
        tr, ti = table_ref[t, :, :half], table_ref[t, :, half:]
        real, imag = real + (tr * xr - ti * xi), imag + (tr * xi + ti * xr)
    return real, imag


def add_all(list_ref, fixed, start, out_ref, radiated_ref, table_ref):
    entries = list_ref.shape[0] // 2 - LIST_ROWS // 2
    half = table_ref.shape[2] // 2

    def one_box(g, carry):
        total = add_entries(list_ref, g, range(fixed), start(g), radiated_ref, table_ref)
        out_ref[g, :, :half], out_ref[g, :, half:] = total
        return carry

    def beyond(g, carry):
        count = list_ref[2 * entries, g]

        @pl.when(count > fixed)
        def _():
            def rest(n, total):
                return add_entries(list_ref, g, (n,), total, radiated_ref, table_ref)

            both = lax.fori_loop(fixed, count, rest, (out_ref[g, :, :half], out_ref[g, :, half:]))
            out_ref[g, :, :half], out_ref[g, :, half:] = both

        return carry

    lax.fori_loop(0, out_ref.shape[0], one_box, 0, unroll=2)
    lax.fori_loop(0, out_ref.shape[0], beyond, 0)


def mid_kernel(
    lists_ref, own_ref, table_ref, block_ref, up0_ref, up1_ref, out_ref, radiated_ref, list_ref, sem
):
    staged = pltpu.make_async_copy(lists_ref, list_ref, sem)
    staged.start()
    boxes, sub, width = own_ref.shape
    radiated_ref[:boxes] = own_ref[...]
    radiated_ref[boxes : 2 * boxes] = radiate(block_ref, (up0_ref[...], up1_ref[...])).reshape(boxes, sub, width)
    radiated_ref[2 * boxes] = jnp.zeros((sub, width), F32)
    staged.wait()
    nothing = jnp.zeros((sub, width // 2), F32)
    add_all(list_ref, EARLY, lambda g: (nothing, nothing), out_ref, radiated_ref, table_ref)


def far_kernel(
    lists_ref, mid_ref, table_ref, block_ref, up0_ref, up1_ref, down0_ref, down1_ref, out_ref, radiated_ref,
    incoming_ref, list_ref, sem,
):
    staged = pltpu.make_async_copy(lists_ref, list_ref, sem)
    staged.start()
    boxes, sub, width = mid_ref.shape
    half = width // 2
    radiated_ref[:boxes] = radiate(block_ref, (up0_ref[...], up1_ref[...])).reshape(boxes, sub, width)
    radiated_ref[boxes] = jnp.zeros((sub, width), F32)
    staged.wait()
    add_all(
        list_ref, LATE, lambda g: (mid_ref[g, :, :half], mid_ref[g, :, half:]), incoming_ref, radiated_ref, table_ref
    )
    far = dot3(split(incoming_ref[...].reshape(boxes * sub, width)), (down0_ref[...], down1_ref[...]), NT_FORM)
    devices, rows, lanes = out_ref.shape
    out_ref[:, : rows // 2, :] = far[:, :lanes].reshape(devices, rows // 2, lanes)
    out_ref[:, rows // 2 :, :] = far[:, lanes:].reshape(devices, rows // 2, lanes)


def join_kernel(far_ref, near_ref, out_ref, rows_ref, block_ref, sum_ref, far_sem, near_sem, out_sem):
    parts, boxes, lanes, illum = out_ref.shape
    devices = far_ref.shape[0]
    own = illum // devices
    pieces = [(c, b) for c in range(parts) for b in range(boxes)]
    loads = []
    for n, (c, b) in enumerate(pieces):
        loads.append(pltpu.make_async_copy(far_ref.at[:, pl.ds(n * own, own), :], rows_ref.at[n], far_sem.at[n]))
        loads.append(pltpu.make_async_copy(near_ref.at[c, b], block_ref.at[n], near_sem.at[n]))
    stores = [pltpu.make_async_copy(sum_ref.at[n], out_ref.at[c, b], out_sem.at[n]) for n, (c, b) in enumerate(pieces)]
    for load in loads:
        load.start()
    for n in range(len(pieces)):
        loads[2 * n].wait()
        turned = rows_ref[n].reshape(illum, lanes).T
        loads[2 * n + 1].wait()
        sum_ref[n] = block_ref[n] + turned
        stores[n].start()
    for store in stores:
        store.wait()


def call(kernel, outs, kinds, scratch=(), limit=16, micros=1, name=None, out_kind=VMEM):
    specs = [pl.BlockSpec(memory_space=kind) for kind in kinds]

    def run(*args):
        return pl.pallas_call(
            kernel,
            out_shape=outs,
            in_specs=specs,
            out_specs=jax.tree.map(lambda _: pl.BlockSpec(memory_space=out_kind), outs),
            scratch_shapes=list(scratch),
            compiler_params=pltpu.CompilerParams(vmem_limit_bytes=limit * MIB),
            cost_estimate=pl.CostEstimate(flops=micros * 1_000_000_000, bytes_accessed=0, transcendentals=0),
            name=name,
        )(*args)

    return run


def shape(*dims, kind=F32):
    return jax.ShapeDtypeStruct(dims, kind)


def body(currents, near_blocks, near_index, aggregate, translations, inter_source, inter_shift, disaggregate):
    devices = lax.axis_size("dir")
    slabs = lax.axis_size("slab")
    parts, box_dev, unknowns, illum = currents.shape
    own = illum // devices
    width = 2 * aggregate.shape[1]
    boxes, entries = inter_source.shape
    ops = translations.shape[1]
    rows = parts * box_dev * own
    ring = [(i, (i + 1) % devices) for i in range(devices)]
    pairs_of = [[(i, i + 1) for i in range(start, slabs - 1, 2)] for start in (0, 1)]
    same, cross = [p + [(j, i) for i, j in p] for p in pairs_of]

    turned = jnp.transpose(translations, (0, 2, 1))
    pieces = parts * box_dev
    blocks = pltpu.VMEM((pieces, unknowns, illum), F32)
    whole = shape(devices, rows + turned.shape[1], unknowns)
    packed = call(
        pack_kernel,
        whole,
        (ANY, ANY),
        scratch=(
            blocks,
            pltpu.VMEM(turned.shape, F32),
            pltpu.VMEM(whole.shape, F32),
            pltpu.SemaphoreType.DMA((pieces + 1,)),
            pltpu.SemaphoreType.DMA((pieces + 1,)),
        ),
        limit=FULL,
        name="pack",
        out_kind=ANY,
    )(currents, turned)
    mine = lax.all_to_all(packed, "dir", 0, 0, tiled=True)
    lists = shape(2 * entries + LIST_ROWS, 128, kind=jnp.int32)
    early, late = call(plan_kernel, (lists, lists), (VMEM, VMEM), name="plan")(inter_source.T, inter_shift.T)
    mine, beside, early, late = lax.optimization_barrier((mine, currents, early, late))
    sent = mine[:, :rows]
    from_cross = lax.ppermute(sent, "slab", cross)
    from_same = lax.ppermute(sent, "slab", same)
    left = lax.ppermute(beside, "dir", ring)
    right = lax.ppermute(beside, "dir", [(j, i) for i, j in ring])
    field = shape(boxes, own, width)
    up, down = shape(width, 2 * unknowns, kind=BF16), shape(2 * unknowns, width, kind=BF16)
    radiated, table, up0, up1, down0, down1 = call(
        own_kernel, (field, shape(ops, own, width), up, up, down, down), (VMEM,) * 3, name="own"
    )(mine, aggregate, disaggregate)
    staging = (pltpu.SMEM(lists.shape, jnp.int32), pltpu.SemaphoreType.DMA)
    partial = call(
        mid_kernel,
        field,
        (VMEM,) * 6,
        scratch=(pltpu.VMEM((2 * boxes + 1, own, width), F32), *staging),
        micros=6,
        name="mid",
    )(early, radiated, table, from_same, up0, up1)
    far = call(
        far_kernel,
        shape(devices, rows, unknowns),
        (VMEM,) * 8,
        scratch=(pltpu.VMEM((boxes + 1, own, width), F32), pltpu.VMEM((boxes, own, width), F32), *staging),
        micros=5,
        name="far",
    )(late, partial, table, from_cross, up0, up1, down0, down1)
    back = lax.all_to_all(far, "dir", 0, 0, tiled=True)

    stack = pltpu.VMEM((3 * box_dev, 2 * unknowns, 2 * illum), BF16)
    near = call(
        near_kernel, shape(*currents.shape), (SMEM,) + (VMEM,) * 4, scratch=(stack, stack), micros=20, name="near"
    )(near_index, near_blocks, currents, left, right)
    return call(
        join_kernel,
        shape(*currents.shape),
        (ANY, ANY),
        scratch=(pltpu.VMEM((pieces, devices, own, unknowns), F32), blocks, blocks, *(pltpu.SemaphoreType.DMA((pieces,)),) * 3),
        limit=FULL,
        name="join",
        out_kind=ANY,
    )(back, near)


def solution(mesh):
    in_specs = (
        P(None, ("slab", "dir"), None, None),
        P(None, ("slab", "dir"), None, None, None),
        P(("slab", "dir"), None),
        P(),
        P(None, None, "dir"),
        P("slab", None),
        P("slab", None),
        P(),
    )
    out_specs = P(None, ("slab", "dir"), None, None)
    return jax.shard_map(body, mesh=mesh, in_specs=in_specs, out_specs=out_specs, check_vma=False)
```

```python
import functools

import jax
import jax.numpy as jnp
from jax import lax
from jax.experimental import pallas as pl
from jax.experimental.pallas import tpu as pltpu
from jax.sharding import PartitionSpec as P

F32, BF16 = jnp.float32, jnp.bfloat16
VMEM = pltpu.MemorySpace.VMEM
SMEM = pltpu.MemorySpace.SMEM
ANY = pl.ANY
MIB = 1 << 20
RE_IM_ROWS = 32
EARLY, LATE = 25, 15
LIST_ROWS = 8
FULL = 63


def split(x):
    high = x.astype(BF16)
    return high, (x - high.astype(F32)).astype(BF16)


def dot3(left, right, contract):
    def one(a, b):
        return lax.dot_general(a, b, (contract, ((), ())), preferred_element_type=F32)

    return one(left[0], right[0]) + (one(left[0], right[1]) + one(left[1], right[0]))


NN_FORM = ((1,), (0,))
NT_FORM = ((1,), (1,))


def pack_kernel(currents_ref, translations_ref, out_ref, block_ref, table_ref, packed_ref, in_sem, out_sem):
    devices, rows, lanes = out_ref.shape
    parts, boxes, _, illum = currents_ref.shape
    own = illum // devices
    pieces = [(c, b) for c in range(parts) for b in range(boxes)]
    last = len(pieces)
    loads = [pltpu.make_async_copy(currents_ref.at[c, b], block_ref.at[n], in_sem.at[n]) for n, (c, b) in enumerate(pieces)]
    loads.append(pltpu.make_async_copy(translations_ref, table_ref, in_sem.at[last]))
    stores = [
        pltpu.make_async_copy(packed_ref.at[:, pl.ds(n * own, own), :], out_ref.at[:, pl.ds(n * own, own), :], out_sem.at[n])
        for n in range(last + 1)
    ]
    for load in loads:
        load.start()
    for n in range(last):
        loads[n].wait()
        packed_ref[:, n * own : (n + 1) * own, :] = block_ref[n].T.reshape(devices, own, lanes)
        stores[n].start()
    loads[last].wait()
    table = jnp.concatenate([table_ref[0], table_ref[1]], axis=1)
    packed_ref[:, last * own :, :] = jnp.broadcast_to(table[None], (devices, own, lanes))
    stores[last].start()
    for store in stores:
        store.wait()


def near_kernel(index_ref, blocks_ref, own_ref, left_ref, right_ref, out_ref, high_ref, low_ref):
    boxes, entries = blocks_ref.shape[1], blocks_ref.shape[2]
    width = own_ref.shape[3]
    for place, ref in enumerate((left_ref, own_ref, right_ref)):
        for b in range(boxes):
            slot = place * boxes + b
            real, imag = split(ref[0, b]), split(ref[1, b])
            for store, x, y in ((high_ref, real[0], imag[0]), (low_ref, real[1], imag[1])):
                store[slot] = jnp.concatenate(
                    [jnp.concatenate([x, y], axis=1), jnp.concatenate([-y, x], axis=1)], axis=0
                )
    for b in range(boxes):

        def step(j, total):
            source = index_ref[b, j]
            block = split(jnp.concatenate([blocks_ref[0, b, j], blocks_ref[1, b, j]], axis=1))
            return total + dot3(block, (high_ref[source], low_ref[source]), NN_FORM)

        total = lax.fori_loop(0, entries, step, jnp.zeros((blocks_ref.shape[3], 2 * width), F32))
        out_ref[0, b] = total[:, :width]
        out_ref[1, b] = total[:, width:]


def radiate(block_ref, weights):
    devices, rows, lanes = block_ref.shape
    half = RE_IM_ROWS // 2
    real = block_ref[:, :half, :].reshape(devices * half, lanes)
    imag = block_ref[:, half : 2 * half, :].reshape(devices * half, lanes)
    return dot3(split(jnp.concatenate([real, imag], axis=1)), weights, NT_FORM)


def complex_rows(ref):
    real, imag = ref[0], ref[1]
    return jnp.concatenate(
        [jnp.concatenate([real, -imag], axis=1), jnp.concatenate([imag, real], axis=1)], axis=0
    )


def plan_kernel(source_ref, shift_ref, early_ref, late_ref):
    entries, boxes = source_ref.shape
    odd = lax.axis_index("slab") % 2
    source, shift = source_ref[...], shift_ref[...]
    part, place = source // boxes, source % boxes
    away = part == 2 * odd
    row = lax.broadcasted_iota(jnp.int32, (entries, boxes), 0)
    across = [lax.broadcasted_iota(jnp.int32, (boxes, boxes), n) for n in range(2)]
    before, same = (across[1] < across[0]).astype(F32), (across[1] == across[0]).astype(F32)
    slot = lax.broadcasted_iota(jnp.int32, (boxes, early_ref.shape[1]), 1).astype(F32)
    for ref, fixed, chosen, where, zeros in (
        (early_ref, EARLY, jnp.logical_not(away), jnp.where(part == 1, place, boxes + place), 2 * boxes),
        (late_ref, LATE, away, place, boxes),
    ):
        one = chosen.astype(jnp.int32)
        count = jnp.zeros((1, boxes), jnp.int32)
        front_where = jnp.full((entries, boxes), zeros, jnp.int32)
        front_shift = jnp.zeros((entries, boxes), jnp.int32)
        for i in range(entries):
            here = (row == count) & (one[i : i + 1] == 1)
            front_where = jnp.where(here, where[i : i + 1], front_where)
            front_shift = jnp.where(here, shift[i : i + 1], front_shift)
            count = count + one[i : i + 1]
        ref[...] = jnp.zeros(ref.shape, jnp.int32)
        ref[:entries, :boxes] = front_where
        ref[entries : 2 * entries, :boxes] = front_shift
        ref[2 * entries : 2 * entries + 1, :boxes] = count
        more = jnp.broadcast_to((count > fixed).astype(F32), (8, boxes))
        rank = lax.dot_general(before, more, (NT_FORM, ((), ())), preferred_element_type=F32)[:, :1]
        flag = lax.dot_general(same, more, (NT_FORM, ((), ())), preferred_element_type=F32)[:, :1]
        box = lax.broadcasted_iota(jnp.int32, slot.shape, 0).astype(F32)
        chosen_box = jnp.where((slot == rank) & (flag > 0.5), box, 0.0)
        ref[2 * entries + 1 : 2 * entries + 2, :] = jnp.sum(chosen_box, axis=0, keepdims=True).astype(jnp.int32)
        total = jnp.sum(more, axis=1, keepdims=True)[:1]
        ref[2 * entries + 2 : 2 * entries + 3, :] = jnp.broadcast_to(total, (1, ref.shape[1])).astype(jnp.int32)


def own_kernel(own_ref, aggregate_ref, disaggregate_ref, radiated_ref, table_ref, up0_ref, up1_ref, down0_ref, down1_ref):
    boxes, sub, width = radiated_ref.shape
    up = split(complex_rows(aggregate_ref))
    up0_ref[...], up1_ref[...] = up
    down0_ref[...], down1_ref[...] = split(complex_rows(disaggregate_ref))
    radiated_ref[...] = radiate(own_ref, up).reshape(boxes, sub, width)
    devices, rows, lanes = own_ref.shape
    table = own_ref[:, RE_IM_ROWS:, :].reshape(devices * (rows - RE_IM_ROWS), lanes).T
    half = lanes // 2
    wide = jnp.concatenate([table[:half], table[half:]], axis=1)
    table_ref[...] = jnp.broadcast_to(wide[:, None, :], table_ref.shape)


def add_entries(list_ref, g, numbers, total, radiated_ref, table_ref):
    entries = list_ref.shape[0] // 2 - LIST_ROWS // 2
    half = table_ref.shape[2] // 2
    real, imag = total
    for n in numbers:
        q, t = list_ref[n, g], list_ref[entries + n, g]
        xr, xi = radiated_ref[q, :, :half], radiated_ref[q, :, half:]
        tr, ti = table_ref[t, :, :half], table_ref[t, :, half:]
        real, imag = real + (tr * xr - ti * xi), imag + (tr * xi + ti * xr)
    return real, imag


def add_all(list_ref, fixed, start, out_ref, radiated_ref, table_ref):
    entries = list_ref.shape[0] // 2 - LIST_ROWS // 2
    half = table_ref.shape[2] // 2

    def one_box(g, carry):
        total = add_entries(list_ref, g, range(fixed), start(g), radiated_ref, table_ref)
        out_ref[g, :, :half], out_ref[g, :, half:] = total
        return carry

    def beyond(place, carry):
        g = list_ref[2 * entries + 1, place]

        def rest(n, total):
            return add_entries(list_ref, g, (n,), total, radiated_ref, table_ref)

        both = lax.fori_loop(fixed, list_ref[2 * entries, g], rest, (out_ref[g, :, :half], out_ref[g, :, half:]))
        out_ref[g, :, :half], out_ref[g, :, half:] = both
        return carry

    lax.fori_loop(0, out_ref.shape[0], one_box, 0, unroll=4)
    lax.fori_loop(0, list_ref[2 * entries + 2, 0], beyond, 0)


def mid_kernel(
    lists_ref, own_ref, table_ref, block_ref, up0_ref, up1_ref, out_ref, radiated_ref, list_ref, sem
):
    staged = pltpu.make_async_copy(lists_ref, list_ref, sem)
    staged.start()
    boxes, sub, width = own_ref.shape
    radiated_ref[:boxes] = own_ref[...]
    radiated_ref[boxes : 2 * boxes] = radiate(block_ref, (up0_ref[...], up1_ref[...])).reshape(boxes, sub, width)
    radiated_ref[2 * boxes] = jnp.zeros((sub, width), F32)
    staged.wait()
    nothing = jnp.zeros((sub, width // 2), F32)
    add_all(list_ref, EARLY, lambda g: (nothing, nothing), out_ref, radiated_ref, table_ref)


def far_kernel(
    lists_ref, mid_ref, table_ref, block_ref, up0_ref, up1_ref, down0_ref, down1_ref, out_ref, radiated_ref,
    incoming_ref, list_ref, sem,
):
    staged = pltpu.make_async_copy(lists_ref, list_ref, sem)
    staged.start()
    boxes, sub, width = mid_ref.shape
    half = width // 2
    radiated_ref[:boxes] = radiate(block_ref, (up0_ref[...], up1_ref[...])).reshape(boxes, sub, width)
    radiated_ref[boxes] = jnp.zeros((sub, width), F32)
    staged.wait()
    add_all(
        list_ref, LATE, lambda g: (mid_ref[g, :, :half], mid_ref[g, :, half:]), incoming_ref, radiated_ref, table_ref
    )
    far = dot3(split(incoming_ref[...].reshape(boxes * sub, width)), (down0_ref[...], down1_ref[...]), NT_FORM)
    devices, rows, lanes = out_ref.shape
    out_ref[:, : rows // 2, :] = far[:, :lanes].reshape(devices, rows // 2, lanes)
    out_ref[:, rows // 2 :, :] = far[:, lanes:].reshape(devices, rows // 2, lanes)


def join_kernel(far_ref, near_ref, out_ref, rows_ref, block_ref, sum_ref, far_sem, near_sem, out_sem):
    parts, boxes, lanes, illum = out_ref.shape
    devices = far_ref.shape[0]
    own = illum // devices
    pieces = [(c, b) for c in range(parts) for b in range(boxes)]
    halves = [pl.ds(h * (devices // 2), devices // 2) for h in range(2)]
    arrive = [pltpu.make_async_copy(far_ref.at[half], rows_ref.at[half], far_sem.at[h]) for h, half in enumerate(halves)]
    loads = [pltpu.make_async_copy(near_ref.at[c, b], block_ref.at[n], near_sem.at[n]) for n, (c, b) in enumerate(pieces)]
    stores = [pltpu.make_async_copy(sum_ref.at[n], out_ref.at[c, b], out_sem.at[n]) for n, (c, b) in enumerate(pieces)]
    for copy in arrive + loads:
        copy.start()
    for h, half in enumerate(halves):
        arrive[h].wait()
        columns = slice(h * (illum // 2), (h + 1) * (illum // 2))
        for n in range(len(pieces)):
            turned = rows_ref[half, n * own : (n + 1) * own, :].reshape(illum // 2, lanes).T
            if h == 0:
                loads[n].wait()
            sum_ref[n, :, columns] = block_ref[n, :, columns] + turned
            if h == 1:
                stores[n].start()
    for store in stores:
        store.wait()


def call(kernel, outs, kinds, scratch=(), limit=16, micros=1, name=None, out_kind=VMEM):
    specs = [pl.BlockSpec(memory_space=kind) for kind in kinds]

    def run(*args):
        moved = 4 * sum(a.size for a in (*args, *jax.tree.leaves(outs)))
        return pl.pallas_call(
            kernel,
            out_shape=outs,
            in_specs=specs,
            out_specs=jax.tree.map(lambda _: pl.BlockSpec(memory_space=out_kind), outs),
            scratch_shapes=list(scratch),
            compiler_params=pltpu.CompilerParams(vmem_limit_bytes=limit * MIB),
            cost_estimate=pl.CostEstimate(flops=micros * 1_000_000_000, bytes_accessed=moved, transcendentals=0),
            name=name,
        )(*args)

    return run


def shape(*dims, kind=F32):
    return jax.ShapeDtypeStruct(dims, kind)


def body(currents, near_blocks, near_index, aggregate, translations, inter_source, inter_shift, disaggregate):
    devices = lax.axis_size("dir")
    slabs = lax.axis_size("slab")
    parts, box_dev, unknowns, illum = currents.shape
    own = illum // devices
    width = 2 * aggregate.shape[1]
    boxes, entries = inter_source.shape
    ops = translations.shape[1]
    rows = parts * box_dev * own
    ring = [(i, (i + 1) % devices) for i in range(devices)]
    pairs_of = [[(i, i + 1) for i in range(start, slabs - 1, 2)] for start in (0, 1)]
    same, cross = [p + [(j, i) for i, j in p] for p in pairs_of]

    turned = jnp.transpose(translations, (0, 2, 1))
    pieces = parts * box_dev
    blocks = pltpu.VMEM((pieces, unknowns, illum), F32)
    whole = shape(devices, rows + turned.shape[1], unknowns)
    packed = call(
        pack_kernel,
        whole,
        (ANY, ANY),
        scratch=(
            blocks,
            pltpu.VMEM(turned.shape, F32),
            pltpu.VMEM(whole.shape, F32),
            pltpu.SemaphoreType.DMA((pieces + 1,)),
            pltpu.SemaphoreType.DMA((pieces + 1,)),
        ),
        limit=FULL,
        name="pack",
        out_kind=ANY,
    )(currents, turned)
    mine = lax.all_to_all(packed, "dir", 0, 0, tiled=True)
    lists = shape(2 * entries + LIST_ROWS, 128, kind=jnp.int32)
    early, late = call(plan_kernel, (lists, lists), (VMEM, VMEM), name="plan")(inter_source.T, inter_shift.T)
    mine, beside, early, late = lax.optimization_barrier((mine, currents, early, late))
    sent = mine[:, :rows]
    from_cross = lax.ppermute(sent, "slab", cross)
    from_same = lax.ppermute(sent, "slab", same)
    left = lax.ppermute(beside, "dir", ring)
    right = lax.ppermute(beside, "dir", [(j, i) for i, j in ring])
    field = shape(boxes, own, width)
    up, down = shape(width, 2 * unknowns, kind=BF16), shape(2 * unknowns, width, kind=BF16)
    radiated, table, up0, up1, down0, down1 = call(
        own_kernel, (field, shape(ops, own, width), up, up, down, down), (VMEM,) * 3, name="own"
    )(mine, aggregate, disaggregate)
    staging = (pltpu.SMEM(lists.shape, jnp.int32), pltpu.SemaphoreType.DMA)
    partial = call(
        mid_kernel,
        field,
        (VMEM,) * 6,
        scratch=(pltpu.VMEM((2 * boxes + 1, own, width), F32), *staging),
        micros=6,
        name="mid",
    )(early, radiated, table, from_same, up0, up1)
    far = call(
        far_kernel,
        shape(devices, rows, unknowns),
        (VMEM,) * 8,
        scratch=(pltpu.VMEM((boxes + 1, own, width), F32), pltpu.VMEM((boxes, own, width), F32), *staging),
        micros=5,
        name="far",
    )(late, partial, table, from_cross, up0, up1, down0, down1)
    back = lax.all_to_all(far, "dir", 0, 0, tiled=True)

    stack = pltpu.VMEM((3 * box_dev, 2 * unknowns, 2 * illum), BF16)
    near = call(
        near_kernel, shape(*currents.shape), (SMEM,) + (VMEM,) * 4, scratch=(stack, stack), micros=20, name="near"
    )(near_index, near_blocks, currents, left, right)
    return call(
        join_kernel,
        shape(*currents.shape),
        (ANY, ANY),
        scratch=(
            pltpu.VMEM(far.shape, F32),
            blocks,
            blocks,
            pltpu.SemaphoreType.DMA((2,)),
            pltpu.SemaphoreType.DMA((pieces,)),
            pltpu.SemaphoreType.DMA((pieces,)),
        ),
        limit=FULL,
        name="join",
        out_kind=ANY,
    )(back, near)


def solution(mesh):
    in_specs = (
        P(None, ("slab", "dir"), None, None),
        P(None, ("slab", "dir"), None, None, None),
        P(("slab", "dir"), None),
        P(),
        P(None, None, "dir"),
        P("slab", None),
        P("slab", None),
        P(),
    )
    out_specs = P(None, ("slab", "dir"), None, None)
    return jax.shard_map(body, mesh=mesh, in_specs=in_specs, out_specs=out_specs, check_vma=False)
```

```python
import functools

import jax
import jax.numpy as jnp
from jax import lax
from jax.experimental import pallas as pl
from jax.experimental.pallas import tpu as pltpu
from jax.sharding import PartitionSpec as P

F32, BF16 = jnp.float32, jnp.bfloat16
VMEM = pltpu.MemorySpace.VMEM
SMEM = pltpu.MemorySpace.SMEM
ANY = pl.ANY
MIB = 1 << 20
RE_IM_ROWS = 32
EARLY, LATE = 25, 15
LIST_ROWS = 8
FULL = 63


def split(x):
    high = x.astype(BF16)
    return high, (x - high.astype(F32)).astype(BF16)


def dot3(left, right, contract):
    def one(a, b):
        return lax.dot_general(a, b, (contract, ((), ())), preferred_element_type=F32)

    return one(left[0], right[0]) + (one(left[0], right[1]) + one(left[1], right[0]))


NN_FORM = ((1,), (0,))
NT_FORM = ((1,), (1,))


def pack_kernel(currents_ref, translations_ref, out_ref, block_ref, table_ref, packed_ref, in_sem, out_sem):
    devices, rows, lanes = out_ref.shape
    parts, boxes, _, illum = currents_ref.shape
    own = illum // devices
    pieces = [(c, b) for c in range(parts) for b in range(boxes)]
    last = len(pieces)
    loads = [pltpu.make_async_copy(currents_ref.at[c, b], block_ref.at[n], in_sem.at[n]) for n, (c, b) in enumerate(pieces)]
    loads.append(pltpu.make_async_copy(translations_ref, table_ref, in_sem.at[last]))
    stores = [
        pltpu.make_async_copy(packed_ref.at[:, pl.ds(n * own, own), :], out_ref.at[:, pl.ds(n * own, own), :], out_sem.at[n])
        for n in range(last + 1)
    ]
    for load in loads:
        load.start()
    for n in range(last):
        loads[n].wait()
        packed_ref[:, n * own : (n + 1) * own, :] = block_ref[n].T.reshape(devices, own, lanes)
        stores[n].start()
    loads[last].wait()
    table = jnp.concatenate([table_ref[0], table_ref[1]], axis=1)
    packed_ref[:, last * own :, :] = jnp.broadcast_to(table[None], (devices, own, lanes))
    stores[last].start()
    for store in stores:
        store.wait()


def near_kernel(index_ref, blocks_ref, own_ref, left_ref, right_ref, out_ref, high_ref, low_ref):
    boxes, entries = blocks_ref.shape[1], blocks_ref.shape[2]
    width = own_ref.shape[3]
    for place, ref in enumerate((left_ref, own_ref, right_ref)):
        for b in range(boxes):
            slot = place * boxes + b
            real, imag = split(ref[0, b]), split(ref[1, b])
            for store, x, y in ((high_ref, real[0], imag[0]), (low_ref, real[1], imag[1])):
                store[slot] = jnp.concatenate(
                    [jnp.concatenate([x, y], axis=1), jnp.concatenate([-y, x], axis=1)], axis=0
                )
    for b in range(boxes):

        def step(j, total):
            source = index_ref[b, j]
            block = split(jnp.concatenate([blocks_ref[0, b, j], blocks_ref[1, b, j]], axis=1))
            return total + dot3(block, (high_ref[source], low_ref[source]), NN_FORM)

        total = lax.fori_loop(0, entries, step, jnp.zeros((blocks_ref.shape[3], 2 * width), F32))
        out_ref[0, b] = total[:, :width]
        out_ref[1, b] = total[:, width:]


def radiate(block_ref, weights):
    devices, rows, lanes = block_ref.shape
    half = RE_IM_ROWS // 2
    real = block_ref[:, :half, :].reshape(devices * half, lanes)
    imag = block_ref[:, half : 2 * half, :].reshape(devices * half, lanes)
    return dot3(split(jnp.concatenate([real, imag], axis=1)), weights, NT_FORM)


def complex_rows(ref):
    real, imag = ref[0], ref[1]
    return jnp.concatenate(
        [jnp.concatenate([real, -imag], axis=1), jnp.concatenate([imag, real], axis=1)], axis=0
    )


def plan_kernel(source_ref, shift_ref, early_ref, late_ref):
    entries, boxes = source_ref.shape
    odd = lax.axis_index("slab") % 2
    source, shift = source_ref[...], shift_ref[...]
    part, place = source // boxes, source % boxes
    away = part == 2 * odd
    row = lax.broadcasted_iota(jnp.int32, (entries, boxes), 0)
    across = [lax.broadcasted_iota(jnp.int32, (boxes, boxes), n) for n in range(2)]
    before, same = (across[1] < across[0]).astype(F32), (across[1] == across[0]).astype(F32)
    slot = lax.broadcasted_iota(jnp.int32, (boxes, early_ref.shape[1]), 1).astype(F32)
    for ref, fixed, chosen, where, zeros in (
        (early_ref, EARLY, jnp.logical_not(away), jnp.where(part == 1, place, boxes + place), 2 * boxes),
        (late_ref, LATE, away, place, boxes),
    ):
        one = chosen.astype(jnp.int32)
        count = jnp.zeros((1, boxes), jnp.int32)
        front_where = jnp.full((entries, boxes), zeros, jnp.int32)
        front_shift = jnp.zeros((entries, boxes), jnp.int32)
        for i in range(entries):
            here = (row == count) & (one[i : i + 1] == 1)
            front_where = jnp.where(here, where[i : i + 1], front_where)
            front_shift = jnp.where(here, shift[i : i + 1], front_shift)
            count = count + one[i : i + 1]
        ref[...] = jnp.zeros(ref.shape, jnp.int32)
        ref[:entries, :boxes] = front_where
        ref[entries : 2 * entries, :boxes] = front_shift
        ref[2 * entries : 2 * entries + 1, :boxes] = count
        more = jnp.broadcast_to((count > fixed).astype(F32), (8, boxes))
        rank = lax.dot_general(before, more, (NT_FORM, ((), ())), preferred_element_type=F32)[:, :1]
        flag = lax.dot_general(same, more, (NT_FORM, ((), ())), preferred_element_type=F32)[:, :1]
        box = lax.broadcasted_iota(jnp.int32, slot.shape, 0).astype(F32)
        chosen_box = jnp.where((slot == rank) & (flag > 0.5), box, 0.0)
        ref[2 * entries + 1 : 2 * entries + 2, :] = jnp.sum(chosen_box, axis=0, keepdims=True).astype(jnp.int32)
        total = jnp.sum(more, axis=1, keepdims=True)[:1]
        ref[2 * entries + 2 : 2 * entries + 3, :] = jnp.broadcast_to(total, (1, ref.shape[1])).astype(jnp.int32)


def own_kernel(own_ref, aggregate_ref, disaggregate_ref, radiated_ref, table_ref, up0_ref, up1_ref, down0_ref, down1_ref):
    boxes, sub, width = radiated_ref.shape
    up = split(complex_rows(aggregate_ref))
    up0_ref[...], up1_ref[...] = up
    down0_ref[...], down1_ref[...] = split(complex_rows(disaggregate_ref))
    radiated_ref[...] = radiate(own_ref, up).reshape(boxes, sub, width)
    devices, rows, lanes = own_ref.shape
    table = own_ref[:, RE_IM_ROWS:, :].reshape(devices * (rows - RE_IM_ROWS), lanes).T
    half = lanes // 2
    wide = jnp.concatenate([table[:half], table[half:]], axis=1)
    table_ref[...] = jnp.broadcast_to(wide[:, None, :], table_ref.shape)


def add_entries(list_ref, g, numbers, total, radiated_ref, table_ref):
    entries = list_ref.shape[0] // 2 - LIST_ROWS // 2
    half = table_ref.shape[2] // 2
    real, imag = total
    for n in numbers:
        q, t = list_ref[n, g], list_ref[entries + n, g]
        xr, xi = radiated_ref[q, :, :half], radiated_ref[q, :, half:]
        tr, ti = table_ref[t, :, :half], table_ref[t, :, half:]
        real, imag = real + (tr * xr - ti * xi), imag + (tr * xi + ti * xr)
    return real, imag


def add_all(list_ref, fixed, start, out_ref, radiated_ref, table_ref):
    entries = list_ref.shape[0] // 2 - LIST_ROWS // 2
    half = table_ref.shape[2] // 2

    def one_box(g, carry):
        total = add_entries(list_ref, g, range(fixed), start(g), radiated_ref, table_ref)
        out_ref[g, :, :half], out_ref[g, :, half:] = total
        return carry

    def beyond(place, carry):
        g = list_ref[2 * entries + 1, place]

        def rest(n, total):
            return add_entries(list_ref, g, (n,), total, radiated_ref, table_ref)

        both = lax.fori_loop(fixed, list_ref[2 * entries, g], rest, (out_ref[g, :, :half], out_ref[g, :, half:]))
        out_ref[g, :, :half], out_ref[g, :, half:] = both
        return carry

    lax.fori_loop(0, out_ref.shape[0], one_box, 0, unroll=4)
    lax.fori_loop(0, list_ref[2 * entries + 2, 0], beyond, 0)


def mid_kernel(
    lists_ref, own_ref, table_ref, block_ref, up0_ref, up1_ref, out_ref, radiated_ref, list_ref, sem
):
    staged = pltpu.make_async_copy(lists_ref, list_ref, sem)
    staged.start()
    boxes, sub, width = own_ref.shape
    radiated_ref[:boxes] = own_ref[...]
    radiated_ref[boxes : 2 * boxes] = radiate(block_ref, (up0_ref[...], up1_ref[...])).reshape(boxes, sub, width)
    radiated_ref[2 * boxes] = jnp.zeros((sub, width), F32)
    staged.wait()
    nothing = jnp.zeros((sub, width // 2), F32)
    add_all(list_ref, EARLY, lambda g: (nothing, nothing), out_ref, radiated_ref, table_ref)


def far_kernel(
    lists_ref, mid_ref, table_ref, block_ref, up0_ref, up1_ref, down0_ref, down1_ref, out_ref, radiated_ref,
    incoming_ref, list_ref, sem,
):
    staged = pltpu.make_async_copy(lists_ref, list_ref, sem)
    staged.start()
    boxes, sub, width = mid_ref.shape
    half = width // 2
    radiated_ref[:boxes] = radiate(block_ref, (up0_ref[...], up1_ref[...])).reshape(boxes, sub, width)
    radiated_ref[boxes] = jnp.zeros((sub, width), F32)
    staged.wait()
    add_all(
        list_ref, LATE, lambda g: (mid_ref[g, :, :half], mid_ref[g, :, half:]), incoming_ref, radiated_ref, table_ref
    )
    far = dot3(split(incoming_ref[...].reshape(boxes * sub, width)), (down0_ref[...], down1_ref[...]), NT_FORM)
    devices, rows, lanes = out_ref.shape
    out_ref[:, : rows // 2, :] = far[:, :lanes].reshape(devices, rows // 2, lanes)
    out_ref[:, rows // 2 :, :] = far[:, lanes:].reshape(devices, rows // 2, lanes)


def join_kernel(far_ref, near_ref, out_ref, sum_ref, sem):
    parts, boxes, lanes, illum = out_ref.shape
    own = illum // far_ref.shape[0]
    stores = []
    for n, (c, b) in enumerate((c, b) for c in range(parts) for b in range(boxes)):
        turned = far_ref[:, n * own : (n + 1) * own, :].reshape(illum, lanes).T
        sum_ref[n] = near_ref[c, b] + turned
        stores.append(pltpu.make_async_copy(sum_ref.at[n], out_ref.at[c, b], sem.at[n]))
        stores[n].start()
    for store in stores:
        store.wait()


def call(kernel, outs, kinds, scratch=(), limit=16, micros=1, name=None, out_kind=VMEM):
    specs = [pl.BlockSpec(memory_space=kind) for kind in kinds]

    def run(*args):
        moved = 4 * sum(a.size for a in (*args, *jax.tree.leaves(outs)))
        return pl.pallas_call(
            kernel,
            out_shape=outs,
            in_specs=specs,
            out_specs=jax.tree.map(lambda _: pl.BlockSpec(memory_space=out_kind), outs),
            scratch_shapes=list(scratch),
            compiler_params=pltpu.CompilerParams(vmem_limit_bytes=limit * MIB),
            cost_estimate=pl.CostEstimate(flops=micros * 1_000_000_000, bytes_accessed=moved, transcendentals=0),
            name=name,
        )(*args)

    return run


def shape(*dims, kind=F32):
    return jax.ShapeDtypeStruct(dims, kind)


def body(currents, near_blocks, near_index, aggregate, translations, inter_source, inter_shift, disaggregate):
    devices = lax.axis_size("dir")
    slabs = lax.axis_size("slab")
    parts, box_dev, unknowns, illum = currents.shape
    own = illum // devices
    width = 2 * aggregate.shape[1]
    boxes, entries = inter_source.shape
    ops = translations.shape[1]
    rows = parts * box_dev * own
    ring = [(i, (i + 1) % devices) for i in range(devices)]
    pairs_of = [[(i, i + 1) for i in range(start, slabs - 1, 2)] for start in (0, 1)]
    same, cross = [p + [(j, i) for i, j in p] for p in pairs_of]

    turned = jnp.transpose(translations, (0, 2, 1))
    pieces = parts * box_dev
    blocks = pltpu.VMEM((pieces, unknowns, illum), F32)
    whole = shape(devices, rows + turned.shape[1], unknowns)
    packed = call(
        pack_kernel,
        whole,
        (ANY, ANY),
        scratch=(
            blocks,
            pltpu.VMEM(turned.shape, F32),
            pltpu.VMEM(whole.shape, F32),
            pltpu.SemaphoreType.DMA((pieces + 1,)),
            pltpu.SemaphoreType.DMA((pieces + 1,)),
        ),
        limit=FULL,
        name="pack",
        out_kind=ANY,
    )(currents, turned)
    mine = lax.all_to_all(packed, "dir", 0, 0, tiled=True)
    lists = shape(2 * entries + LIST_ROWS, 128, kind=jnp.int32)
    early, late = call(plan_kernel, (lists, lists), (VMEM, VMEM), name="plan")(inter_source.T, inter_shift.T)
    mine, beside, early, late = lax.optimization_barrier((mine, currents, early, late))
    sent = mine[:, :rows]
    from_cross = lax.ppermute(sent, "slab", cross)
    from_same = lax.ppermute(sent, "slab", same)
    left = lax.ppermute(beside, "dir", ring)
    right = lax.ppermute(beside, "dir", [(j, i) for i, j in ring])
    field = shape(boxes, own, width)
    up, down = shape(width, 2 * unknowns, kind=BF16), shape(2 * unknowns, width, kind=BF16)
    radiated, table, up0, up1, down0, down1 = call(
        own_kernel, (field, shape(ops, own, width), up, up, down, down), (VMEM,) * 3, name="own"
    )(mine, aggregate, disaggregate)
    staging = (pltpu.SMEM(lists.shape, jnp.int32), pltpu.SemaphoreType.DMA)
    partial = call(
        mid_kernel,
        field,
        (VMEM,) * 6,
        scratch=(pltpu.VMEM((2 * boxes + 1, own, width), F32), *staging),
        micros=6,
        name="mid",
    )(early, radiated, table, from_same, up0, up1)
    far = call(
        far_kernel,
        shape(devices, rows, unknowns),
        (VMEM,) * 8,
        scratch=(pltpu.VMEM((boxes + 1, own, width), F32), pltpu.VMEM((boxes, own, width), F32), *staging),
        micros=5,
        name="far",
    )(late, partial, table, from_cross, up0, up1, down0, down1)
    back = lax.all_to_all(far, "dir", 0, 0, tiled=True)

    stack = pltpu.VMEM((3 * box_dev, 2 * unknowns, 2 * illum), BF16)
    near = call(
        near_kernel, shape(*currents.shape), (SMEM,) + (VMEM,) * 4, scratch=(stack, stack), micros=20, name="near"
    )(near_index, near_blocks, currents, left, right)
    return call(
        join_kernel,
        shape(*currents.shape),
        (VMEM, VMEM),
        scratch=(blocks, pltpu.SemaphoreType.DMA((pieces,))),
        micros=0,
        name="join",
        out_kind=ANY,
    )(back, near)


def solution(mesh):
    in_specs = (
        P(None, ("slab", "dir"), None, None),
        P(None, ("slab", "dir"), None, None, None),
        P(("slab", "dir"), None),
        P(),
        P(None, None, "dir"),
        P("slab", None),
        P("slab", None),
        P(),
    )
    out_specs = P(None, ("slab", "dir"), None, None)
    return jax.shard_map(body, mesh=mesh, in_specs=in_specs, out_specs=out_specs, check_vma=False)
```

```python
import functools

import jax
import jax.numpy as jnp
from jax import lax
from jax.experimental import pallas as pl
from jax.experimental.pallas import tpu as pltpu
from jax.sharding import PartitionSpec as P

F32, BF16 = jnp.float32, jnp.bfloat16
VMEM = pltpu.MemorySpace.VMEM
SMEM = pltpu.MemorySpace.SMEM
ANY = pl.ANY
MIB = 1 << 20
RE_IM_ROWS = 32
EARLY, LATE = 25, 15
LIST_ROWS = 8
FULL = 63


def split(x):
    high = x.astype(BF16)
    return high, (x - high.astype(F32)).astype(BF16)


def dot3(left, right, contract):
    def one(a, b):
        return lax.dot_general(a, b, (contract, ((), ())), preferred_element_type=F32)

    return one(left[0], right[0]) + (one(left[0], right[1]) + one(left[1], right[0]))


NN_FORM = ((1,), (0,))
NT_FORM = ((1,), (1,))


def pack_kernel(currents_ref, out_ref, block_ref, packed_ref, in_sem, out_sem):
    devices, rows, lanes = out_ref.shape
    parts, boxes, _, illum = currents_ref.shape
    own = illum // devices
    pieces = [(c, b) for c in range(parts) for b in range(boxes)]
    last = len(pieces)
    loads = [pltpu.make_async_copy(currents_ref.at[c, b], block_ref.at[n], in_sem.at[n]) for n, (c, b) in enumerate(pieces)]
    stores = [
        pltpu.make_async_copy(packed_ref.at[:, pl.ds(n * own, own), :], out_ref.at[:, pl.ds(n * own, own), :], out_sem.at[n])
        for n in range(last)
    ]
    for load in loads:
        load.start()
    for n in range(last):
        loads[n].wait()
        packed_ref[:, n * own : (n + 1) * own, :] = block_ref[n].T.reshape(devices, own, lanes)
        stores[n].start()
    for store in stores:
        store.wait()


def near_kernel(index_ref, blocks_ref, own_ref, left_ref, right_ref, out_ref, high_ref, low_ref):
    boxes, entries = blocks_ref.shape[1], blocks_ref.shape[2]
    width = own_ref.shape[3]
    for place, ref in enumerate((left_ref, own_ref, right_ref)):
        for b in range(boxes):
            slot = place * boxes + b
            real, imag = split(ref[0, b]), split(ref[1, b])
            for store, x, y in ((high_ref, real[0], imag[0]), (low_ref, real[1], imag[1])):
                store[slot] = jnp.concatenate(
                    [jnp.concatenate([x, y], axis=1), jnp.concatenate([-y, x], axis=1)], axis=0
                )
    for b in range(boxes):

        def step(j, total):
            source = index_ref[b, j]
            block = split(jnp.concatenate([blocks_ref[0, b, j], blocks_ref[1, b, j]], axis=1))
            return total + dot3(block, (high_ref[source], low_ref[source]), NN_FORM)

        total = lax.fori_loop(0, entries, step, jnp.zeros((blocks_ref.shape[3], 2 * width), F32))
        out_ref[0, b] = total[:, :width]
        out_ref[1, b] = total[:, width:]


def radiate(block_ref, weights):
    devices, rows, lanes = block_ref.shape
    half = RE_IM_ROWS // 2
    real = block_ref[:, :half, :].reshape(devices * half, lanes)
    imag = block_ref[:, half : 2 * half, :].reshape(devices * half, lanes)
    return dot3(split(jnp.concatenate([real, imag], axis=1)), weights, NT_FORM)


def complex_rows(ref):
    real, imag = ref[0], ref[1]
    return jnp.concatenate(
        [jnp.concatenate([real, -imag], axis=1), jnp.concatenate([imag, real], axis=1)], axis=0
    )


def plan_kernel(source_ref, shift_ref, early_ref, late_ref):
    entries, boxes = source_ref.shape
    odd = lax.axis_index("slab") % 2
    source, shift = source_ref[...], shift_ref[...]
    part, place = source // boxes, source % boxes
    away = part == 2 * odd
    row = lax.broadcasted_iota(jnp.int32, (entries, boxes), 0)
    across = [lax.broadcasted_iota(jnp.int32, (boxes, boxes), n) for n in range(2)]
    before, same = (across[1] < across[0]).astype(F32), (across[1] == across[0]).astype(F32)
    slot = lax.broadcasted_iota(jnp.int32, (boxes, early_ref.shape[1]), 1).astype(F32)
    for ref, fixed, chosen, where, zeros in (
        (early_ref, EARLY, jnp.logical_not(away), jnp.where(part == 1, place, boxes + place), 2 * boxes),
        (late_ref, LATE, away, place, boxes),
    ):
        one = chosen.astype(jnp.int32)
        count = jnp.zeros((1, boxes), jnp.int32)
        front_where = jnp.full((entries, boxes), zeros, jnp.int32)
        front_shift = jnp.zeros((entries, boxes), jnp.int32)
        for i in range(entries):
            here = (row == count) & (one[i : i + 1] == 1)
            front_where = jnp.where(here, where[i : i + 1], front_where)
            front_shift = jnp.where(here, shift[i : i + 1], front_shift)
            count = count + one[i : i + 1]
        ref[...] = jnp.zeros(ref.shape, jnp.int32)
        ref[:entries, :boxes] = front_where
        ref[entries : 2 * entries, :boxes] = front_shift
        ref[2 * entries : 2 * entries + 1, :boxes] = count
        more = jnp.broadcast_to((count > fixed).astype(F32), (8, boxes))
        rank = lax.dot_general(before, more, (NT_FORM, ((), ())), preferred_element_type=F32)[:, :1]
        flag = lax.dot_general(same, more, (NT_FORM, ((), ())), preferred_element_type=F32)[:, :1]
        box = lax.broadcasted_iota(jnp.int32, slot.shape, 0).astype(F32)
        chosen_box = jnp.where((slot == rank) & (flag > 0.5), box, 0.0)
        ref[2 * entries + 1 : 2 * entries + 2, :] = jnp.sum(chosen_box, axis=0, keepdims=True).astype(jnp.int32)
        total = jnp.sum(more, axis=1, keepdims=True)[:1]
        ref[2 * entries + 2 : 2 * entries + 3, :] = jnp.broadcast_to(total, (1, ref.shape[1])).astype(jnp.int32)


def own_kernel(own_ref, tables_ref, aggregate_ref, disaggregate_ref, radiated_ref, table_ref, up0_ref, up1_ref, down0_ref, down1_ref):
    boxes, sub, width = radiated_ref.shape
    up = split(complex_rows(aggregate_ref))
    up0_ref[...], up1_ref[...] = up
    down0_ref[...], down1_ref[...] = split(complex_rows(disaggregate_ref))
    radiated_ref[...] = radiate(own_ref, up).reshape(boxes, sub, width)
    devices, lanes = own_ref.shape[0], tables_ref.shape[1]
    rows = tables_ref.shape[0] // devices
    me = lax.axis_index("dir")
    ordered = [tables_ref[pl.ds(pl.multiple_of((me ^ d) * rows, rows), rows), :] for d in range(devices)]
    table = jnp.concatenate(ordered, axis=0).T
    half = lanes // 2
    wide = jnp.concatenate([table[:half], table[half:]], axis=1)
    table_ref[...] = jnp.broadcast_to(wide[:, None, :], table_ref.shape)


def add_entries(list_ref, g, numbers, total, radiated_ref, table_ref):
    entries = list_ref.shape[0] // 2 - LIST_ROWS // 2
    half = table_ref.shape[2] // 2
    real, imag = total
    for n in numbers:
        q, t = list_ref[n, g], list_ref[entries + n, g]
        xr, xi = radiated_ref[q, :, :half], radiated_ref[q, :, half:]
        tr, ti = table_ref[t, :, :half], table_ref[t, :, half:]
        real, imag = real + (tr * xr - ti * xi), imag + (tr * xi + ti * xr)
    return real, imag


def add_all(list_ref, fixed, start, out_ref, radiated_ref, table_ref):
    entries = list_ref.shape[0] // 2 - LIST_ROWS // 2
    half = table_ref.shape[2] // 2

    def one_box(g, carry):
        total = add_entries(list_ref, g, range(fixed), start(g), radiated_ref, table_ref)
        out_ref[g, :, :half], out_ref[g, :, half:] = total
        return carry

    def beyond(place, carry):
        g = list_ref[2 * entries + 1, place]

        def rest(n, total):
            return add_entries(list_ref, g, (n,), total, radiated_ref, table_ref)

        both = lax.fori_loop(fixed, list_ref[2 * entries, g], rest, (out_ref[g, :, :half], out_ref[g, :, half:]))
        out_ref[g, :, :half], out_ref[g, :, half:] = both
        return carry

    lax.fori_loop(0, out_ref.shape[0], one_box, 0, unroll=4)
    lax.fori_loop(0, list_ref[2 * entries + 2, 0], beyond, 0)


def mid_kernel(
    lists_ref, own_ref, table_ref, block_ref, up0_ref, up1_ref, out_ref, radiated_ref, list_ref, sem
):
    staged = pltpu.make_async_copy(lists_ref, list_ref, sem)
    staged.start()
    boxes, sub, width = own_ref.shape
    radiated_ref[:boxes] = own_ref[...]
    radiated_ref[boxes : 2 * boxes] = radiate(block_ref, (up0_ref[...], up1_ref[...])).reshape(boxes, sub, width)
    radiated_ref[2 * boxes] = jnp.zeros((sub, width), F32)
    staged.wait()
    nothing = jnp.zeros((sub, width // 2), F32)
    add_all(list_ref, EARLY, lambda g: (nothing, nothing), out_ref, radiated_ref, table_ref)


def far_kernel(
    lists_ref, mid_ref, table_ref, block_ref, up0_ref, up1_ref, down0_ref, down1_ref, out_ref, radiated_ref,
    incoming_ref, list_ref, sem,
):
    staged = pltpu.make_async_copy(lists_ref, list_ref, sem)
    staged.start()
    boxes, sub, width = mid_ref.shape
    half = width // 2
    radiated_ref[:boxes] = radiate(block_ref, (up0_ref[...], up1_ref[...])).reshape(boxes, sub, width)
    radiated_ref[boxes] = jnp.zeros((sub, width), F32)
    staged.wait()
    add_all(
        list_ref, LATE, lambda g: (mid_ref[g, :, :half], mid_ref[g, :, half:]), incoming_ref, radiated_ref, table_ref
    )
    far = dot3(split(incoming_ref[...].reshape(boxes * sub, width)), (down0_ref[...], down1_ref[...]), NT_FORM)
    devices, rows, lanes = out_ref.shape
    out_ref[:, : rows // 2, :] = far[:, :lanes].reshape(devices, rows // 2, lanes)
    out_ref[:, rows // 2 :, :] = far[:, lanes:].reshape(devices, rows // 2, lanes)


def join_kernel(far_ref, near_ref, out_ref, sum_ref, sem):
    parts, boxes, lanes, illum = out_ref.shape
    own = illum // far_ref.shape[0]
    stores = []
    for n, (c, b) in enumerate((c, b) for c in range(parts) for b in range(boxes)):
        turned = far_ref[:, n * own : (n + 1) * own, :].reshape(illum, lanes).T
        sum_ref[n] = near_ref[c, b] + turned
        stores.append(pltpu.make_async_copy(sum_ref.at[n], out_ref.at[c, b], sem.at[n]))
        stores[n].start()
    for store in stores:
        store.wait()


def call(kernel, outs, kinds, scratch=(), limit=16, micros=1, name=None, out_kind=VMEM):
    specs = [pl.BlockSpec(memory_space=kind) for kind in kinds]

    def run(*args):
        moved = 4 * sum(a.size for a in (*args, *jax.tree.leaves(outs)))
        return pl.pallas_call(
            kernel,
            out_shape=outs,
            in_specs=specs,
            out_specs=jax.tree.map(lambda _: pl.BlockSpec(memory_space=out_kind), outs),
            scratch_shapes=list(scratch),
            compiler_params=pltpu.CompilerParams(vmem_limit_bytes=limit * MIB),
            cost_estimate=pl.CostEstimate(flops=micros * 1_000_000_000, bytes_accessed=moved, transcendentals=0),
            name=name,
        )(*args)

    return run


def shape(*dims, kind=F32):
    return jax.ShapeDtypeStruct(dims, kind)


def gathered(block, devices):
    step = 1
    while step < devices:
        count = min(4, devices // step)
        blocks = [block]
        for p in range(1, count):
            pairs = [(i, i ^ (p * step)) for i in range(devices)]
            blocks.append(lax.ppermute(block, "dir", pairs))
        block = jnp.concatenate(blocks, axis=0)
        step *= count
    return block


def body(currents, near_blocks, near_index, aggregate, translations, inter_source, inter_shift, disaggregate):
    devices = lax.axis_size("dir")
    slabs = lax.axis_size("slab")
    parts, box_dev, unknowns, illum = currents.shape
    own = illum // devices
    width = 2 * aggregate.shape[1]
    boxes, entries = inter_source.shape
    ops = translations.shape[1]
    rows = parts * box_dev * own
    ring = [(i, (i + 1) % devices) for i in range(devices)]
    pairs_of = [[(i, i + 1) for i in range(start, slabs - 1, 2)] for start in (0, 1)]
    same, cross = [p + [(j, i) for i, j in p] for p in pairs_of]

    pieces = parts * box_dev
    blocks = pltpu.VMEM((pieces, unknowns, illum), F32)
    whole = shape(devices, rows, unknowns)
    packed = call(
        pack_kernel,
        whole,
        (ANY,),
        scratch=(
            blocks,
            pltpu.VMEM(whole.shape, F32),
            pltpu.SemaphoreType.DMA((pieces,)),
            pltpu.SemaphoreType.DMA((pieces,)),
        ),
        limit=FULL,
        name="pack",
        out_kind=ANY,
    )(currents)
    mine = lax.all_to_all(packed, "dir", 0, 0, tiled=True)
    tables = gathered(jnp.transpose(translations, (2, 0, 1)).reshape(-1, parts * ops), devices)
    lists = shape(2 * entries + LIST_ROWS, 128, kind=jnp.int32)
    early, late = call(plan_kernel, (lists, lists), (VMEM, VMEM), name="plan")(inter_source.T, inter_shift.T)
    mine, beside, early, late, tables = lax.optimization_barrier((mine, currents, early, late, tables))
    from_cross = lax.ppermute(mine, "slab", cross)
    from_same = lax.ppermute(mine, "slab", same)
    left = lax.ppermute(beside, "dir", ring)
    right = lax.ppermute(beside, "dir", [(j, i) for i, j in ring])
    field = shape(boxes, own, width)
    up, down = shape(width, 2 * unknowns, kind=BF16), shape(2 * unknowns, width, kind=BF16)
    radiated, table, up0, up1, down0, down1 = call(
        own_kernel, (field, shape(ops, own, width), up, up, down, down), (VMEM,) * 4, name="own"
    )(mine, tables, aggregate, disaggregate)
    staging = (pltpu.SMEM(lists.shape, jnp.int32), pltpu.SemaphoreType.DMA)
    partial = call(
        mid_kernel,
        field,
        (VMEM,) * 6,
        scratch=(pltpu.VMEM((2 * boxes + 1, own, width), F32), *staging),
        micros=6,
        name="mid",
    )(early, radiated, table, from_same, up0, up1)
    far = call(
        far_kernel,
        shape(devices, rows, unknowns),
        (VMEM,) * 8,
        scratch=(pltpu.VMEM((boxes + 1, own, width), F32), pltpu.VMEM((boxes, own, width), F32), *staging),
        micros=5,
        name="far",
    )(late, partial, table, from_cross, up0, up1, down0, down1)
    back = lax.all_to_all(far, "dir", 0, 0, tiled=True)

    stack = pltpu.VMEM((3 * box_dev, 2 * unknowns, 2 * illum), BF16)
    near = call(
        near_kernel, shape(*currents.shape), (SMEM,) + (VMEM,) * 4, scratch=(stack, stack), micros=20, name="near"
    )(near_index, near_blocks, currents, left, right)
    return call(
        join_kernel,
        shape(*currents.shape),
        (VMEM, VMEM),
        scratch=(blocks, pltpu.SemaphoreType.DMA((pieces,))),
        micros=0,
        name="join",
        out_kind=ANY,
    )(back, near)


def solution(mesh):
    in_specs = (
        P(None, ("slab", "dir"), None, None),
        P(None, ("slab", "dir"), None, None, None),
        P(("slab", "dir"), None),
        P(),
        P(None, None, "dir"),
        P("slab", None),
        P("slab", None),
        P(),
    )
    out_specs = P(None, ("slab", "dir"), None, None)
    return jax.shard_map(body, mesh=mesh, in_specs=in_specs, out_specs=out_specs, check_vma=False)
```

```python
import functools

import jax
import jax.numpy as jnp
from jax import lax
from jax.experimental import pallas as pl
from jax.experimental.pallas import tpu as pltpu
from jax.sharding import PartitionSpec as P

F32, BF16 = jnp.float32, jnp.bfloat16
VMEM = pltpu.MemorySpace.VMEM
SMEM = pltpu.MemorySpace.SMEM
ANY = pl.ANY
MIB = 1 << 20
RE_IM_ROWS = 32
EARLY, LATE = 25, 15
LIST_ROWS = 8
FULL = 63


def split(x):
    high = x.astype(BF16)
    return high, (x - high.astype(F32)).astype(BF16)


def dot3(left, right, contract):
    def one(a, b):
        return lax.dot_general(a, b, (contract, ((), ())), preferred_element_type=F32)

    return one(left[0], right[0]) + (one(left[0], right[1]) + one(left[1], right[0]))


NN_FORM = ((1,), (0,))
NT_FORM = ((1,), (1,))


def pack_kernel(currents_ref, out_ref, block_ref, packed_ref, in_sem, out_sem):
    devices, rows, lanes = out_ref.shape
    parts, boxes, _, illum = currents_ref.shape
    own = illum // devices
    pieces = [(c, b) for c in range(parts) for b in range(boxes)]
    last = len(pieces)
    loads = [pltpu.make_async_copy(currents_ref.at[c, b], block_ref.at[n], in_sem.at[n]) for n, (c, b) in enumerate(pieces)]
    stores = [
        pltpu.make_async_copy(packed_ref.at[:, pl.ds(n * own, own), :], out_ref.at[:, pl.ds(n * own, own), :], out_sem.at[n])
        for n in range(last)
    ]
    for load in loads:
        load.start()
    for n in range(last):
        loads[n].wait()
        packed_ref[:, n * own : (n + 1) * own, :] = block_ref[n].T.reshape(devices, own, lanes)
        stores[n].start()
    for store in stores:
        store.wait()


def near_kernel(index_ref, blocks_ref, own_ref, left_ref, right_ref, out_ref, high_ref, low_ref):
    boxes, entries = blocks_ref.shape[1], blocks_ref.shape[2]
    width = own_ref.shape[3]
    for place, ref in enumerate((left_ref, own_ref, right_ref)):
        for b in range(boxes):
            slot = place * boxes + b
            real, imag = split(ref[0, b]), split(ref[1, b])
            for store, x, y in ((high_ref, real[0], imag[0]), (low_ref, real[1], imag[1])):
                store[slot] = jnp.concatenate(
                    [jnp.concatenate([x, y], axis=1), jnp.concatenate([-y, x], axis=1)], axis=0
                )
    for b in range(boxes):

        def step(j, total):
            source = index_ref[b, j]
            block = split(jnp.concatenate([blocks_ref[0, b, j], blocks_ref[1, b, j]], axis=1))
            return total + dot3(block, (high_ref[source], low_ref[source]), NN_FORM)

        total = lax.fori_loop(0, entries, step, jnp.zeros((blocks_ref.shape[3], 2 * width), F32))
        out_ref[0, b] = total[:, :width]
        out_ref[1, b] = total[:, width:]


def radiate(block_ref, weights):
    devices, rows, lanes = block_ref.shape
    half = RE_IM_ROWS // 2
    real = block_ref[:, :half, :].reshape(devices * half, lanes)
    imag = block_ref[:, half : 2 * half, :].reshape(devices * half, lanes)
    return dot3(split(jnp.concatenate([real, imag], axis=1)), weights, NT_FORM)


def complex_rows(ref):
    real, imag = ref[0], ref[1]
    return jnp.concatenate(
        [jnp.concatenate([real, -imag], axis=1), jnp.concatenate([imag, real], axis=1)], axis=0
    )


def plan_kernel(source_ref, shift_ref, early_ref, late_ref):
    entries, boxes = source_ref.shape
    odd = lax.axis_index("slab") % 2
    source, shift = source_ref[...], shift_ref[...]
    part, place = source // boxes, source % boxes
    away = part == 2 * odd
    row = lax.broadcasted_iota(jnp.int32, (entries, boxes), 0)
    across = [lax.broadcasted_iota(jnp.int32, (boxes, boxes), n) for n in range(2)]
    before, same = (across[1] < across[0]).astype(F32), (across[1] == across[0]).astype(F32)
    slot = lax.broadcasted_iota(jnp.int32, (boxes, early_ref.shape[1]), 1).astype(F32)
    for ref, fixed, chosen, where, zeros in (
        (early_ref, EARLY, jnp.logical_not(away), jnp.where(part == 1, place, boxes + place), 2 * boxes),
        (late_ref, LATE, away, place, boxes),
    ):
        one = chosen.astype(jnp.int32)
        count = jnp.zeros((1, boxes), jnp.int32)
        front_where = jnp.full((entries, boxes), zeros, jnp.int32)
        front_shift = jnp.zeros((entries, boxes), jnp.int32)
        for i in range(entries):
            here = (row == count) & (one[i : i + 1] == 1)
            front_where = jnp.where(here, where[i : i + 1], front_where)
            front_shift = jnp.where(here, shift[i : i + 1], front_shift)
            count = count + one[i : i + 1]
        ref[...] = jnp.zeros(ref.shape, jnp.int32)
        ref[:entries, :boxes] = front_where
        ref[entries : 2 * entries, :boxes] = front_shift
        ref[2 * entries : 2 * entries + 1, :boxes] = count
        more = jnp.broadcast_to((count > fixed).astype(F32), (8, boxes))
        rank = lax.dot_general(before, more, (NT_FORM, ((), ())), preferred_element_type=F32)[:, :1]
        flag = lax.dot_general(same, more, (NT_FORM, ((), ())), preferred_element_type=F32)[:, :1]
        box = lax.broadcasted_iota(jnp.int32, slot.shape, 0).astype(F32)
        chosen_box = jnp.where((slot == rank) & (flag > 0.5), box, 0.0)
        ref[2 * entries + 1 : 2 * entries + 2, :] = jnp.sum(chosen_box, axis=0, keepdims=True).astype(jnp.int32)
        total = jnp.sum(more, axis=1, keepdims=True)[:1]
        ref[2 * entries + 2 : 2 * entries + 3, :] = jnp.broadcast_to(total, (1, ref.shape[1])).astype(jnp.int32)


def own_kernel(own_ref, aggregate_ref, disaggregate_ref, radiated_ref, up0_ref, up1_ref, down0_ref, down1_ref):
    boxes, sub, width = radiated_ref.shape
    up = split(complex_rows(aggregate_ref))
    up0_ref[...], up1_ref[...] = up
    down0_ref[...], down1_ref[...] = split(complex_rows(disaggregate_ref))
    radiated_ref[...] = radiate(own_ref, up).reshape(boxes, sub, width)


def table_kernel(first_ref, second_ref, table_ref, both_ref):
    devices = lax.axis_size("dir")
    count, lanes = both_ref.shape
    rows = count // devices
    both_ref[: count // 2] = first_ref[...]
    both_ref[count // 2 :] = second_ref[...]
    me = lax.axis_index("dir")
    ordered = [both_ref[pl.ds(pl.multiple_of((me ^ d) * rows, rows), rows), :] for d in range(devices)]
    table = jnp.concatenate(ordered, axis=0).T
    half = lanes // 2
    wide = jnp.concatenate([table[:half], table[half:]], axis=1)
    table_ref[...] = jnp.broadcast_to(wide[:, None, :], table_ref.shape)


def add_entries(list_ref, g, numbers, total, radiated_ref, table_ref):
    entries = list_ref.shape[0] // 2 - LIST_ROWS // 2
    half = table_ref.shape[2] // 2
    real, imag = total
    for n in numbers:
        q, t = list_ref[n, g], list_ref[entries + n, g]
        xr, xi = radiated_ref[q, :, :half], radiated_ref[q, :, half:]
        tr, ti = table_ref[t, :, :half], table_ref[t, :, half:]
        real, imag = real + (tr * xr - ti * xi), imag + (tr * xi + ti * xr)
    return real, imag


def add_all(list_ref, fixed, start, out_ref, radiated_ref, table_ref):
    entries = list_ref.shape[0] // 2 - LIST_ROWS // 2
    half = table_ref.shape[2] // 2

    def one_box(g, carry):
        total = add_entries(list_ref, g, range(fixed), start(g), radiated_ref, table_ref)
        out_ref[g, :, :half], out_ref[g, :, half:] = total
        return carry

    def beyond(place, carry):
        g = list_ref[2 * entries + 1, place]

        def rest(n, total):
            return add_entries(list_ref, g, (n,), total, radiated_ref, table_ref)

        both = lax.fori_loop(fixed, list_ref[2 * entries, g], rest, (out_ref[g, :, :half], out_ref[g, :, half:]))
        out_ref[g, :, :half], out_ref[g, :, half:] = both
        return carry

    lax.fori_loop(0, out_ref.shape[0], one_box, 0, unroll=4)
    lax.fori_loop(0, list_ref[2 * entries + 2, 0], beyond, 0)


def mid_kernel(
    lists_ref, own_ref, table_ref, block_ref, up0_ref, up1_ref, out_ref, radiated_ref, list_ref, sem
):
    staged = pltpu.make_async_copy(lists_ref, list_ref, sem)
    staged.start()
    boxes, sub, width = own_ref.shape
    radiated_ref[:boxes] = own_ref[...]
    radiated_ref[boxes : 2 * boxes] = radiate(block_ref, (up0_ref[...], up1_ref[...])).reshape(boxes, sub, width)
    radiated_ref[2 * boxes] = jnp.zeros((sub, width), F32)
    staged.wait()
    nothing = jnp.zeros((sub, width // 2), F32)
    add_all(list_ref, EARLY, lambda g: (nothing, nothing), out_ref, radiated_ref, table_ref)


def far_kernel(
    lists_ref, mid_ref, table_ref, block_ref, up0_ref, up1_ref, down0_ref, down1_ref, out_ref, radiated_ref,
    incoming_ref, list_ref, sem,
):
    staged = pltpu.make_async_copy(lists_ref, list_ref, sem)
    staged.start()
    boxes, sub, width = mid_ref.shape
    half = width // 2
    radiated_ref[:boxes] = radiate(block_ref, (up0_ref[...], up1_ref[...])).reshape(boxes, sub, width)
    radiated_ref[boxes] = jnp.zeros((sub, width), F32)
    staged.wait()
    add_all(
        list_ref, LATE, lambda g: (mid_ref[g, :, :half], mid_ref[g, :, half:]), incoming_ref, radiated_ref, table_ref
    )
    far = dot3(split(incoming_ref[...].reshape(boxes * sub, width)), (down0_ref[...], down1_ref[...]), NT_FORM)
    devices, rows, lanes = out_ref.shape
    out_ref[:, : rows // 2, :] = far[:, :lanes].reshape(devices, rows // 2, lanes)
    out_ref[:, rows // 2 :, :] = far[:, lanes:].reshape(devices, rows // 2, lanes)


def join_kernel(far_ref, near_ref, out_ref, sum_ref, sem):
    parts, boxes, lanes, illum = out_ref.shape
    own = illum // far_ref.shape[0]
    stores = []
    for n, (c, b) in enumerate((c, b) for c in range(parts) for b in range(boxes)):
        turned = far_ref[:, n * own : (n + 1) * own, :].reshape(illum, lanes).T
        sum_ref[n] = near_ref[c, b] + turned
        stores.append(pltpu.make_async_copy(sum_ref.at[n], out_ref.at[c, b], sem.at[n]))
        stores[n].start()
    for store in stores:
        store.wait()


def call(kernel, outs, kinds, scratch=(), limit=16, micros=1, name=None, out_kind=VMEM):
    specs = [pl.BlockSpec(memory_space=kind) for kind in kinds]

    def run(*args):
        moved = 4 * sum(a.size for a in (*args, *jax.tree.leaves(outs)))
        return pl.pallas_call(
            kernel,
            out_shape=outs,
            in_specs=specs,
            out_specs=jax.tree.map(lambda _: pl.BlockSpec(memory_space=out_kind), outs),
            scratch_shapes=list(scratch),
            compiler_params=pltpu.CompilerParams(vmem_limit_bytes=limit * MIB),
            cost_estimate=pl.CostEstimate(flops=micros * 1_000_000_000, bytes_accessed=moved, transcendentals=0),
            name=name,
        )(*args)

    return run


def shape(*dims, kind=F32):
    return jax.ShapeDtypeStruct(dims, kind)


def gathered(block, devices, steps):
    step = 1
    while step < steps:
        count = min(4, steps // step)
        blocks = [block]
        for p in range(1, count):
            pairs = [(i, i ^ (p * step)) for i in range(devices)]
            blocks.append(lax.ppermute(block, "dir", pairs))
        block = jnp.concatenate(blocks, axis=0)
        step *= count
    return block


def body(currents, near_blocks, near_index, aggregate, translations, inter_source, inter_shift, disaggregate):
    devices = lax.axis_size("dir")
    slabs = lax.axis_size("slab")
    parts, box_dev, unknowns, illum = currents.shape
    own = illum // devices
    width = 2 * aggregate.shape[1]
    boxes, entries = inter_source.shape
    ops = translations.shape[1]
    rows = parts * box_dev * own
    ring = [(i, (i + 1) % devices) for i in range(devices)]
    pairs_of = [[(i, i + 1) for i in range(start, slabs - 1, 2)] for start in (0, 1)]
    same, cross = [p + [(j, i) for i, j in p] for p in pairs_of]

    pieces = parts * box_dev
    blocks = pltpu.VMEM((pieces, unknowns, illum), F32)
    whole = shape(devices, rows, unknowns)
    packed = call(
        pack_kernel,
        whole,
        (ANY,),
        scratch=(
            blocks,
            pltpu.VMEM(whole.shape, F32),
            pltpu.SemaphoreType.DMA((pieces,)),
            pltpu.SemaphoreType.DMA((pieces,)),
        ),
        limit=FULL,
        name="pack",
        out_kind=ANY,
    )(currents)
    mine = lax.all_to_all(packed, "dir", 0, 0, tiled=True)
    tables = gathered(jnp.transpose(translations, (2, 0, 1)).reshape(-1, parts * ops), devices, devices // 2)
    lists = shape(2 * entries + LIST_ROWS, 128, kind=jnp.int32)
    early, late = call(plan_kernel, (lists, lists), (VMEM, VMEM), name="plan")(inter_source.T, inter_shift.T)
    mine, beside, early, late, tables = lax.optimization_barrier((mine, currents, early, late, tables))
    from_cross = lax.ppermute(mine, "slab", cross)
    from_same = lax.ppermute(mine, "slab", same)
    others = lax.ppermute(tables, "dir", [(i, i ^ (devices // 2)) for i in range(devices)])
    field = shape(boxes, own, width)
    up, down = shape(width, 2 * unknowns, kind=BF16), shape(2 * unknowns, width, kind=BF16)
    radiated, up0, up1, down0, down1 = call(
        own_kernel, (field, up, up, down, down), (VMEM,) * 3, name="own"
    )(mine, aggregate, disaggregate)
    radiated, beside = lax.optimization_barrier((radiated, beside))
    left = lax.ppermute(beside, "dir", ring)
    right = lax.ppermute(beside, "dir", [(j, i) for i, j in ring])
    table = call(
        table_kernel,
        shape(ops, own, width),
        (VMEM, VMEM),
        scratch=(pltpu.VMEM((width // 2, parts * ops), F32),),
        name="table",
    )(tables, others)
    staging = (pltpu.SMEM(lists.shape, jnp.int32), pltpu.SemaphoreType.DMA)
    partial = call(
        mid_kernel,
        field,
        (VMEM,) * 6,
        scratch=(pltpu.VMEM((2 * boxes + 1, own, width), F32), *staging),
        micros=6,
        name="mid",
    )(early, radiated, table, from_same, up0, up1)
    far = call(
        far_kernel,
        shape(devices, rows, unknowns),
        (VMEM,) * 8,
        scratch=(pltpu.VMEM((boxes + 1, own, width), F32), pltpu.VMEM((boxes, own, width), F32), *staging),
        micros=5,
        name="far",
    )(late, partial, table, from_cross, up0, up1, down0, down1)
    back = lax.all_to_all(far, "dir", 0, 0, tiled=True)

    stack = pltpu.VMEM((3 * box_dev, 2 * unknowns, 2 * illum), BF16)
    near = call(
        near_kernel, shape(*currents.shape), (SMEM,) + (VMEM,) * 4, scratch=(stack, stack), micros=20, name="near"
    )(near_index, near_blocks, currents, left, right)
    return call(
        join_kernel,
        shape(*currents.shape),
        (VMEM, VMEM),
        scratch=(blocks, pltpu.SemaphoreType.DMA((pieces,))),
        micros=0,
        name="join",
        out_kind=ANY,
    )(back, near)


def solution(mesh):
    in_specs = (
        P(None, ("slab", "dir"), None, None),
        P(None, ("slab", "dir"), None, None, None),
        P(("slab", "dir"), None),
        P(),
        P(None, None, "dir"),
        P("slab", None),
        P("slab", None),
        P(),
    )
    out_specs = P(None, ("slab", "dir"), None, None)
    return jax.shard_map(body, mesh=mesh, in_specs=in_specs, out_specs=out_specs, check_vma=False)
```

```python
import functools

import jax
import jax.numpy as jnp
from jax import lax
from jax.experimental import pallas as pl
from jax.experimental.pallas import tpu as pltpu
from jax.sharding import PartitionSpec as P

F32, BF16 = jnp.float32, jnp.bfloat16
VMEM = pltpu.MemorySpace.VMEM
SMEM = pltpu.MemorySpace.SMEM
ANY = pl.ANY
MIB = 1 << 20
RE_IM_ROWS = 32
FIRST = 16
LIST_ROWS = 8
FULL = 63


def split(x):
    high = x.astype(BF16)
    return high, (x - high.astype(F32)).astype(BF16)


def dot3(left, right, contract):
    def one(a, b):
        return lax.dot_general(a, b, (contract, ((), ())), preferred_element_type=F32)

    return one(left[0], right[0]) + (one(left[0], right[1]) + one(left[1], right[0]))


NN_FORM = ((1,), (0,))
NT_FORM = ((1,), (1,))


def plan_kernel(source_ref, shift_ref, early_ref, late_ref):
    entries, boxes = source_ref.shape
    odd = lax.axis_index("slab") % 2
    source, shift = source_ref[...], shift_ref[...]
    part, place = source // boxes, source % boxes
    away = part == 2 * odd
    where = jnp.where(part == 1, place, jnp.where(away, 2 * boxes + place, boxes + place))
    one = jnp.where(away, 0, 1)
    near_count = jnp.sum(one, axis=0, keepdims=True)
    row = lax.broadcasted_iota(jnp.int32, (entries, boxes), 0)
    to_near, to_away = jnp.zeros((1, boxes), jnp.int32), near_count
    sorted_where = jnp.zeros((entries, boxes), jnp.int32)
    sorted_shift = jnp.zeros((entries, boxes), jnp.int32)
    for i in range(entries):
        is_near = one[i : i + 1]
        here = row == jnp.where(is_near == 1, to_near, to_away)
        sorted_where = jnp.where(here, where[i : i + 1], sorted_where)
        sorted_shift = jnp.where(here, shift[i : i + 1], sorted_shift)
        to_near, to_away = to_near + is_near, to_away + (1 - is_near)
    for ref in (early_ref, late_ref):
        ref[...] = jnp.zeros(ref.shape, jnp.int32)
        ref[entries : 2 * entries, :boxes] = sorted_shift
    early_ref[:entries, :boxes] = jnp.minimum(sorted_where, 2 * boxes)
    late_ref[:entries, :boxes] = sorted_where
    late_ref[2 * entries : 2 * entries + 1, :boxes] = near_count
    across = [lax.broadcasted_iota(jnp.int32, (boxes, boxes), n) for n in range(2)]
    before, same = (across[1] < across[0]).astype(F32), (across[1] == across[0]).astype(F32)
    lanes = late_ref.shape[1]
    slot = lax.broadcasted_iota(jnp.int32, (boxes, lanes), 1).astype(F32)
    box = lax.broadcasted_iota(jnp.int32, (boxes, lanes), 0).astype(F32)
    few = jnp.broadcast_to((near_count < FIRST).astype(F32), (8, boxes))
    rank = lax.dot_general(before, few, (NT_FORM, ((), ())), preferred_element_type=F32)[:, :1]
    flag = lax.dot_general(same, few, (NT_FORM, ((), ())), preferred_element_type=F32)[:, :1]
    listed = jnp.sum(jnp.where((slot == rank) & (flag > 0.5), box, 0.0), axis=0, keepdims=True)
    late_ref[2 * entries + 1 : 2 * entries + 2, :] = listed.astype(jnp.int32)
    total = jnp.sum(few, axis=1, keepdims=True)[:1]
    late_ref[2 * entries + 2 : 2 * entries + 3, :] = jnp.broadcast_to(total, (1, lanes)).astype(jnp.int32)


def pack_kernel(currents_ref, translations_ref, out_ref, block_ref, table_ref, packed_ref, in_sem, out_sem):
    devices, rows, lanes = out_ref.shape
    parts, boxes, _, illum = currents_ref.shape
    own = illum // devices
    pieces = [(c, b) for c in range(parts) for b in range(boxes)]
    last = len(pieces)
    loads = [pltpu.make_async_copy(currents_ref.at[c, b], block_ref.at[n], in_sem.at[n]) for n, (c, b) in enumerate(pieces)]
    loads.append(pltpu.make_async_copy(translations_ref, table_ref, in_sem.at[last]))
    stores = [
        pltpu.make_async_copy(packed_ref.at[:, pl.ds(n * own, own), :], out_ref.at[:, pl.ds(n * own, own), :], out_sem.at[n])
        for n in range(last + 1)
    ]
    for load in loads:
        load.start()
    for n in range(last):
        loads[n].wait()
        packed_ref[:, n * own : (n + 1) * own, :] = block_ref[n].T.reshape(devices, own, lanes)
        stores[n].start()
    loads[last].wait()
    table = jnp.concatenate([table_ref[0], table_ref[1]], axis=1)
    packed_ref[:, last * own :, :] = jnp.broadcast_to(table[None], (devices, own, lanes))
    stores[last].start()
    for store in stores:
        store.wait()


def near_kernel(index_ref, blocks_ref, own_ref, left_ref, right_ref, out_ref, high_ref, low_ref):
    boxes, entries = blocks_ref.shape[1], blocks_ref.shape[2]
    width = own_ref.shape[3]
    for place, ref in enumerate((left_ref, own_ref, right_ref)):
        for b in range(boxes):
            slot = place * boxes + b
            real, imag = split(ref[0, b]), split(ref[1, b])
            for store, x, y in ((high_ref, real[0], imag[0]), (low_ref, real[1], imag[1])):
                store[slot] = jnp.concatenate(
                    [jnp.concatenate([x, y], axis=1), jnp.concatenate([-y, x], axis=1)], axis=0
                )
    for b in range(boxes):

        def step(j, total):
            source = index_ref[b, j]
            block = split(jnp.concatenate([blocks_ref[0, b, j], blocks_ref[1, b, j]], axis=1))
            return total + dot3(block, (high_ref[source], low_ref[source]), NN_FORM)

        total = lax.fori_loop(0, entries, step, jnp.zeros((blocks_ref.shape[3], 2 * width), F32))
        out_ref[0, b] = total[:, :width]
        out_ref[1, b] = total[:, width:]


def radiate(block_ref, weights):
    devices, rows, lanes = block_ref.shape
    half = RE_IM_ROWS // 2
    real = block_ref[:, :half, :].reshape(devices * half, lanes)
    imag = block_ref[:, half : 2 * half, :].reshape(devices * half, lanes)
    return dot3(split(jnp.concatenate([real, imag], axis=1)), weights, NT_FORM)


def complex_rows(ref):
    real, imag = ref[0], ref[1]
    return jnp.concatenate(
        [jnp.concatenate([real, -imag], axis=1), jnp.concatenate([imag, real], axis=1)], axis=0
    )


def own_kernel(own_ref, aggregate_ref, disaggregate_ref, radiated_ref, table_ref, up0_ref, up1_ref, down0_ref, down1_ref):
    boxes, sub, width = radiated_ref.shape
    up = split(complex_rows(aggregate_ref))
    up0_ref[...], up1_ref[...] = up
    down0_ref[...], down1_ref[...] = split(complex_rows(disaggregate_ref))
    radiated_ref[...] = radiate(own_ref, up).reshape(boxes, sub, width)
    devices, rows, lanes = own_ref.shape
    table = own_ref[:, RE_IM_ROWS:, :].reshape(devices * (rows - RE_IM_ROWS), lanes).T
    half = lanes // 2
    wide = jnp.concatenate([table[:half], table[half:]], axis=1)
    table_ref[...] = jnp.broadcast_to(wide[:, None, :], table_ref.shape)


def add_entries(list_ref, g, numbers, total, radiated_ref, table_ref):
    entries = list_ref.shape[0] // 2 - LIST_ROWS // 2
    half = table_ref.shape[2] // 2
    real, imag = total
    for n in numbers:
        q, t = list_ref[n, g], list_ref[entries + n, g]
        xr, xi = radiated_ref[q, :, :half], radiated_ref[q, :, half:]
        tr, ti = table_ref[t, :, :half], table_ref[t, :, half:]
        real, imag = real + (tr * xr - ti * xi), imag + (tr * xi + ti * xr)
    return real, imag


def add_all(list_ref, numbers, start, out_ref, radiated_ref, table_ref):
    half = table_ref.shape[2] // 2

    def one_box(g, carry):
        total = add_entries(list_ref, g, numbers, start(g), radiated_ref, table_ref)
        out_ref[g, :, :half], out_ref[g, :, half:] = total
        return carry

    lax.fori_loop(0, out_ref.shape[0], one_box, 0, unroll=4)


def mid_kernel(
    lists_ref, own_ref, table_ref, block_ref, up0_ref, up1_ref, out_ref, radiated_ref, list_ref, sem
):
    staged = pltpu.make_async_copy(lists_ref, list_ref, sem)
    staged.start()
    boxes, sub, width = own_ref.shape
    radiated_ref[:boxes] = own_ref[...]
    radiated_ref[boxes : 2 * boxes] = radiate(block_ref, (up0_ref[...], up1_ref[...])).reshape(boxes, sub, width)
    radiated_ref[2 * boxes] = jnp.zeros((sub, width), F32)
    staged.wait()
    nothing = jnp.zeros((sub, width // 2), F32)
    add_all(list_ref, range(FIRST), lambda g: (nothing, nothing), out_ref, radiated_ref, table_ref)


def far_kernel(
    lists_ref, mid_ref, near_ref, table_ref, block_ref, up0_ref, up1_ref, down0_ref, down1_ref, out_ref, radiated_ref,
    incoming_ref, list_ref, sem,
):
    staged = pltpu.make_async_copy(lists_ref, list_ref, sem)
    staged.start()
    boxes, sub, width = mid_ref.shape
    half = width // 2
    entries = list_ref.shape[0] // 2 - LIST_ROWS // 2
    radiated_ref[: 2 * boxes] = near_ref[: 2 * boxes]
    radiated_ref[2 * boxes :] = radiate(block_ref, (up0_ref[...], up1_ref[...])).reshape(boxes, sub, width)
    staged.wait()
    rest = range(FIRST, entries)
    add_all(
        list_ref, rest, lambda g: (mid_ref[g, :, :half], mid_ref[g, :, half:]), incoming_ref, radiated_ref, table_ref
    )

    def skipped(place, carry):
        g = list_ref[2 * entries + 1, place]

        def one(n, total):
            return add_entries(list_ref, g, (n,), total, radiated_ref, table_ref)

        both = (incoming_ref[g, :, :half], incoming_ref[g, :, half:])
        both = lax.fori_loop(list_ref[2 * entries, g], FIRST, one, both)
        incoming_ref[g, :, :half], incoming_ref[g, :, half:] = both
        return carry

    lax.fori_loop(0, list_ref[2 * entries + 2, 0], skipped, 0)
    far = dot3(split(incoming_ref[...].reshape(boxes * sub, width)), (down0_ref[...], down1_ref[...]), NT_FORM)
    devices, rows, lanes = out_ref.shape
    out_ref[:, : rows // 2, :] = far[:, :lanes].reshape(devices, rows // 2, lanes)
    out_ref[:, rows // 2 :, :] = far[:, lanes:].reshape(devices, rows // 2, lanes)


def join_kernel(far_ref, near_ref, out_ref, sum_ref, sem):
    parts, boxes, lanes, illum = out_ref.shape
    own = illum // far_ref.shape[0]
    stores = []
    for n, (c, b) in enumerate((c, b) for c in range(parts) for b in range(boxes)):
        turned = far_ref[:, n * own : (n + 1) * own, :].reshape(illum, lanes).T
        sum_ref[n] = near_ref[c, b] + turned
        stores.append(pltpu.make_async_copy(sum_ref.at[n], out_ref.at[c, b], sem.at[n]))
        stores[n].start()
    for store in stores:
        store.wait()


def call(kernel, outs, kinds, scratch=(), limit=16, micros=1, name=None, out_kind=VMEM):
    specs = [pl.BlockSpec(memory_space=kind) for kind in kinds]

    def run(*args):
        moved = 4 * sum(a.size for a in (*args, *jax.tree.leaves(outs)))
        return pl.pallas_call(
            kernel,
            out_shape=outs,
            in_specs=specs,
            out_specs=jax.tree.map(lambda _: pl.BlockSpec(memory_space=out_kind), outs),
            scratch_shapes=list(scratch),
            compiler_params=pltpu.CompilerParams(vmem_limit_bytes=limit * MIB),
            cost_estimate=pl.CostEstimate(flops=micros * 1_000_000_000, bytes_accessed=moved, transcendentals=0),
            name=name,
        )(*args)

    return run


def shape(*dims, kind=F32):
    return jax.ShapeDtypeStruct(dims, kind)


def body(currents, near_blocks, near_index, aggregate, translations, inter_source, inter_shift, disaggregate):
    devices = lax.axis_size("dir")
    slabs = lax.axis_size("slab")
    parts, box_dev, unknowns, illum = currents.shape
    own = illum // devices
    width = 2 * aggregate.shape[1]
    boxes, entries = inter_source.shape
    ops = translations.shape[1]
    rows = parts * box_dev * own
    ring = [(i, (i + 1) % devices) for i in range(devices)]
    pairs_of = [[(i, i + 1) for i in range(start, slabs - 1, 2)] for start in (0, 1)]
    same, cross = [p + [(j, i) for i, j in p] for p in pairs_of]

    turned = jnp.transpose(translations, (0, 2, 1))
    pieces = parts * box_dev
    blocks = pltpu.VMEM((pieces, unknowns, illum), F32)
    whole = shape(devices, rows + turned.shape[1], unknowns)
    packed = call(
        pack_kernel,
        whole,
        (ANY, ANY),
        scratch=(
            blocks,
            pltpu.VMEM(turned.shape, F32),
            pltpu.VMEM(whole.shape, F32),
            pltpu.SemaphoreType.DMA((pieces + 1,)),
            pltpu.SemaphoreType.DMA((pieces + 1,)),
        ),
        limit=FULL,
        name="pack",
        out_kind=ANY,
    )(currents, turned)
    mine = lax.all_to_all(packed, "dir", 0, 0, tiled=True)
    lists = shape(2 * entries + LIST_ROWS, 128, kind=jnp.int32)
    early, late = call(plan_kernel, (lists, lists), (VMEM, VMEM), name="plan")(inter_source.T, inter_shift.T)
    mine, beside, early, late = lax.optimization_barrier((mine, currents, early, late))
    sent = mine[:, :rows]
    from_cross = lax.ppermute(sent, "slab", cross)
    from_same = lax.ppermute(sent, "slab", same)
    left = lax.ppermute(beside, "dir", ring)
    right = lax.ppermute(beside, "dir", [(j, i) for i, j in ring])
    field = shape(boxes, own, width)
    up, down = shape(width, 2 * unknowns, kind=BF16), shape(2 * unknowns, width, kind=BF16)
    radiated, table, up0, up1, down0, down1 = call(
        own_kernel, (field, shape(ops, own, width), up, up, down, down), (VMEM,) * 3, name="own"
    )(mine, aggregate, disaggregate)
    staging = (pltpu.SMEM(lists.shape, jnp.int32), pltpu.SemaphoreType.DMA)
    partial, near_fields = call(
        mid_kernel,
        (field, shape(2 * boxes + 1, own, width)),
        (VMEM,) * 6,
        scratch=staging,
        micros=6,
        name="mid",
    )(early, radiated, table, from_same, up0, up1)
    far = call(
        far_kernel,
        shape(devices, rows, unknowns),
        (VMEM,) * 9,
        scratch=(pltpu.VMEM((3 * boxes, own, width), F32), pltpu.VMEM((boxes, own, width), F32), *staging),
        micros=5,
        name="far",
    )(late, partial, near_fields, table, from_cross, up0, up1, down0, down1)
    back = lax.all_to_all(far, "dir", 0, 0, tiled=True)

    stack = pltpu.VMEM((3 * box_dev, 2 * unknowns, 2 * illum), BF16)
    near = call(
        near_kernel, shape(*currents.shape), (SMEM,) + (VMEM,) * 4, scratch=(stack, stack), micros=20, name="near"
    )(near_index, near_blocks, currents, left, right)
    return call(
        join_kernel,
        shape(*currents.shape),
        (VMEM, VMEM),
        scratch=(blocks, pltpu.SemaphoreType.DMA((pieces,))),
        micros=0,
        name="join",
        out_kind=ANY,
    )(back, near)


def solution(mesh):
    in_specs = (
        P(None, ("slab", "dir"), None, None),
        P(None, ("slab", "dir"), None, None, None),
        P(("slab", "dir"), None),
        P(),
        P(None, None, "dir"),
        P("slab", None),
        P("slab", None),
        P(),
    )
    out_specs = P(None, ("slab", "dir"), None, None)
    return jax.shard_map(body, mesh=mesh, in_specs=in_specs, out_specs=out_specs, check_vma=False)
```

```python
import functools

import jax
import jax.numpy as jnp
from jax import lax
from jax.experimental import pallas as pl
from jax.experimental.pallas import tpu as pltpu
from jax.sharding import PartitionSpec as P

F32, BF16 = jnp.float32, jnp.bfloat16
VMEM = pltpu.MemorySpace.VMEM
SMEM = pltpu.MemorySpace.SMEM
ANY = pl.ANY
MIB = 1 << 20
RE_IM_ROWS = 32
FIRST = 16
PARTS = 4
LIST_ROWS = 8
FULL = 63


def split(x):
    high = x.astype(BF16)
    return high, (x - high.astype(F32)).astype(BF16)


def dot3(left, right, contract):
    def one(a, b):
        return lax.dot_general(a, b, (contract, ((), ())), preferred_element_type=F32)

    return one(left[0], right[0]) + (one(left[0], right[1]) + one(left[1], right[0]))


NN_FORM = ((1,), (0,))
NT_FORM = ((1,), (1,))


def plan_kernel(source_ref, shift_ref, early_ref, late_ref):
    entries, boxes = source_ref.shape
    odd = lax.axis_index("slab") % 2
    source, shift = source_ref[...], shift_ref[...]
    part, place = source // boxes, source % boxes
    away = part == 2 * odd
    where = jnp.where(part == 1, place, jnp.where(away, 2 * boxes + place, boxes + place))
    one = jnp.where(away, 0, 1)
    near_count = jnp.sum(one, axis=0, keepdims=True)
    row = lax.broadcasted_iota(jnp.int32, (entries, boxes), 0)
    to_near, to_away = jnp.zeros((1, boxes), jnp.int32), near_count
    sorted_where = jnp.zeros((entries, boxes), jnp.int32)
    sorted_shift = jnp.zeros((entries, boxes), jnp.int32)
    for i in range(entries):
        is_near = one[i : i + 1]
        here = row == jnp.where(is_near == 1, to_near, to_away)
        sorted_where = jnp.where(here, where[i : i + 1], sorted_where)
        sorted_shift = jnp.where(here, shift[i : i + 1], sorted_shift)
        to_near, to_away = to_near + is_near, to_away + (1 - is_near)
    for ref in (early_ref, late_ref):
        ref[...] = jnp.zeros(ref.shape, jnp.int32)
        ref[entries : 2 * entries, :boxes] = sorted_shift
    early_ref[:entries, :boxes] = jnp.minimum(sorted_where, 2 * boxes)
    late_ref[:entries, :boxes] = sorted_where
    late_ref[2 * entries : 2 * entries + 1, :boxes] = near_count
    across = [lax.broadcasted_iota(jnp.int32, (boxes, boxes), n) for n in range(2)]
    before, same = (across[1] < across[0]).astype(F32), (across[1] == across[0]).astype(F32)
    lanes = late_ref.shape[1]
    slot = lax.broadcasted_iota(jnp.int32, (boxes, lanes), 1).astype(F32)
    box = lax.broadcasted_iota(jnp.int32, (boxes, lanes), 0).astype(F32)
    few = jnp.broadcast_to((near_count < FIRST).astype(F32), (8, boxes))
    rank = lax.dot_general(before, few, (NT_FORM, ((), ())), preferred_element_type=F32)[:, :1]
    flag = lax.dot_general(same, few, (NT_FORM, ((), ())), preferred_element_type=F32)[:, :1]
    listed = jnp.sum(jnp.where((slot == rank) & (flag > 0.5), box, 0.0), axis=0, keepdims=True)
    late_ref[2 * entries + 1 : 2 * entries + 2, :] = listed.astype(jnp.int32)
    total = jnp.sum(few, axis=1, keepdims=True)[:1]
    late_ref[2 * entries + 2 : 2 * entries + 3, :] = jnp.broadcast_to(total, (1, lanes)).astype(jnp.int32)


def pack_kernel(currents_ref, translations_ref, out_ref, block_ref, table_ref, packed_ref, in_sem, out_sem):
    devices, rows, lanes = out_ref.shape
    parts, boxes, _, illum = currents_ref.shape
    own = illum // devices
    pieces = [(c, b) for c in range(parts) for b in range(boxes)]
    last = len(pieces)
    loads = [pltpu.make_async_copy(currents_ref.at[c, b], block_ref.at[n], in_sem.at[n]) for n, (c, b) in enumerate(pieces)]
    loads.append(pltpu.make_async_copy(translations_ref, table_ref, in_sem.at[last]))
    stores = [
        pltpu.make_async_copy(packed_ref.at[:, pl.ds(n * own, own), :], out_ref.at[:, pl.ds(n * own, own), :], out_sem.at[n])
        for n in range(last + 1)
    ]
    for load in loads:
        load.start()
    for n in range(last):
        loads[n].wait()
        packed_ref[:, n * own : (n + 1) * own, :] = block_ref[n].T.reshape(devices, own, lanes)
        stores[n].start()
    loads[last].wait()
    table = jnp.concatenate([table_ref[0], table_ref[1]], axis=1)
    packed_ref[:, last * own :, :] = jnp.broadcast_to(table[None], (devices, own, lanes))
    stores[last].start()
    for store in stores:
        store.wait()


def near_kernel(index_ref, blocks_ref, own_ref, left_ref, right_ref, out_ref, high_ref, low_ref):
    boxes, entries = blocks_ref.shape[1], blocks_ref.shape[2]
    width = own_ref.shape[3]
    for place, ref in enumerate((left_ref, own_ref, right_ref)):
        for b in range(boxes):
            slot = place * boxes + b
            real, imag = split(ref[0, b]), split(ref[1, b])
            for store, x, y in ((high_ref, real[0], imag[0]), (low_ref, real[1], imag[1])):
                store[slot] = jnp.concatenate(
                    [jnp.concatenate([x, y], axis=1), jnp.concatenate([-y, x], axis=1)], axis=0
                )
    for b in range(boxes):

        def step(j, total):
            source = index_ref[b, j]
            block = split(jnp.concatenate([blocks_ref[0, b, j], blocks_ref[1, b, j]], axis=1))
            return total + dot3(block, (high_ref[source], low_ref[source]), NN_FORM)

        total = lax.fori_loop(0, entries, step, jnp.zeros((blocks_ref.shape[3], 2 * width), F32))
        out_ref[0, b] = total[:, :width]
        out_ref[1, b] = total[:, width:]


def radiate(block_ref, weights):
    devices, rows, lanes = block_ref.shape
    half = RE_IM_ROWS // 2
    real = block_ref[:, :half, :].reshape(devices * half, lanes)
    imag = block_ref[:, half : 2 * half, :].reshape(devices * half, lanes)
    return dot3(split(jnp.concatenate([real, imag], axis=1)), weights, NT_FORM)


def complex_rows(ref):
    real, imag = ref[0], ref[1]
    return jnp.concatenate(
        [jnp.concatenate([real, -imag], axis=1), jnp.concatenate([imag, real], axis=1)], axis=0
    )


def own_kernel(own_ref, aggregate_ref, disaggregate_ref, radiated_ref, table_ref, up0_ref, up1_ref, down0_ref, down1_ref):
    boxes, sub, width = radiated_ref.shape
    up = split(complex_rows(aggregate_ref))
    up0_ref[...], up1_ref[...] = up
    down0_ref[...], down1_ref[...] = split(complex_rows(disaggregate_ref))
    radiated_ref[...] = radiate(own_ref, up).reshape(boxes, sub, width)
    devices, rows, lanes = own_ref.shape
    table = own_ref[:, RE_IM_ROWS:, :].reshape(devices * (rows - RE_IM_ROWS), lanes).T
    half = lanes // 2
    wide = jnp.concatenate([table[:half], table[half:]], axis=1)
    table_ref[...] = jnp.broadcast_to(wide[:, None, :], table_ref.shape)


def add_entries(list_ref, g, numbers, total, radiated_ref, table_ref):
    entries = list_ref.shape[0] // 2 - LIST_ROWS // 2
    half = table_ref.shape[2] // 2
    real, imag = total
    for n in numbers:
        q, t = list_ref[n, g], list_ref[entries + n, g]
        xr, xi = radiated_ref[q, :, :half], radiated_ref[q, :, half:]
        tr, ti = table_ref[t, :, :half], table_ref[t, :, half:]
        real, imag = real + (tr * xr - ti * xi), imag + (tr * xi + ti * xr)
    return real, imag


def add_all(list_ref, numbers, start, out_ref, radiated_ref, table_ref):
    half = table_ref.shape[2] // 2

    def one_box(g, carry):
        total = add_entries(list_ref, g, numbers, start(g), radiated_ref, table_ref)
        out_ref[g, :, :half], out_ref[g, :, half:] = total
        return carry

    lax.fori_loop(0, out_ref.shape[0], one_box, 0, unroll=4)


def mid_kernel(
    lists_ref, own_ref, table_ref, block_ref, up0_ref, up1_ref, out_ref, radiated_ref, list_ref, sem
):
    staged = pltpu.make_async_copy(lists_ref, list_ref, sem)
    staged.start()
    boxes, sub, width = own_ref.shape
    radiated_ref[:boxes] = own_ref[...]
    radiated_ref[boxes : 2 * boxes] = radiate(block_ref, (up0_ref[...], up1_ref[...])).reshape(boxes, sub, width)
    radiated_ref[2 * boxes] = jnp.zeros((sub, width), F32)
    staged.wait()
    nothing = jnp.zeros((sub, width // 2), F32)
    add_all(list_ref, range(FIRST), lambda g: (nothing, nothing), out_ref, radiated_ref, table_ref)


def far_kernel(
    lists_ref, mid_ref, near_ref, table_ref, block_ref, up0_ref, up1_ref, down0_ref, down1_ref, out_ref, radiated_ref,
    incoming_ref, rows_ref, store_sem, list_ref, sem,
):
    staged = pltpu.make_async_copy(lists_ref, list_ref, sem)
    staged.start()
    boxes, sub, width = mid_ref.shape
    half = width // 2
    entries = list_ref.shape[0] // 2 - LIST_ROWS // 2
    radiated_ref[: 2 * boxes] = near_ref[: 2 * boxes]
    radiated_ref[2 * boxes :] = radiate(block_ref, (up0_ref[...], up1_ref[...])).reshape(boxes, sub, width)
    staged.wait()
    rest = range(FIRST, entries)
    add_all(
        list_ref, rest, lambda g: (mid_ref[g, :, :half], mid_ref[g, :, half:]), incoming_ref, radiated_ref, table_ref
    )

    def skipped(place, carry):
        g = list_ref[2 * entries + 1, place]

        def one(n, total):
            return add_entries(list_ref, g, (n,), total, radiated_ref, table_ref)

        both = (incoming_ref[g, :, :half], incoming_ref[g, :, half:])
        both = lax.fori_loop(list_ref[2 * entries, g], FIRST, one, both)
        incoming_ref[g, :, :half], incoming_ref[g, :, half:] = both
        return carry

    lax.fori_loop(0, list_ref[2 * entries + 2, 0], skipped, 0)
    down = down0_ref[...], down1_ref[...]
    devices, rows, lanes = out_ref.shape
    half_rows, some, batch = rows // 2, devices // PARTS, boxes // PARTS
    stores = []
    for n in range(PARTS):
        here = pl.ds(n * some, some)
        far = dot3(split(incoming_ref[n * batch : (n + 1) * batch].reshape(batch * sub, width)), down, NT_FORM)
        rows_ref[here, :half_rows, :] = far[:, :lanes].reshape(some, half_rows, lanes)
        rows_ref[here, half_rows:, :] = far[:, lanes:].reshape(some, half_rows, lanes)
        stores.append(pltpu.make_async_copy(rows_ref.at[here], out_ref.at[here], store_sem.at[n]))
        stores[n].start()
    for store in stores:
        store.wait()


def join_kernel(far_ref, near_ref, out_ref, sum_ref, sem):
    parts, boxes, lanes, illum = out_ref.shape
    own = illum // far_ref.shape[0]
    stores = []
    for n, (c, b) in enumerate((c, b) for c in range(parts) for b in range(boxes)):
        turned = far_ref[:, n * own : (n + 1) * own, :].reshape(illum, lanes).T
        sum_ref[n] = near_ref[c, b] + turned
        stores.append(pltpu.make_async_copy(sum_ref.at[n], out_ref.at[c, b], sem.at[n]))
        stores[n].start()
    for store in stores:
        store.wait()


def call(kernel, outs, kinds, scratch=(), limit=16, micros=1, name=None, out_kind=VMEM):
    specs = [pl.BlockSpec(memory_space=kind) for kind in kinds]

    def run(*args):
        moved = 4 * sum(a.size for a in (*args, *jax.tree.leaves(outs)))
        return pl.pallas_call(
            kernel,
            out_shape=outs,
            in_specs=specs,
            out_specs=jax.tree.map(lambda _: pl.BlockSpec(memory_space=out_kind), outs),
            scratch_shapes=list(scratch),
            compiler_params=pltpu.CompilerParams(vmem_limit_bytes=limit * MIB),
            cost_estimate=pl.CostEstimate(flops=micros * 1_000_000_000, bytes_accessed=moved, transcendentals=0),
            name=name,
        )(*args)

    return run


def shape(*dims, kind=F32):
    return jax.ShapeDtypeStruct(dims, kind)


def body(currents, near_blocks, near_index, aggregate, translations, inter_source, inter_shift, disaggregate):
    devices = lax.axis_size("dir")
    slabs = lax.axis_size("slab")
    parts, box_dev, unknowns, illum = currents.shape
    own = illum // devices
    width = 2 * aggregate.shape[1]
    boxes, entries = inter_source.shape
    ops = translations.shape[1]
    rows = parts * box_dev * own
    ring = [(i, (i + 1) % devices) for i in range(devices)]
    pairs_of = [[(i, i + 1) for i in range(start, slabs - 1, 2)] for start in (0, 1)]
    same, cross = [p + [(j, i) for i, j in p] for p in pairs_of]

    turned = jnp.transpose(translations, (0, 2, 1))
    pieces = parts * box_dev
    blocks = pltpu.VMEM((pieces, unknowns, illum), F32)
    whole = shape(devices, rows + turned.shape[1], unknowns)
    packed = call(
        pack_kernel,
        whole,
        (ANY, ANY),
        scratch=(
            blocks,
            pltpu.VMEM(turned.shape, F32),
            pltpu.VMEM(whole.shape, F32),
            pltpu.SemaphoreType.DMA((pieces + 1,)),
            pltpu.SemaphoreType.DMA((pieces + 1,)),
        ),
        limit=FULL,
        name="pack",
        out_kind=ANY,
    )(currents, turned)
    mine = lax.all_to_all(packed, "dir", 0, 0, tiled=True)
    lists = shape(2 * entries + LIST_ROWS, 128, kind=jnp.int32)
    early, late = call(plan_kernel, (lists, lists), (VMEM, VMEM), name="plan")(inter_source.T, inter_shift.T)
    mine, beside, early, late = lax.optimization_barrier((mine, currents, early, late))
    sent = mine[:, :rows]
    from_cross = lax.ppermute(sent, "slab", cross)
    from_same = lax.ppermute(sent, "slab", same)
    left = lax.ppermute(beside, "dir", ring)
    right = lax.ppermute(beside, "dir", [(j, i) for i, j in ring])
    field = shape(boxes, own, width)
    up, down = shape(width, 2 * unknowns, kind=BF16), shape(2 * unknowns, width, kind=BF16)
    radiated, table, up0, up1, down0, down1 = call(
        own_kernel, (field, shape(ops, own, width), up, up, down, down), (VMEM,) * 3, name="own"
    )(mine, aggregate, disaggregate)
    staging = (pltpu.SMEM(lists.shape, jnp.int32), pltpu.SemaphoreType.DMA)
    partial, near_fields = call(
        mid_kernel,
        (field, shape(2 * boxes + 1, own, width)),
        (VMEM,) * 6,
        scratch=staging,
        micros=6,
        name="mid",
    )(early, radiated, table, from_same, up0, up1)
    far = call(
        far_kernel,
        shape(devices, rows, unknowns),
        (VMEM,) * 9,
        scratch=(
            pltpu.VMEM((3 * boxes, own, width), F32),
            pltpu.VMEM((boxes, own, width), F32),
            pltpu.VMEM((devices, rows, unknowns), F32),
            pltpu.SemaphoreType.DMA((PARTS,)),
            *staging,
        ),
        micros=5,
        name="far",
        out_kind=ANY,
    )(late, partial, near_fields, table, from_cross, up0, up1, down0, down1)
    back = lax.all_to_all(far, "dir", 0, 0, tiled=True)

    stack = pltpu.VMEM((3 * box_dev, 2 * unknowns, 2 * illum), BF16)
    near = call(
        near_kernel, shape(*currents.shape), (SMEM,) + (VMEM,) * 4, scratch=(stack, stack), micros=20, name="near"
    )(near_index, near_blocks, currents, left, right)
    return call(
        join_kernel,
        shape(*currents.shape),
        (VMEM, VMEM),
        scratch=(blocks, pltpu.SemaphoreType.DMA((pieces,))),
        micros=0,
        name="join",
        out_kind=ANY,
    )(back, near)


def solution(mesh):
    in_specs = (
        P(None, ("slab", "dir"), None, None),
        P(None, ("slab", "dir"), None, None, None),
        P(("slab", "dir"), None),
        P(),
        P(None, None, "dir"),
        P("slab", None),
        P("slab", None),
        P(),
    )
    out_specs = P(None, ("slab", "dir"), None, None)
    return jax.shard_map(body, mesh=mesh, in_specs=in_specs, out_specs=out_specs, check_vma=False)
```

```python
import functools

import jax
import jax.numpy as jnp
from jax import lax
from jax.experimental import pallas as pl
from jax.experimental.pallas import tpu as pltpu
from jax.sharding import PartitionSpec as P

F32, BF16 = jnp.float32, jnp.bfloat16
VMEM = pltpu.MemorySpace.VMEM
SMEM = pltpu.MemorySpace.SMEM
ANY = pl.ANY
MIB = 1 << 20
RE_IM_ROWS = 32
FIRST = 16
PARTS = 2
HALVES = 2
LIST_ROWS = 8
FULL = 63


def split(x):
    high = x.astype(BF16)
    return high, (x - high.astype(F32)).astype(BF16)


def dot3(left, right, contract):
    def one(a, b):
        return lax.dot_general(a, b, (contract, ((), ())), preferred_element_type=F32)

    return one(left[0], right[0]) + (one(left[0], right[1]) + one(left[1], right[0]))


NN_FORM = ((1,), (0,))
NT_FORM = ((1,), (1,))


def plan_kernel(
    source_ref, shift_ref, aggregate_ref, disaggregate_ref, early_ref, late_ref, up0_ref, up1_ref, down0_ref, down1_ref
):
    up0_ref[...], up1_ref[...] = split(complex_rows(aggregate_ref))
    down0_ref[...], down1_ref[...] = split(complex_rows(disaggregate_ref))
    entries, boxes = source_ref.shape
    odd = lax.axis_index("slab") % 2
    source, shift = source_ref[...], shift_ref[...]
    part, place = source // boxes, source % boxes
    away = part == 2 * odd
    where = jnp.where(part == 1, place, jnp.where(away, 2 * boxes + place, boxes + place))
    one = jnp.where(away, 0, 1)
    near_count = jnp.sum(one, axis=0, keepdims=True)
    row = lax.broadcasted_iota(jnp.int32, (entries, boxes), 0)
    to_near, to_away = jnp.zeros((1, boxes), jnp.int32), near_count
    sorted_where = jnp.zeros((entries, boxes), jnp.int32)
    sorted_shift = jnp.zeros((entries, boxes), jnp.int32)
    for i in range(entries):
        is_near = one[i : i + 1]
        here = row == jnp.where(is_near == 1, to_near, to_away)
        sorted_where = jnp.where(here, where[i : i + 1], sorted_where)
        sorted_shift = jnp.where(here, shift[i : i + 1], sorted_shift)
        to_near, to_away = to_near + is_near, to_away + (1 - is_near)
    for ref in (early_ref, late_ref):
        ref[...] = jnp.zeros(ref.shape, jnp.int32)
        ref[entries : 2 * entries, :boxes] = sorted_shift
    early_ref[:entries, :boxes] = jnp.minimum(sorted_where, 2 * boxes)
    late_ref[:entries, :boxes] = sorted_where
    late_ref[2 * entries : 2 * entries + 1, :boxes] = near_count
    across = [lax.broadcasted_iota(jnp.int32, (boxes, boxes), n) for n in range(2)]
    before, same = (across[1] < across[0]).astype(F32), (across[1] == across[0]).astype(F32)
    lanes = late_ref.shape[1]
    slot = lax.broadcasted_iota(jnp.int32, (boxes, lanes), 1).astype(F32)
    box = lax.broadcasted_iota(jnp.int32, (boxes, lanes), 0).astype(F32)
    few = jnp.broadcast_to((near_count < FIRST).astype(F32), (8, boxes))
    rank = lax.dot_general(before, few, (NT_FORM, ((), ())), preferred_element_type=F32)[:, :1]
    flag = lax.dot_general(same, few, (NT_FORM, ((), ())), preferred_element_type=F32)[:, :1]
    listed = jnp.sum(jnp.where((slot == rank) & (flag > 0.5), box, 0.0), axis=0, keepdims=True)
    late_ref[2 * entries + 1 : 2 * entries + 2, :] = listed.astype(jnp.int32)
    total = jnp.sum(few, axis=1, keepdims=True)[:1]
    late_ref[2 * entries + 2 : 2 * entries + 3, :] = jnp.broadcast_to(total, (1, lanes)).astype(jnp.int32)


def pack_kernel(currents_ref, translations_ref, out_ref, block_ref, table_ref, packed_ref, in_sem, out_sem):
    devices, _, lanes = out_ref.shape
    parts, boxes, _, illum = currents_ref.shape
    own = illum // devices
    pieces = parts * boxes
    some, columns = devices // HALVES, illum // HALVES
    table_load = pltpu.make_async_copy(translations_ref, table_ref, in_sem.at[HALVES * pieces])
    loads = []
    for h in range(HALVES):
        for n in range(pieces):
            piece = currents_ref.at[n // boxes, n % boxes, :, pl.ds(h * columns, columns)]
            loads.append(pltpu.make_async_copy(piece, block_ref.at[h, n], in_sem.at[h * pieces + n]))
    table_load.start()
    for load in loads:
        load.start()
    table_load.wait()
    table = jnp.concatenate([table_ref[0], table_ref[1]], axis=1)
    packed_ref[:, pieces * own :, :] = jnp.broadcast_to(table[None], (devices, table.shape[0], lanes))
    stores = []
    for h in range(HALVES):
        here = pl.ds(h * some, some)
        for n in range(pieces):
            loads[h * pieces + n].wait()
            packed_ref[here, n * own : (n + 1) * own, :] = block_ref[h, n].T.reshape(some, own, lanes)
        stores.append(pltpu.make_async_copy(packed_ref.at[here], out_ref.at[here], out_sem.at[h]))
        stores[h].start()
    for store in stores:
        store.wait()


def near_kernel(index_ref, blocks_ref, own_ref, left_ref, right_ref, out_ref, high_ref, low_ref):
    boxes, entries = blocks_ref.shape[1], blocks_ref.shape[2]
    width = own_ref.shape[3]
    for place, ref in enumerate((left_ref, own_ref, right_ref)):
        for b in range(boxes):
            slot = place * boxes + b
            real, imag = split(ref[0, b]), split(ref[1, b])
            for store, x, y in ((high_ref, real[0], imag[0]), (low_ref, real[1], imag[1])):
                store[slot] = jnp.concatenate(
                    [jnp.concatenate([x, y], axis=1), jnp.concatenate([-y, x], axis=1)], axis=0
                )
    for b in range(boxes):

        def step(j, total):
            source = index_ref[b, j]
            block = split(jnp.concatenate([blocks_ref[0, b, j], blocks_ref[1, b, j]], axis=1))
            return total + dot3(block, (high_ref[source], low_ref[source]), NN_FORM)

        total = lax.fori_loop(0, entries, step, jnp.zeros((blocks_ref.shape[3], 2 * width), F32))
        out_ref[0, b] = total[:, :width]
        out_ref[1, b] = total[:, width:]


def radiate(block_ref, weights):
    devices, rows, lanes = block_ref.shape
    half = RE_IM_ROWS // 2
    real = block_ref[:, :half, :].reshape(devices * half, lanes)
    imag = block_ref[:, half : 2 * half, :].reshape(devices * half, lanes)
    return dot3(split(jnp.concatenate([real, imag], axis=1)), weights, NT_FORM)


def complex_rows(ref):
    real, imag = ref[0], ref[1]
    return jnp.concatenate(
        [jnp.concatenate([real, -imag], axis=1), jnp.concatenate([imag, real], axis=1)], axis=0
    )


def own_kernel(own_ref, up0_ref, up1_ref, radiated_ref, table_ref):
    boxes, sub, width = radiated_ref.shape
    radiated_ref[...] = radiate(own_ref, (up0_ref[...], up1_ref[...])).reshape(boxes, sub, width)
    devices, rows, lanes = own_ref.shape
    table = own_ref[:, RE_IM_ROWS:, :].reshape(devices * (rows - RE_IM_ROWS), lanes).T
    half = lanes // 2
    wide = jnp.concatenate([table[:half], table[half:]], axis=1)
    table_ref[...] = jnp.broadcast_to(wide[:, None, :], table_ref.shape)


def add_entries(list_ref, g, numbers, total, radiated_ref, table_ref):
    entries = list_ref.shape[0] // 2 - LIST_ROWS // 2
    half = table_ref.shape[2] // 2
    real, imag = total
    for n in numbers:
        q, t = list_ref[n, g], list_ref[entries + n, g]
        xr, xi = radiated_ref[q, :, :half], radiated_ref[q, :, half:]
        tr, ti = table_ref[t, :, :half], table_ref[t, :, half:]
        real, imag = real + (tr * xr - ti * xi), imag + (tr * xi + ti * xr)
    return real, imag


def add_all(list_ref, numbers, start, out_ref, radiated_ref, table_ref):
    half = table_ref.shape[2] // 2

    def one_box(g, carry):
        total = add_entries(list_ref, g, numbers, start(g), radiated_ref, table_ref)
        out_ref[g, :, :half], out_ref[g, :, half:] = total
        return carry

    lax.fori_loop(0, out_ref.shape[0], one_box, 0, unroll=4)


def mid_kernel(
    lists_ref, own_ref, table_ref, block_ref, up0_ref, up1_ref, out_ref, radiated_ref, list_ref, sem
):
    staged = pltpu.make_async_copy(lists_ref, list_ref, sem)
    staged.start()
    boxes, sub, width = own_ref.shape
    radiated_ref[:boxes] = own_ref[...]
    radiated_ref[boxes : 2 * boxes] = radiate(block_ref, (up0_ref[...], up1_ref[...])).reshape(boxes, sub, width)
    radiated_ref[2 * boxes] = jnp.zeros((sub, width), F32)
    staged.wait()
    nothing = jnp.zeros((sub, width // 2), F32)
    add_all(list_ref, range(FIRST), lambda g: (nothing, nothing), out_ref, radiated_ref, table_ref)


def far_kernel(
    lists_ref, mid_ref, near_ref, table_ref, block_ref, up0_ref, up1_ref, down0_ref, down1_ref, out_ref, radiated_ref,
    incoming_ref, rows_ref, store_sem, list_ref, sem,
):
    staged = pltpu.make_async_copy(lists_ref, list_ref, sem)
    staged.start()
    boxes, sub, width = mid_ref.shape
    half = width // 2
    entries = list_ref.shape[0] // 2 - LIST_ROWS // 2
    radiated_ref[: 2 * boxes] = near_ref[: 2 * boxes]
    radiated_ref[2 * boxes :] = radiate(block_ref, (up0_ref[...], up1_ref[...])).reshape(boxes, sub, width)
    staged.wait()
    rest = range(FIRST, entries)
    add_all(
        list_ref, rest, lambda g: (mid_ref[g, :, :half], mid_ref[g, :, half:]), incoming_ref, radiated_ref, table_ref
    )

    def skipped(place, carry):
        g = list_ref[2 * entries + 1, place]

        def one(n, total):
            return add_entries(list_ref, g, (n,), total, radiated_ref, table_ref)

        both = (incoming_ref[g, :, :half], incoming_ref[g, :, half:])
        both = lax.fori_loop(list_ref[2 * entries, g], FIRST, one, both)
        incoming_ref[g, :, :half], incoming_ref[g, :, half:] = both
        return carry

    lax.fori_loop(0, list_ref[2 * entries + 2, 0], skipped, 0)
    down = down0_ref[...], down1_ref[...]
    devices, rows, lanes = out_ref.shape
    half_rows, some, batch = rows // 2, devices // PARTS, boxes // PARTS
    stores = []
    for n in range(PARTS):
        here = pl.ds(n * some, some)
        far = dot3(split(incoming_ref[n * batch : (n + 1) * batch].reshape(batch * sub, width)), down, NT_FORM)
        rows_ref[here, :half_rows, :] = far[:, :lanes].reshape(some, half_rows, lanes)
        rows_ref[here, half_rows:, :] = far[:, lanes:].reshape(some, half_rows, lanes)
        stores.append(pltpu.make_async_copy(rows_ref.at[here], out_ref.at[here], store_sem.at[n]))
        stores[n].start()
    for store in stores:
        store.wait()


def join_kernel(far_ref, near_ref, out_ref, sum_ref, sem):
    parts, boxes, lanes, illum = out_ref.shape
    own = illum // far_ref.shape[0]
    stores = []
    for n, (c, b) in enumerate((c, b) for c in range(parts) for b in range(boxes)):
        turned = far_ref[:, n * own : (n + 1) * own, :].reshape(illum, lanes).T
        sum_ref[n] = near_ref[c, b] + turned
        stores.append(pltpu.make_async_copy(sum_ref.at[n], out_ref.at[c, b], sem.at[n]))
        stores[n].start()
    for store in stores:
        store.wait()


def call(kernel, outs, kinds, scratch=(), limit=16, micros=1, name=None, out_kind=VMEM):
    specs = [pl.BlockSpec(memory_space=kind) for kind in kinds]

    def run(*args):
        moved = 4 * sum(a.size for a in (*args, *jax.tree.leaves(outs)))
        return pl.pallas_call(
            kernel,
            out_shape=outs,
            in_specs=specs,
            out_specs=jax.tree.map(lambda _: pl.BlockSpec(memory_space=out_kind), outs),
            scratch_shapes=list(scratch),
            compiler_params=pltpu.CompilerParams(vmem_limit_bytes=limit * MIB),
            cost_estimate=pl.CostEstimate(flops=micros * 1_000_000_000, bytes_accessed=moved, transcendentals=0),
            name=name,
        )(*args)

    return run


def shape(*dims, kind=F32):
    return jax.ShapeDtypeStruct(dims, kind)


def body(currents, near_blocks, near_index, aggregate, translations, inter_source, inter_shift, disaggregate):
    devices = lax.axis_size("dir")
    slabs = lax.axis_size("slab")
    parts, box_dev, unknowns, illum = currents.shape
    own = illum // devices
    width = 2 * aggregate.shape[1]
    boxes, entries = inter_source.shape
    ops = translations.shape[1]
    rows = parts * box_dev * own
    ring = [(i, (i + 1) % devices) for i in range(devices)]
    pairs_of = [[(i, i + 1) for i in range(start, slabs - 1, 2)] for start in (0, 1)]
    same, cross = [p + [(j, i) for i, j in p] for p in pairs_of]

    turned = jnp.transpose(translations, (0, 2, 1))
    pieces = parts * box_dev
    blocks = pltpu.VMEM((pieces, unknowns, illum), F32)
    whole = shape(devices, rows + turned.shape[1], unknowns)
    packed = call(
        pack_kernel,
        whole,
        (ANY, ANY),
        scratch=(
            pltpu.VMEM((HALVES, pieces, unknowns, illum // HALVES), F32),
            pltpu.VMEM(turned.shape, F32),
            pltpu.VMEM(whole.shape, F32),
            pltpu.SemaphoreType.DMA((HALVES * pieces + 1,)),
            pltpu.SemaphoreType.DMA((HALVES,)),
        ),
        limit=FULL,
        name="pack",
        out_kind=ANY,
    )(currents, turned)
    mine = lax.all_to_all(packed, "dir", 0, 0, tiled=True)
    lists = shape(2 * entries + LIST_ROWS, 128, kind=jnp.int32)
    up, down = shape(width, 2 * unknowns, kind=BF16), shape(2 * unknowns, width, kind=BF16)
    planned = call(plan_kernel, (lists, lists, up, up, down, down), (VMEM,) * 4, name="plan")(
        inter_source.T, inter_shift.T, aggregate, disaggregate
    )
    mine, beside, planned = lax.optimization_barrier((mine, currents, planned))
    early, late, up0, up1, down0, down1 = planned
    sent = mine[:, :rows]
    from_cross = lax.ppermute(sent, "slab", cross)
    from_same = lax.ppermute(sent, "slab", same)
    left = lax.ppermute(beside, "dir", ring)
    right = lax.ppermute(beside, "dir", [(j, i) for i, j in ring])
    field = shape(boxes, own, width)
    radiated, table = call(own_kernel, (field, shape(ops, own, width)), (VMEM,) * 3, micros=0, name="own")(mine, up0, up1)
    staging = (pltpu.SMEM(lists.shape, jnp.int32), pltpu.SemaphoreType.DMA)
    partial, near_fields = call(
        mid_kernel,
        (field, shape(2 * boxes + 1, own, width)),
        (VMEM,) * 6,
        scratch=staging,
        micros=0,
        name="mid",
    )(early, radiated, table, from_same, up0, up1)
    far = call(
        far_kernel,
        shape(devices, rows, unknowns),
        (VMEM,) * 9,
        scratch=(
            pltpu.VMEM((3 * boxes, own, width), F32),
            pltpu.VMEM((boxes, own, width), F32),
            pltpu.VMEM((devices, rows, unknowns), F32),
            pltpu.SemaphoreType.DMA((PARTS,)),
            *staging,
        ),
        micros=0,
        name="far",
        out_kind=ANY,
    )(late, partial, near_fields, table, from_cross, up0, up1, down0, down1)
    back = lax.all_to_all(far, "dir", 0, 0, tiled=True)

    stack = pltpu.VMEM((3 * box_dev, 2 * unknowns, 2 * illum), BF16)
    near = call(
        near_kernel, shape(*currents.shape), (SMEM,) + (VMEM,) * 4, scratch=(stack, stack), micros=20, name="near"
    )(near_index, near_blocks, currents, left, right)
    return call(
        join_kernel,
        shape(*currents.shape),
        (VMEM, VMEM),
        scratch=(blocks, pltpu.SemaphoreType.DMA((pieces,))),
        micros=0,
        name="join",
        out_kind=ANY,
    )(back, near)


def solution(mesh):
    in_specs = (
        P(None, ("slab", "dir"), None, None),
        P(None, ("slab", "dir"), None, None, None),
        P(("slab", "dir"), None),
        P(),
        P(None, None, "dir"),
        P("slab", None),
        P("slab", None),
        P(),
    )
    out_specs = P(None, ("slab", "dir"), None, None)
    return jax.shard_map(body, mesh=mesh, in_specs=in_specs, out_specs=out_specs, check_vma=False)
```

```python
import functools

import jax
import jax.numpy as jnp
from jax import lax
from jax.experimental import pallas as pl
from jax.experimental.pallas import tpu as pltpu
from jax.sharding import PartitionSpec as P

F32, BF16 = jnp.float32, jnp.bfloat16
VMEM = pltpu.MemorySpace.VMEM
SMEM = pltpu.MemorySpace.SMEM
ANY = pl.ANY
MIB = 1 << 20
RE_IM_ROWS = 32
FIRST = 16
PARTS = 2
LIST_ROWS = 8
FULL = 63


def split(x):
    high = x.astype(BF16)
    return high, (x - high.astype(F32)).astype(BF16)


def dot3(left, right, contract):
    def one(a, b):
        return lax.dot_general(a, b, (contract, ((), ())), preferred_element_type=F32)

    return one(left[0], right[0]) + (one(left[0], right[1]) + one(left[1], right[0]))


NN_FORM = ((1,), (0,))
NT_FORM = ((1,), (1,))


def plan_kernel(
    source_ref, shift_ref, aggregate_ref, disaggregate_ref, early_ref, late_ref, up0_ref, up1_ref, down0_ref, down1_ref
):
    up0_ref[...], up1_ref[...] = split(complex_rows(aggregate_ref))
    down0_ref[...], down1_ref[...] = split(complex_rows(disaggregate_ref))
    entries, boxes = source_ref.shape
    odd = lax.axis_index("slab") % 2
    source, shift = source_ref[...], shift_ref[...]
    part, place = source // boxes, source % boxes
    away = part == 2 * odd
    where = jnp.where(part == 1, place, jnp.where(away, 2 * boxes + place, boxes + place))
    one = jnp.where(away, 0, 1)
    near_count = jnp.sum(one, axis=0, keepdims=True)
    row = lax.broadcasted_iota(jnp.int32, (entries, boxes), 0)
    to_near, to_away = jnp.zeros((1, boxes), jnp.int32), near_count
    sorted_where = jnp.zeros((entries, boxes), jnp.int32)
    sorted_shift = jnp.zeros((entries, boxes), jnp.int32)
    for i in range(entries):
        is_near = one[i : i + 1]
        here = row == jnp.where(is_near == 1, to_near, to_away)
        sorted_where = jnp.where(here, where[i : i + 1], sorted_where)
        sorted_shift = jnp.where(here, shift[i : i + 1], sorted_shift)
        to_near, to_away = to_near + is_near, to_away + (1 - is_near)
    for ref in (early_ref, late_ref):
        ref[...] = jnp.zeros(ref.shape, jnp.int32)
        ref[entries : 2 * entries, :boxes] = sorted_shift
    early_ref[:entries, :boxes] = jnp.minimum(sorted_where, 2 * boxes)
    late_ref[:entries, :boxes] = sorted_where
    late_ref[2 * entries : 2 * entries + 1, :boxes] = near_count
    across = [lax.broadcasted_iota(jnp.int32, (boxes, boxes), n) for n in range(2)]
    before, same = (across[1] < across[0]).astype(F32), (across[1] == across[0]).astype(F32)
    lanes = late_ref.shape[1]
    slot = lax.broadcasted_iota(jnp.int32, (boxes, lanes), 1).astype(F32)
    box = lax.broadcasted_iota(jnp.int32, (boxes, lanes), 0).astype(F32)
    few = jnp.broadcast_to((near_count < FIRST).astype(F32), (8, boxes))
    rank = lax.dot_general(before, few, (NT_FORM, ((), ())), preferred_element_type=F32)[:, :1]
    flag = lax.dot_general(same, few, (NT_FORM, ((), ())), preferred_element_type=F32)[:, :1]
    listed = jnp.sum(jnp.where((slot == rank) & (flag > 0.5), box, 0.0), axis=0, keepdims=True)
    late_ref[2 * entries + 1 : 2 * entries + 2, :] = listed.astype(jnp.int32)
    total = jnp.sum(few, axis=1, keepdims=True)[:1]
    late_ref[2 * entries + 2 : 2 * entries + 3, :] = jnp.broadcast_to(total, (1, lanes)).astype(jnp.int32)


def pack_kernel(currents_ref, translations_ref, out_ref, block_ref, table_ref, packed_ref, in_sem, out_sem):
    devices, rows, lanes = out_ref.shape
    parts, boxes, _, illum = currents_ref.shape
    own = illum // devices
    pieces = [(c, b) for c in range(parts) for b in range(boxes)]
    last = len(pieces)
    loads = [pltpu.make_async_copy(currents_ref.at[c, b], block_ref.at[n], in_sem.at[n]) for n, (c, b) in enumerate(pieces)]
    loads.append(pltpu.make_async_copy(translations_ref, table_ref, in_sem.at[last]))
    stores = [
        pltpu.make_async_copy(packed_ref.at[:, pl.ds(n * own, own), :], out_ref.at[:, pl.ds(n * own, own), :], out_sem.at[n])
        for n in range(last + 1)
    ]
    for load in [loads[last], *loads[:last]]:
        load.start()
    loads[last].wait()
    table = jnp.concatenate([table_ref[0], table_ref[1]], axis=1)
    packed_ref[:, last * own :, :] = jnp.broadcast_to(table[None], (devices, own, lanes))
    stores[last].start()
    for n in range(last):
        loads[n].wait()
        packed_ref[:, n * own : (n + 1) * own, :] = block_ref[n].T.reshape(devices, own, lanes)
        stores[n].start()
    for store in stores:
        store.wait()


def near_kernel(index_ref, blocks_ref, own_ref, left_ref, right_ref, out_ref, high_ref, low_ref):
    boxes, entries = blocks_ref.shape[1], blocks_ref.shape[2]
    width = own_ref.shape[3]
    for place, ref in enumerate((left_ref, own_ref, right_ref)):
        for b in range(boxes):
            slot = place * boxes + b
            real, imag = split(ref[0, b]), split(ref[1, b])
            for store, x, y in ((high_ref, real[0], imag[0]), (low_ref, real[1], imag[1])):
                store[slot] = jnp.concatenate(
                    [jnp.concatenate([x, y], axis=1), jnp.concatenate([-y, x], axis=1)], axis=0
                )
    for b in range(boxes):

        def step(j, total):
            source = index_ref[b, j]
            block = split(jnp.concatenate([blocks_ref[0, b, j], blocks_ref[1, b, j]], axis=1))
            return total + dot3(block, (high_ref[source], low_ref[source]), NN_FORM)

        total = lax.fori_loop(0, entries, step, jnp.zeros((blocks_ref.shape[3], 2 * width), F32))
        out_ref[0, b] = total[:, :width]
        out_ref[1, b] = total[:, width:]


def radiate(block_ref, weights):
    devices, rows, lanes = block_ref.shape
    half = RE_IM_ROWS // 2
    real = block_ref[:, :half, :].reshape(devices * half, lanes)
    imag = block_ref[:, half : 2 * half, :].reshape(devices * half, lanes)
    return dot3(split(jnp.concatenate([real, imag], axis=1)), weights, NT_FORM)


def complex_rows(ref):
    real, imag = ref[0], ref[1]
    return jnp.concatenate(
        [jnp.concatenate([real, -imag], axis=1), jnp.concatenate([imag, real], axis=1)], axis=0
    )


def own_kernel(own_ref, up0_ref, up1_ref, radiated_ref, table_ref):
    boxes, sub, width = radiated_ref.shape
    radiated_ref[...] = radiate(own_ref, (up0_ref[...], up1_ref[...])).reshape(boxes, sub, width)
    devices, rows, lanes = own_ref.shape
    table = own_ref[:, RE_IM_ROWS:, :].reshape(devices * (rows - RE_IM_ROWS), lanes).T
    half = lanes // 2
    wide = jnp.concatenate([table[:half], table[half:]], axis=1)
    table_ref[...] = jnp.broadcast_to(wide[:, None, :], table_ref.shape)


def add_entries(list_ref, g, numbers, total, radiated_ref, table_ref):
    entries = list_ref.shape[0] // 2 - LIST_ROWS // 2
    half = table_ref.shape[2] // 2
    real, imag = total
    for n in numbers:
        q, t = list_ref[n, g], list_ref[entries + n, g]
        xr, xi = radiated_ref[q, :, :half], radiated_ref[q, :, half:]
        tr, ti = table_ref[t, :, :half], table_ref[t, :, half:]
        real, imag = real + (tr * xr - ti * xi), imag + (tr * xi + ti * xr)
    return real, imag


def add_all(list_ref, numbers, start, out_ref, radiated_ref, table_ref):
    half = table_ref.shape[2] // 2

    def one_box(g, carry):
        total = add_entries(list_ref, g, numbers, start(g), radiated_ref, table_ref)
        out_ref[g, :, :half], out_ref[g, :, half:] = total
        return carry

    lax.fori_loop(0, out_ref.shape[0], one_box, 0, unroll=4)


def mid_kernel(
    lists_ref, own_ref, table_ref, block_ref, up0_ref, up1_ref, out_ref, radiated_ref, list_ref, sem
):
    staged = pltpu.make_async_copy(lists_ref, list_ref, sem)
    staged.start()
    boxes, sub, width = own_ref.shape
    radiated_ref[:boxes] = own_ref[...]
    radiated_ref[boxes : 2 * boxes] = radiate(block_ref, (up0_ref[...], up1_ref[...])).reshape(boxes, sub, width)
    radiated_ref[2 * boxes] = jnp.zeros((sub, width), F32)
    staged.wait()
    nothing = jnp.zeros((sub, width // 2), F32)
    add_all(list_ref, range(FIRST), lambda g: (nothing, nothing), out_ref, radiated_ref, table_ref)


def far_kernel(
    lists_ref, mid_ref, near_ref, table_ref, block_ref, up0_ref, up1_ref, down0_ref, down1_ref, out_ref, radiated_ref,
    incoming_ref, rows_ref, store_sem, list_ref, sem,
):
    staged = pltpu.make_async_copy(lists_ref, list_ref, sem)
    staged.start()
    boxes, sub, width = mid_ref.shape
    half = width // 2
    entries = list_ref.shape[0] // 2 - LIST_ROWS // 2
    radiated_ref[: 2 * boxes] = near_ref[: 2 * boxes]
    radiated_ref[2 * boxes :] = radiate(block_ref, (up0_ref[...], up1_ref[...])).reshape(boxes, sub, width)
    staged.wait()
    rest = range(FIRST, entries)
    add_all(
        list_ref, rest, lambda g: (mid_ref[g, :, :half], mid_ref[g, :, half:]), incoming_ref, radiated_ref, table_ref
    )

    def skipped(place, carry):
        g = list_ref[2 * entries + 1, place]

        def one(n, total):
            return add_entries(list_ref, g, (n,), total, radiated_ref, table_ref)

        both = (incoming_ref[g, :, :half], incoming_ref[g, :, half:])
        both = lax.fori_loop(list_ref[2 * entries, g], FIRST, one, both)
        incoming_ref[g, :, :half], incoming_ref[g, :, half:] = both
        return carry

    lax.fori_loop(0, list_ref[2 * entries + 2, 0], skipped, 0)
    down = down0_ref[...], down1_ref[...]
    devices, rows, lanes = out_ref.shape
    half_rows, some, batch = rows // 2, devices // PARTS, boxes // PARTS
    stores = []
    for n in range(PARTS):
        here = pl.ds(n * some, some)
        far = dot3(split(incoming_ref[n * batch : (n + 1) * batch].reshape(batch * sub, width)), down, NT_FORM)
        rows_ref[here, :half_rows, :] = far[:, :lanes].reshape(some, half_rows, lanes)
        rows_ref[here, half_rows:, :] = far[:, lanes:].reshape(some, half_rows, lanes)
        stores.append(pltpu.make_async_copy(rows_ref.at[here], out_ref.at[here], store_sem.at[n]))
        stores[n].start()
    for store in stores:
        store.wait()


def join_kernel(far_ref, near_ref, out_ref, sum_ref, sem):
    parts, boxes, lanes, illum = out_ref.shape
    own = illum // far_ref.shape[0]
    stores = []
    for n, (c, b) in enumerate((c, b) for c in range(parts) for b in range(boxes)):
        turned = far_ref[:, n * own : (n + 1) * own, :].reshape(illum, lanes).T
        sum_ref[n] = near_ref[c, b] + turned
        stores.append(pltpu.make_async_copy(sum_ref.at[n], out_ref.at[c, b], sem.at[n]))
        stores[n].start()
    for store in stores:
        store.wait()


def call(kernel, outs, kinds, scratch=(), limit=16, micros=1, name=None, out_kind=VMEM):
    specs = [pl.BlockSpec(memory_space=kind) for kind in kinds]

    def run(*args):
        moved = 4 * sum(a.size for a in (*args, *jax.tree.leaves(outs)))
        return pl.pallas_call(
            kernel,
            out_shape=outs,
            in_specs=specs,
            out_specs=jax.tree.map(lambda _: pl.BlockSpec(memory_space=out_kind), outs),
            scratch_shapes=list(scratch),
            compiler_params=pltpu.CompilerParams(vmem_limit_bytes=limit * MIB),
            cost_estimate=pl.CostEstimate(flops=micros * 1_000_000_000, bytes_accessed=moved, transcendentals=0),
            name=name,
        )(*args)

    return run


def shape(*dims, kind=F32):
    return jax.ShapeDtypeStruct(dims, kind)


def body(currents, near_blocks, near_index, aggregate, translations, inter_source, inter_shift, disaggregate):
    devices = lax.axis_size("dir")
    slabs = lax.axis_size("slab")
    parts, box_dev, unknowns, illum = currents.shape
    own = illum // devices
    width = 2 * aggregate.shape[1]
    boxes, entries = inter_source.shape
    ops = translations.shape[1]
    rows = parts * box_dev * own
    ring = [(i, (i + 1) % devices) for i in range(devices)]
    pairs_of = [[(i, i + 1) for i in range(start, slabs - 1, 2)] for start in (0, 1)]
    same, cross = [p + [(j, i) for i, j in p] for p in pairs_of]

    turned = jnp.transpose(translations, (0, 2, 1))
    pieces = parts * box_dev
    blocks = pltpu.VMEM((pieces, unknowns, illum), F32)
    whole = shape(devices, rows + turned.shape[1], unknowns)
    packed = call(
        pack_kernel,
        whole,
        (ANY, ANY),
        scratch=(
            blocks,
            pltpu.VMEM(turned.shape, F32),
            pltpu.VMEM(whole.shape, F32),
            pltpu.SemaphoreType.DMA((pieces + 1,)),
            pltpu.SemaphoreType.DMA((pieces + 1,)),
        ),
        limit=FULL,
        name="pack",
        out_kind=ANY,
    )(currents, turned)
    mine = lax.all_to_all(packed, "dir", 0, 0, tiled=True)
    lists = shape(2 * entries + LIST_ROWS, 128, kind=jnp.int32)
    up, down = shape(width, 2 * unknowns, kind=BF16), shape(2 * unknowns, width, kind=BF16)
    planned = call(plan_kernel, (lists, lists, up, up, down, down), (VMEM,) * 4, name="plan")(
        inter_source.T, inter_shift.T, aggregate, disaggregate
    )
    mine, beside, planned = lax.optimization_barrier((mine, currents, planned))
    early, late, up0, up1, down0, down1 = planned
    sent = mine[:, :rows]
    from_cross = lax.ppermute(sent, "slab", cross)
    from_same = lax.ppermute(sent, "slab", same)
    left = lax.ppermute(beside, "dir", ring)
    right = lax.ppermute(beside, "dir", [(j, i) for i, j in ring])
    field = shape(boxes, own, width)
    radiated, table = call(own_kernel, (field, shape(ops, own, width)), (VMEM,) * 3, micros=0, name="own")(mine, up0, up1)
    staging = (pltpu.SMEM(lists.shape, jnp.int32), pltpu.SemaphoreType.DMA)
    partial, near_fields = call(
        mid_kernel,
        (field, shape(2 * boxes + 1, own, width)),
        (VMEM,) * 6,
        scratch=staging,
        micros=0,
        name="mid",
    )(early, radiated, table, from_same, up0, up1)
    far = call(
        far_kernel,
        shape(devices, rows, unknowns),
        (VMEM,) * 9,
        scratch=(
            pltpu.VMEM((3 * boxes, own, width), F32),
            pltpu.VMEM((boxes, own, width), F32),
            pltpu.VMEM((devices, rows, unknowns), F32),
            pltpu.SemaphoreType.DMA((PARTS,)),
            *staging,
        ),
        micros=0,
        name="far",
        out_kind=ANY,
    )(late, partial, near_fields, table, from_cross, up0, up1, down0, down1)
    back = lax.all_to_all(far, "dir", 0, 0, tiled=True)

    stack = pltpu.VMEM((3 * box_dev, 2 * unknowns, 2 * illum), BF16)
    near = call(
        near_kernel, shape(*currents.shape), (SMEM,) + (VMEM,) * 4, scratch=(stack, stack), micros=20, name="near"
    )(near_index, near_blocks, currents, left, right)
    return call(
        join_kernel,
        shape(*currents.shape),
        (VMEM, VMEM),
        scratch=(blocks, pltpu.SemaphoreType.DMA((pieces,))),
        micros=0,
        name="join",
        out_kind=ANY,
    )(back, near)


def solution(mesh):
    in_specs = (
        P(None, ("slab", "dir"), None, None),
        P(None, ("slab", "dir"), None, None, None),
        P(("slab", "dir"), None),
        P(),
        P(None, None, "dir"),
        P("slab", None),
        P("slab", None),
        P(),
    )
    out_specs = P(None, ("slab", "dir"), None, None)
    return jax.shard_map(body, mesh=mesh, in_specs=in_specs, out_specs=out_specs, check_vma=False)
```

```python
import functools

import jax
import jax.numpy as jnp
from jax import lax
from jax.experimental import pallas as pl
from jax.experimental.pallas import tpu as pltpu
from jax.sharding import PartitionSpec as P

F32, BF16 = jnp.float32, jnp.bfloat16
VMEM = pltpu.MemorySpace.VMEM
SMEM = pltpu.MemorySpace.SMEM
ANY = pl.ANY
MIB = 1 << 20
RE_IM_ROWS = 32
FIRST = 16
PARTS = 2
LIST_ROWS = 8
FULL = 63


def split(x):
    high = x.astype(BF16)
    return high, (x - high.astype(F32)).astype(BF16)


def dot3(left, right, contract):
    def one(a, b):
        return lax.dot_general(a, b, (contract, ((), ())), preferred_element_type=F32)

    return one(left[0], right[0]) + (one(left[0], right[1]) + one(left[1], right[0]))


NN_FORM = ((1,), (0,))
NT_FORM = ((1,), (1,))


def plan_kernel(
    source_ref, shift_ref, aggregate_ref, disaggregate_ref, early_ref, late_ref, up0_ref, up1_ref, down0_ref, down1_ref
):
    up0_ref[...], up1_ref[...] = split(complex_rows(aggregate_ref))
    down0_ref[...], down1_ref[...] = split(complex_rows(disaggregate_ref))
    entries, boxes = source_ref.shape
    odd = lax.axis_index("slab") % 2
    source, shift = source_ref[...], shift_ref[...]
    part, place = source // boxes, source % boxes
    away = part == 2 * odd
    where = jnp.where(part == 1, place, jnp.where(away, 2 * boxes + place, boxes + place))
    one = jnp.where(away, 0, 1)
    near_count = jnp.sum(one, axis=0, keepdims=True)
    row = lax.broadcasted_iota(jnp.int32, (entries, boxes), 0)
    to_near, to_away = jnp.zeros((1, boxes), jnp.int32), near_count
    sorted_where = jnp.zeros((entries, boxes), jnp.int32)
    sorted_shift = jnp.zeros((entries, boxes), jnp.int32)
    for i in range(entries):
        is_near = one[i : i + 1]
        here = row == jnp.where(is_near == 1, to_near, to_away)
        sorted_where = jnp.where(here, where[i : i + 1], sorted_where)
        sorted_shift = jnp.where(here, shift[i : i + 1], sorted_shift)
        to_near, to_away = to_near + is_near, to_away + (1 - is_near)
    for ref in (early_ref, late_ref):
        ref[...] = jnp.zeros(ref.shape, jnp.int32)
        ref[entries : 2 * entries, :boxes] = sorted_shift
    early_ref[:entries, :boxes] = jnp.minimum(sorted_where, 2 * boxes)
    late_ref[:entries, :boxes] = sorted_where
    late_ref[2 * entries : 2 * entries + 1, :boxes] = near_count
    across = [lax.broadcasted_iota(jnp.int32, (boxes, boxes), n) for n in range(2)]
    before, same = (across[1] < across[0]).astype(F32), (across[1] == across[0]).astype(F32)
    lanes = late_ref.shape[1]
    slot = lax.broadcasted_iota(jnp.int32, (boxes, lanes), 1).astype(F32)
    box = lax.broadcasted_iota(jnp.int32, (boxes, lanes), 0).astype(F32)
    few = jnp.broadcast_to((near_count < FIRST).astype(F32), (8, boxes))
    rank = lax.dot_general(before, few, (NT_FORM, ((), ())), preferred_element_type=F32)[:, :1]
    flag = lax.dot_general(same, few, (NT_FORM, ((), ())), preferred_element_type=F32)[:, :1]
    listed = jnp.sum(jnp.where((slot == rank) & (flag > 0.5), box, 0.0), axis=0, keepdims=True)
    late_ref[2 * entries + 1 : 2 * entries + 2, :] = listed.astype(jnp.int32)
    total = jnp.sum(few, axis=1, keepdims=True)[:1]
    late_ref[2 * entries + 2 : 2 * entries + 3, :] = jnp.broadcast_to(total, (1, lanes)).astype(jnp.int32)


def pack_kernel(currents_ref, translations_ref, out_ref, block_ref, table_ref, packed_ref, in_sem, out_sem):
    devices, rows, lanes = out_ref.shape
    parts, boxes, _, illum = currents_ref.shape
    own = illum // devices
    pieces = [(c, b) for c in range(parts) for b in range(boxes)]
    last = len(pieces)
    loads = [pltpu.make_async_copy(currents_ref.at[c, b], block_ref.at[n], in_sem.at[n]) for n, (c, b) in enumerate(pieces)]
    loads.append(pltpu.make_async_copy(translations_ref, table_ref, in_sem.at[last]))
    stores = [
        pltpu.make_async_copy(packed_ref.at[:, pl.ds(n * own, own), :], out_ref.at[:, pl.ds(n * own, own), :], out_sem.at[n])
        for n in range(last + 1)
    ]
    for load in [loads[last], *loads[:last]]:
        load.start()
    loads[last].wait()
    table = jnp.concatenate([table_ref[0], table_ref[1]], axis=1)
    packed_ref[:, last * own :, :] = jnp.broadcast_to(table[None], (devices, own, lanes))
    stores[last].start()
    for n in range(last):
        loads[n].wait()
        packed_ref[:, n * own : (n + 1) * own, :] = block_ref[n].T.reshape(devices, own, lanes)
        stores[n].start()
    for store in stores:
        store.wait()


def near_kernel(index_ref, blocks_ref, own_ref, left_ref, right_ref, out_ref, high_ref, low_ref):
    boxes, entries = blocks_ref.shape[1], blocks_ref.shape[2]
    width = own_ref.shape[3]
    for place, ref in enumerate((left_ref, own_ref, right_ref)):
        for b in range(boxes):
            slot = place * boxes + b
            real, imag = split(ref[0, b]), split(ref[1, b])
            for store, x, y in ((high_ref, real[0], imag[0]), (low_ref, real[1], imag[1])):
                store[slot] = jnp.concatenate(
                    [jnp.concatenate([x, y], axis=1), jnp.concatenate([-y, x], axis=1)], axis=0
                )
    for b in range(boxes):

        def step(j, total):
            source = index_ref[b, j]
            block = split(jnp.concatenate([blocks_ref[0, b, j], blocks_ref[1, b, j]], axis=1))
            return total + dot3(block, (high_ref[source], low_ref[source]), NN_FORM)

        total = lax.fori_loop(0, entries, step, jnp.zeros((blocks_ref.shape[3], 2 * width), F32))
        out_ref[0, b] = total[:, :width]
        out_ref[1, b] = total[:, width:]


def radiate(block_ref, weights):
    devices, rows, lanes = block_ref.shape
    half = RE_IM_ROWS // 2
    real = block_ref[:, :half, :].reshape(devices * half, lanes)
    imag = block_ref[:, half : 2 * half, :].reshape(devices * half, lanes)
    return dot3(split(jnp.concatenate([real, imag], axis=1)), weights, NT_FORM)


def complex_rows(ref):
    real, imag = ref[0], ref[1]
    return jnp.concatenate(
        [jnp.concatenate([real, -imag], axis=1), jnp.concatenate([imag, real], axis=1)], axis=0
    )


def own_kernel(own_ref, up0_ref, up1_ref, radiated_ref, table_ref):
    boxes, sub, width = radiated_ref.shape
    radiated_ref[...] = radiate(own_ref, (up0_ref[...], up1_ref[...])).reshape(boxes, sub, width)
    devices, rows, lanes = own_ref.shape
    table = own_ref[:, RE_IM_ROWS:, :].reshape(devices * (rows - RE_IM_ROWS), lanes).T
    half = lanes // 2
    wide = jnp.concatenate([table[:half], table[half:]], axis=1)
    table_ref[...] = jnp.broadcast_to(wide[:, None, :], table_ref.shape)


def add_entries(list_ref, g, numbers, total, radiated_ref, table_ref):
    entries = list_ref.shape[0] // 2 - LIST_ROWS // 2
    half = table_ref.shape[2] // 2
    real, imag = total
    for n in numbers:
        q, t = list_ref[n, g], list_ref[entries + n, g]
        xr, xi = radiated_ref[q, :, :half], radiated_ref[q, :, half:]
        tr, ti = table_ref[t, :, :half], table_ref[t, :, half:]
        real, imag = real + (tr * xr - ti * xi), imag + (tr * xi + ti * xr)
    return real, imag


def add_all(list_ref, numbers, start, out_ref, radiated_ref, table_ref):
    half = table_ref.shape[2] // 2

    def one_box(g, carry):
        total = add_entries(list_ref, g, numbers, start(g), radiated_ref, table_ref)
        out_ref[g, :, :half], out_ref[g, :, half:] = total
        return carry

    lax.fori_loop(0, out_ref.shape[0], one_box, 0, unroll=4)


def mid_kernel(
    lists_ref, own_ref, table_ref, block_ref, up0_ref, up1_ref, out_ref, radiated_ref, list_ref, sem
):
    staged = pltpu.make_async_copy(lists_ref, list_ref, sem)
    staged.start()
    boxes, sub, width = own_ref.shape
    radiated_ref[:boxes] = own_ref[...]
    radiated_ref[boxes : 2 * boxes] = radiate(block_ref, (up0_ref[...], up1_ref[...])).reshape(boxes, sub, width)
    radiated_ref[2 * boxes] = jnp.zeros((sub, width), F32)
    staged.wait()
    nothing = jnp.zeros((sub, width // 2), F32)
    add_all(list_ref, range(FIRST), lambda g: (nothing, nothing), out_ref, radiated_ref, table_ref)


def far_kernel(
    lists_ref, mid_ref, near_ref, table_ref, block_ref, up0_ref, up1_ref, down0_ref, down1_ref, out_ref, radiated_ref,
    incoming_ref, rows_ref, store_sem, list_ref, sem,
):
    staged = pltpu.make_async_copy(lists_ref, list_ref, sem)
    staged.start()
    boxes, sub, width = mid_ref.shape
    half = width // 2
    entries = list_ref.shape[0] // 2 - LIST_ROWS // 2
    radiated_ref[: 2 * boxes] = near_ref[: 2 * boxes]
    radiated_ref[2 * boxes :] = radiate(block_ref, (up0_ref[...], up1_ref[...])).reshape(boxes, sub, width)
    staged.wait()
    rest = range(FIRST, entries)
    add_all(
        list_ref, rest, lambda g: (mid_ref[g, :, :half], mid_ref[g, :, half:]), incoming_ref, radiated_ref, table_ref
    )

    def skipped(place, carry):
        g = list_ref[2 * entries + 1, place]

        def one(n, total):
            return add_entries(list_ref, g, (n,), total, radiated_ref, table_ref)

        both = (incoming_ref[g, :, :half], incoming_ref[g, :, half:])
        both = lax.fori_loop(list_ref[2 * entries, g], FIRST, one, both)
        incoming_ref[g, :, :half], incoming_ref[g, :, half:] = both
        return carry

    lax.fori_loop(0, list_ref[2 * entries + 2, 0], skipped, 0)
    down = down0_ref[...], down1_ref[...]
    devices, rows, lanes = out_ref.shape
    half_rows, some, batch = rows // 2, devices // PARTS, boxes // PARTS
    stores = []
    for n in range(PARTS):
        here = pl.ds(n * some, some)
        far = dot3(split(incoming_ref[n * batch : (n + 1) * batch].reshape(batch * sub, width)), down, NT_FORM)
        rows_ref[here, :half_rows, :] = far[:, :lanes].reshape(some, half_rows, lanes)
        rows_ref[here, half_rows:, :] = far[:, lanes:].reshape(some, half_rows, lanes)
        stores.append(pltpu.make_async_copy(rows_ref.at[here], out_ref.at[here], store_sem.at[n]))
        stores[n].start()
    for store in stores:
        store.wait()


def join_kernel(far_ref, near_ref, out_ref, sum_ref, sem):
    parts, boxes, lanes, illum = out_ref.shape
    own = illum // far_ref.shape[0]
    stores = []
    for n, (c, b) in enumerate((c, b) for c in range(parts) for b in range(boxes)):
        turned = far_ref[:, n * own : (n + 1) * own, :].reshape(illum, lanes).T
        sum_ref[n] = near_ref[c, b] + turned
        stores.append(pltpu.make_async_copy(sum_ref.at[n], out_ref.at[c, b], sem.at[n]))
        stores[n].start()
    for store in stores:
        store.wait()


def call(kernel, outs, kinds, scratch=(), limit=16, micros=1, name=None, out_kind=VMEM):
    specs = [pl.BlockSpec(memory_space=kind) for kind in kinds]

    def run(*args):
        moved = 4 * sum(a.size for a in (*args, *jax.tree.leaves(outs)))
        return pl.pallas_call(
            kernel,
            out_shape=outs,
            in_specs=specs,
            out_specs=jax.tree.map(lambda _: pl.BlockSpec(memory_space=out_kind), outs),
            scratch_shapes=list(scratch),
            compiler_params=pltpu.CompilerParams(vmem_limit_bytes=limit * MIB),
            cost_estimate=pl.CostEstimate(flops=micros * 1_000_000_000, bytes_accessed=moved, transcendentals=0),
            name=name,
        )(*args)

    return run


def shape(*dims, kind=F32):
    return jax.ShapeDtypeStruct(dims, kind)


def body(currents, near_blocks, near_index, aggregate, translations, inter_source, inter_shift, disaggregate):
    devices = lax.axis_size("dir")
    slabs = lax.axis_size("slab")
    parts, box_dev, unknowns, illum = currents.shape
    own = illum // devices
    width = 2 * aggregate.shape[1]
    boxes, entries = inter_source.shape
    ops = translations.shape[1]
    rows = parts * box_dev * own
    ring = [(i, (i + 1) % devices) for i in range(devices)]
    pairs_of = [[(i, i + 1) for i in range(start, slabs - 1, 2)] for start in (0, 1)]
    same, cross = [p + [(j, i) for i, j in p] for p in pairs_of]

    turned = jnp.transpose(translations, (0, 2, 1))
    pieces = parts * box_dev
    blocks = pltpu.VMEM((pieces, unknowns, illum), F32)
    whole = shape(devices, rows + turned.shape[1], unknowns)
    packed = call(
        pack_kernel,
        whole,
        (ANY, ANY),
        scratch=(
            blocks,
            pltpu.VMEM(turned.shape, F32),
            pltpu.VMEM(whole.shape, F32),
            pltpu.SemaphoreType.DMA((pieces + 1,)),
            pltpu.SemaphoreType.DMA((pieces + 1,)),
        ),
        limit=FULL,
        name="pack",
        out_kind=ANY,
    )(currents, turned)
    mine = lax.all_to_all(packed, "dir", 0, 0, tiled=True)
    lists = shape(2 * entries + LIST_ROWS, 128, kind=jnp.int32)
    up, down = shape(width, 2 * unknowns, kind=BF16), shape(2 * unknowns, width, kind=BF16)
    planned = call(plan_kernel, (lists, lists, up, up, down, down), (VMEM,) * 4, name="plan")(
        inter_source.T, inter_shift.T, aggregate, disaggregate
    )
    mine, beside, planned = lax.optimization_barrier((mine, currents, planned))
    early, late, up0, up1, down0, down1 = planned
    sent = mine[:, :rows]
    from_cross = lax.ppermute(sent, "slab", cross)
    from_same = lax.ppermute(sent, "slab", same)
    field = shape(boxes, own, width)
    radiated, table = call(own_kernel, (field, shape(ops, own, width)), (VMEM,) * 3, micros=0, name="own")(mine, up0, up1)
    staging = (pltpu.SMEM(lists.shape, jnp.int32), pltpu.SemaphoreType.DMA)
    partial, near_fields = call(
        mid_kernel,
        (field, shape(2 * boxes + 1, own, width)),
        (VMEM,) * 6,
        scratch=staging,
        micros=0,
        name="mid",
    )(early, radiated, table, from_same, up0, up1)
    partial, beside = lax.optimization_barrier((partial, beside))
    left = lax.ppermute(beside, "dir", ring)
    right = lax.ppermute(beside, "dir", [(j, i) for i, j in ring])
    far = call(
        far_kernel,
        shape(devices, rows, unknowns),
        (VMEM,) * 9,
        scratch=(
            pltpu.VMEM((3 * boxes, own, width), F32),
            pltpu.VMEM((boxes, own, width), F32),
            pltpu.VMEM((devices, rows, unknowns), F32),
            pltpu.SemaphoreType.DMA((PARTS,)),
            *staging,
        ),
        micros=0,
        name="far",
        out_kind=ANY,
    )(late, partial, near_fields, table, from_cross, up0, up1, down0, down1)
    back = lax.all_to_all(far, "dir", 0, 0, tiled=True)

    stack = pltpu.VMEM((3 * box_dev, 2 * unknowns, 2 * illum), BF16)
    near = call(
        near_kernel, shape(*currents.shape), (SMEM,) + (VMEM,) * 4, scratch=(stack, stack), micros=20, name="near"
    )(near_index, near_blocks, currents, left, right)
    return call(
        join_kernel,
        shape(*currents.shape),
        (VMEM, VMEM),
        scratch=(blocks, pltpu.SemaphoreType.DMA((pieces,))),
        micros=0,
        name="join",
        out_kind=ANY,
    )(back, near)


def solution(mesh):
    in_specs = (
        P(None, ("slab", "dir"), None, None),
        P(None, ("slab", "dir"), None, None, None),
        P(("slab", "dir"), None),
        P(),
        P(None, None, "dir"),
        P("slab", None),
        P("slab", None),
        P(),
    )
    out_specs = P(None, ("slab", "dir"), None, None)
    return jax.shard_map(body, mesh=mesh, in_specs=in_specs, out_specs=out_specs, check_vma=False)
```

```python
import functools

import jax
import jax.numpy as jnp
from jax import lax
from jax.experimental import pallas as pl
from jax.experimental.pallas import tpu as pltpu
from jax.sharding import PartitionSpec as P

F32, BF16 = jnp.float32, jnp.bfloat16
VMEM = pltpu.MemorySpace.VMEM
SMEM = pltpu.MemorySpace.SMEM
ANY = pl.ANY
MIB = 1 << 20
RE_IM_ROWS = 32
FIRST = 16
PARTS = 2
LIST_ROWS = 8
FULL = 63


def split(x):
    high = x.astype(BF16)
    return high, (x - high.astype(F32)).astype(BF16)


def dot3(left, right, contract):
    def one(a, b):
        return lax.dot_general(a, b, (contract, ((), ())), preferred_element_type=F32)

    return one(left[0], right[0]) + (one(left[0], right[1]) + one(left[1], right[0]))


NN_FORM = ((1,), (0,))
NT_FORM = ((1,), (1,))


def plan_kernel(
    source_ref, shift_ref, aggregate_ref, disaggregate_ref, early_ref, late_ref, up0_ref, up1_ref, down0_ref, down1_ref
):
    up0_ref[...], up1_ref[...] = split(complex_rows(aggregate_ref))
    down0_ref[...], down1_ref[...] = split(complex_rows(disaggregate_ref))
    entries, boxes = source_ref.shape
    odd = lax.axis_index("slab") % 2
    source, shift = source_ref[...], shift_ref[...]
    part, place = source // boxes, source % boxes
    away = part == 2 * odd
    where = jnp.where(part == 1, place, jnp.where(away, 2 * boxes + place, boxes + place))
    one = jnp.where(away, 0, 1)
    near_count = jnp.sum(one, axis=0, keepdims=True)
    row = lax.broadcasted_iota(jnp.int32, (entries, boxes), 0)
    to_near, to_away = jnp.zeros((1, boxes), jnp.int32), near_count
    sorted_where = jnp.zeros((entries, boxes), jnp.int32)
    sorted_shift = jnp.zeros((entries, boxes), jnp.int32)
    for i in range(entries):
        is_near = one[i : i + 1]
        here = row == jnp.where(is_near == 1, to_near, to_away)
        sorted_where = jnp.where(here, where[i : i + 1], sorted_where)
        sorted_shift = jnp.where(here, shift[i : i + 1], sorted_shift)
        to_near, to_away = to_near + is_near, to_away + (1 - is_near)
    for ref in (early_ref, late_ref):
        ref[...] = jnp.zeros(ref.shape, jnp.int32)
        ref[entries : 2 * entries, :boxes] = sorted_shift
    early_ref[:entries, :boxes] = jnp.minimum(sorted_where, 2 * boxes)
    late_ref[:entries, :boxes] = sorted_where
    late_ref[2 * entries : 2 * entries + 1, :boxes] = near_count
    across = [lax.broadcasted_iota(jnp.int32, (boxes, boxes), n) for n in range(2)]
    before, same = (across[1] < across[0]).astype(F32), (across[1] == across[0]).astype(F32)
    lanes = late_ref.shape[1]
    slot = lax.broadcasted_iota(jnp.int32, (boxes, lanes), 1).astype(F32)
    box = lax.broadcasted_iota(jnp.int32, (boxes, lanes), 0).astype(F32)
    few = jnp.broadcast_to((near_count < FIRST).astype(F32), (8, boxes))
    rank = lax.dot_general(before, few, (NT_FORM, ((), ())), preferred_element_type=F32)[:, :1]
    flag = lax.dot_general(same, few, (NT_FORM, ((), ())), preferred_element_type=F32)[:, :1]
    listed = jnp.sum(jnp.where((slot == rank) & (flag > 0.5), box, 0.0), axis=0, keepdims=True)
    late_ref[2 * entries + 1 : 2 * entries + 2, :] = listed.astype(jnp.int32)
    total = jnp.sum(few, axis=1, keepdims=True)[:1]
    late_ref[2 * entries + 2 : 2 * entries + 3, :] = jnp.broadcast_to(total, (1, lanes)).astype(jnp.int32)


def pack_kernel(currents_ref, translations_ref, out_ref, block_ref, table_ref, packed_ref, in_sem, out_sem):
    devices, rows, lanes = out_ref.shape
    parts, boxes, _, illum = currents_ref.shape
    own = illum // devices
    pieces = [(c, b) for c in range(parts) for b in range(boxes)]
    last = len(pieces)
    loads = [pltpu.make_async_copy(currents_ref.at[c, b], block_ref.at[n], in_sem.at[n]) for n, (c, b) in enumerate(pieces)]
    loads.append(pltpu.make_async_copy(translations_ref, table_ref, in_sem.at[last]))
    stores = [
        pltpu.make_async_copy(packed_ref.at[:, pl.ds(n * own, own), :], out_ref.at[:, pl.ds(n * own, own), :], out_sem.at[n])
        for n in range(last + 1)
    ]
    for load in [loads[last], *loads[:last]]:
        load.start()
    loads[last].wait()
    table = jnp.concatenate([table_ref[0], table_ref[1]], axis=1)
    packed_ref[:, last * own :, :] = jnp.broadcast_to(table[None], (devices, own, lanes))
    stores[last].start()
    for n in range(last):
        loads[n].wait()
        packed_ref[:, n * own : (n + 1) * own, :] = block_ref[n].T.reshape(devices, own, lanes)
        stores[n].start()
    for store in stores:
        store.wait()


def near_kernel(index_ref, blocks_ref, own_ref, left_ref, right_ref, out_ref, high_ref, low_ref):
    boxes, entries = blocks_ref.shape[1], blocks_ref.shape[2]
    width = own_ref.shape[3]
    for place, ref in enumerate((left_ref, own_ref, right_ref)):
        for b in range(boxes):
            slot = place * boxes + b
            real, imag = split(ref[0, b]), split(ref[1, b])
            for store, x, y in ((high_ref, real[0], imag[0]), (low_ref, real[1], imag[1])):
                store[slot] = jnp.concatenate(
                    [jnp.concatenate([x, y], axis=1), jnp.concatenate([-y, x], axis=1)], axis=0
                )
    for b in range(boxes):

        def step(j, total):
            source = index_ref[b, j]
            block = split(jnp.concatenate([blocks_ref[0, b, j], blocks_ref[1, b, j]], axis=1))
            return total + dot3(block, (high_ref[source], low_ref[source]), NN_FORM)

        total = lax.fori_loop(0, entries, step, jnp.zeros((blocks_ref.shape[3], 2 * width), F32))
        out_ref[0, b] = total[:, :width]
        out_ref[1, b] = total[:, width:]


def radiate(block_ref, weights):
    devices, rows, lanes = block_ref.shape
    half = RE_IM_ROWS // 2
    real = block_ref[:, :half, :].reshape(devices * half, lanes)
    imag = block_ref[:, half : 2 * half, :].reshape(devices * half, lanes)
    return dot3(split(jnp.concatenate([real, imag], axis=1)), weights, NT_FORM)


def complex_rows(ref):
    real, imag = ref[0], ref[1]
    return jnp.concatenate(
        [jnp.concatenate([real, -imag], axis=1), jnp.concatenate([imag, real], axis=1)], axis=0
    )


def own_kernel(own_ref, up0_ref, up1_ref, radiated_ref, table_ref):
    boxes, sub, width = radiated_ref.shape
    radiated_ref[...] = radiate(own_ref, (up0_ref[...], up1_ref[...])).reshape(boxes, sub, width)
    devices, rows, lanes = own_ref.shape
    table = own_ref[:, RE_IM_ROWS:, :].reshape(devices * (rows - RE_IM_ROWS), lanes).T
    half = lanes // 2
    wide = jnp.concatenate([table[:half], table[half:]], axis=1)
    table_ref[...] = jnp.broadcast_to(wide[:, None, :], table_ref.shape)


def add_entries(list_ref, g, numbers, total, radiated_ref, table_ref):
    entries = list_ref.shape[0] // 2 - LIST_ROWS // 2
    half = table_ref.shape[2] // 2
    real, imag = total
    for n in numbers:
        q, t = list_ref[n, g], list_ref[entries + n, g]
        xr, xi = radiated_ref[q, :, :half], radiated_ref[q, :, half:]
        tr, ti = table_ref[t, :, :half], table_ref[t, :, half:]
        real, imag = real + (tr * xr - ti * xi), imag + (tr * xi + ti * xr)
    return real, imag


def add_all(list_ref, numbers, start, out_ref, radiated_ref, table_ref):
    half = table_ref.shape[2] // 2

    def one_box(g, carry):
        total = add_entries(list_ref, g, numbers, start(g), radiated_ref, table_ref)
        out_ref[g, :, :half], out_ref[g, :, half:] = total
        return carry

    lax.fori_loop(0, out_ref.shape[0], one_box, 0, unroll=8)


def mid_kernel(
    lists_ref, own_ref, table_ref, block_ref, up0_ref, up1_ref, out_ref, radiated_ref, list_ref, sem
):
    staged = pltpu.make_async_copy(lists_ref, list_ref, sem)
    staged.start()
    boxes, sub, width = own_ref.shape
    radiated_ref[:boxes] = own_ref[...]
    radiated_ref[boxes : 2 * boxes] = radiate(block_ref, (up0_ref[...], up1_ref[...])).reshape(boxes, sub, width)
    radiated_ref[2 * boxes] = jnp.zeros((sub, width), F32)
    staged.wait()
    nothing = jnp.zeros((sub, width // 2), F32)
    add_all(list_ref, range(FIRST), lambda g: (nothing, nothing), out_ref, radiated_ref, table_ref)


def far_kernel(
    lists_ref, mid_ref, near_ref, table_ref, block_ref, up0_ref, up1_ref, down0_ref, down1_ref, out_ref, radiated_ref,
    incoming_ref, rows_ref, store_sem, list_ref, sem,
):
    staged = pltpu.make_async_copy(lists_ref, list_ref, sem)
    staged.start()
    boxes, sub, width = mid_ref.shape
    half = width // 2
    entries = list_ref.shape[0] // 2 - LIST_ROWS // 2
    radiated_ref[: 2 * boxes] = near_ref[: 2 * boxes]
    radiated_ref[2 * boxes :] = radiate(block_ref, (up0_ref[...], up1_ref[...])).reshape(boxes, sub, width)
    staged.wait()
    rest = range(FIRST, entries)
    add_all(
        list_ref, rest, lambda g: (mid_ref[g, :, :half], mid_ref[g, :, half:]), incoming_ref, radiated_ref, table_ref
    )

    def skipped(place, carry):
        g = list_ref[2 * entries + 1, place]

        def one(n, total):
            return add_entries(list_ref, g, (n,), total, radiated_ref, table_ref)

        both = (incoming_ref[g, :, :half], incoming_ref[g, :, half:])
        both = lax.fori_loop(list_ref[2 * entries, g], FIRST, one, both)
        incoming_ref[g, :, :half], incoming_ref[g, :, half:] = both
        return carry

    lax.fori_loop(0, list_ref[2 * entries + 2, 0], skipped, 0)
    down = down0_ref[...], down1_ref[...]
    devices, rows, lanes = out_ref.shape
    half_rows, some, batch = rows // 2, devices // PARTS, boxes // PARTS
    stores = []
    for n in range(PARTS):
        here = pl.ds(n * some, some)
        far = dot3(split(incoming_ref[n * batch : (n + 1) * batch].reshape(batch * sub, width)), down, NT_FORM)
        rows_ref[here, :half_rows, :] = far[:, :lanes].reshape(some, half_rows, lanes)
        rows_ref[here, half_rows:, :] = far[:, lanes:].reshape(some, half_rows, lanes)
        stores.append(pltpu.make_async_copy(rows_ref.at[here], out_ref.at[here], store_sem.at[n]))
        stores[n].start()
    for store in stores:
        store.wait()


def join_kernel(far_ref, near_ref, out_ref, sum_ref, sem):
    parts, boxes, lanes, illum = out_ref.shape
    own = illum // far_ref.shape[0]
    stores = []
    for n, (c, b) in enumerate((c, b) for c in range(parts) for b in range(boxes)):
        turned = far_ref[:, n * own : (n + 1) * own, :].reshape(illum, lanes).T
        sum_ref[n] = near_ref[c, b] + turned
        stores.append(pltpu.make_async_copy(sum_ref.at[n], out_ref.at[c, b], sem.at[n]))
        stores[n].start()
    for store in stores:
        store.wait()


def call(kernel, outs, kinds, scratch=(), limit=16, micros=1, name=None, out_kind=VMEM):
    specs = [pl.BlockSpec(memory_space=kind) for kind in kinds]

    def run(*args):
        moved = 4 * sum(a.size for a in (*args, *jax.tree.leaves(outs)))
        return pl.pallas_call(
            kernel,
            out_shape=outs,
            in_specs=specs,
            out_specs=jax.tree.map(lambda _: pl.BlockSpec(memory_space=out_kind), outs),
            scratch_shapes=list(scratch),
            compiler_params=pltpu.CompilerParams(vmem_limit_bytes=limit * MIB),
            cost_estimate=pl.CostEstimate(flops=micros * 1_000_000_000, bytes_accessed=moved, transcendentals=0),
            name=name,
        )(*args)

    return run


def shape(*dims, kind=F32):
    return jax.ShapeDtypeStruct(dims, kind)


def body(currents, near_blocks, near_index, aggregate, translations, inter_source, inter_shift, disaggregate):
    devices = lax.axis_size("dir")
    slabs = lax.axis_size("slab")
    parts, box_dev, unknowns, illum = currents.shape
    own = illum // devices
    width = 2 * aggregate.shape[1]
    boxes, entries = inter_source.shape
    ops = translations.shape[1]
    rows = parts * box_dev * own
    ring = [(i, (i + 1) % devices) for i in range(devices)]
    pairs_of = [[(i, i + 1) for i in range(start, slabs - 1, 2)] for start in (0, 1)]
    same, cross = [p + [(j, i) for i, j in p] for p in pairs_of]

    turned = jnp.transpose(translations, (0, 2, 1))
    pieces = parts * box_dev
    blocks = pltpu.VMEM((pieces, unknowns, illum), F32)
    whole = shape(devices, rows + turned.shape[1], unknowns)
    packed = call(
        pack_kernel,
        whole,
        (ANY, ANY),
        scratch=(
            blocks,
            pltpu.VMEM(turned.shape, F32),
            pltpu.VMEM(whole.shape, F32),
            pltpu.SemaphoreType.DMA((pieces + 1,)),
            pltpu.SemaphoreType.DMA((pieces + 1,)),
        ),
        limit=FULL,
        name="pack",
        out_kind=ANY,
    )(currents, turned)
    mine = lax.all_to_all(packed, "dir", 0, 0, tiled=True)
    lists = shape(2 * entries + LIST_ROWS, 128, kind=jnp.int32)
    up, down = shape(width, 2 * unknowns, kind=BF16), shape(2 * unknowns, width, kind=BF16)
    planned = call(plan_kernel, (lists, lists, up, up, down, down), (VMEM,) * 4, name="plan")(
        inter_source.T, inter_shift.T, aggregate, disaggregate
    )
    mine, beside, planned = lax.optimization_barrier((mine, currents, planned))
    early, late, up0, up1, down0, down1 = planned
    sent = mine[:, :rows]
    from_cross = lax.ppermute(sent, "slab", cross)
    from_same = lax.ppermute(sent, "slab", same)
    left = lax.ppermute(beside, "dir", ring)
    right = lax.ppermute(beside, "dir", [(j, i) for i, j in ring])
    field = shape(boxes, own, width)
    radiated, table = call(own_kernel, (field, shape(ops, own, width)), (VMEM,) * 3, micros=0, name="own")(mine, up0, up1)
    staging = (pltpu.SMEM(lists.shape, jnp.int32), pltpu.SemaphoreType.DMA)
    partial, near_fields = call(
        mid_kernel,
        (field, shape(2 * boxes + 1, own, width)),
        (VMEM,) * 6,
        scratch=staging,
        micros=0,
        name="mid",
    )(early, radiated, table, from_same, up0, up1)
    far = call(
        far_kernel,
        shape(devices, rows, unknowns),
        (VMEM,) * 9,
        scratch=(
            pltpu.VMEM((3 * boxes, own, width), F32),
            pltpu.VMEM((boxes, own, width), F32),
            pltpu.VMEM((devices, rows, unknowns), F32),
            pltpu.SemaphoreType.DMA((PARTS,)),
            *staging,
        ),
        micros=0,
        name="far",
        out_kind=ANY,
    )(late, partial, near_fields, table, from_cross, up0, up1, down0, down1)
    back = lax.all_to_all(far, "dir", 0, 0, tiled=True)

    stack = pltpu.VMEM((3 * box_dev, 2 * unknowns, 2 * illum), BF16)
    near = call(
        near_kernel, shape(*currents.shape), (SMEM,) + (VMEM,) * 4, scratch=(stack, stack), micros=20, name="near"
    )(near_index, near_blocks, currents, left, right)
    return call(
        join_kernel,
        shape(*currents.shape),
        (VMEM, VMEM),
        scratch=(blocks, pltpu.SemaphoreType.DMA((pieces,))),
        micros=0,
        name="join",
        out_kind=ANY,
    )(back, near)


def solution(mesh):
    in_specs = (
        P(None, ("slab", "dir"), None, None),
        P(None, ("slab", "dir"), None, None, None),
        P(("slab", "dir"), None),
        P(),
        P(None, None, "dir"),
        P("slab", None),
        P("slab", None),
        P(),
    )
    out_specs = P(None, ("slab", "dir"), None, None)
    return jax.shard_map(body, mesh=mesh, in_specs=in_specs, out_specs=out_specs, check_vma=False)
```

```python
import functools

import jax
import jax.numpy as jnp
from jax import lax
from jax.experimental import pallas as pl
from jax.experimental.pallas import tpu as pltpu
from jax.sharding import PartitionSpec as P

F32, BF16 = jnp.float32, jnp.bfloat16
VMEM = pltpu.MemorySpace.VMEM
SMEM = pltpu.MemorySpace.SMEM
ANY = pl.ANY
MIB = 1 << 20
RE_IM_ROWS = 32
FIRST = 17
PARTS = 2
LIST_ROWS = 8
FULL = 63


def split(x):
    high = x.astype(BF16)
    return high, (x - high.astype(F32)).astype(BF16)


def dot3(left, right, contract):
    def one(a, b):
        return lax.dot_general(a, b, (contract, ((), ())), preferred_element_type=F32)

    return one(left[0], right[0]) + (one(left[0], right[1]) + one(left[1], right[0]))


NN_FORM = ((1,), (0,))
NT_FORM = ((1,), (1,))


def plan_kernel(
    source_ref, shift_ref, aggregate_ref, disaggregate_ref, early_ref, late_ref, up0_ref, up1_ref, down0_ref, down1_ref
):
    up0_ref[...], up1_ref[...] = split(complex_rows(aggregate_ref))
    down0_ref[...], down1_ref[...] = split(complex_rows(disaggregate_ref))
    entries, boxes = source_ref.shape
    odd = lax.axis_index("slab") % 2
    source, shift = source_ref[...], shift_ref[...]
    part, place = source // boxes, source % boxes
    away = part == 2 * odd
    where = jnp.where(part == 1, place, jnp.where(away, 2 * boxes + place, boxes + place))
    one = jnp.where(away, 0, 1)
    near_count = jnp.sum(one, axis=0, keepdims=True)
    row = lax.broadcasted_iota(jnp.int32, (entries, boxes), 0)
    to_near, to_away = jnp.zeros((1, boxes), jnp.int32), near_count
    sorted_where = jnp.zeros((entries, boxes), jnp.int32)
    sorted_shift = jnp.zeros((entries, boxes), jnp.int32)
    for i in range(entries):
        is_near = one[i : i + 1]
        here = row == jnp.where(is_near == 1, to_near, to_away)
        sorted_where = jnp.where(here, where[i : i + 1], sorted_where)
        sorted_shift = jnp.where(here, shift[i : i + 1], sorted_shift)
        to_near, to_away = to_near + is_near, to_away + (1 - is_near)
    for ref in (early_ref, late_ref):
        ref[...] = jnp.zeros(ref.shape, jnp.int32)
        ref[entries : 2 * entries, :boxes] = sorted_shift
    early_ref[:entries, :boxes] = jnp.minimum(sorted_where, 2 * boxes)
    late_ref[:entries, :boxes] = sorted_where
    late_ref[2 * entries : 2 * entries + 1, :boxes] = near_count
    across = [lax.broadcasted_iota(jnp.int32, (boxes, boxes), n) for n in range(2)]
    before, same = (across[1] < across[0]).astype(F32), (across[1] == across[0]).astype(F32)
    lanes = late_ref.shape[1]
    slot = lax.broadcasted_iota(jnp.int32, (boxes, lanes), 1).astype(F32)
    box = lax.broadcasted_iota(jnp.int32, (boxes, lanes), 0).astype(F32)
    few = jnp.broadcast_to((near_count < FIRST).astype(F32), (8, boxes))
    rank = lax.dot_general(before, few, (NT_FORM, ((), ())), preferred_element_type=F32)[:, :1]
    flag = lax.dot_general(same, few, (NT_FORM, ((), ())), preferred_element_type=F32)[:, :1]
    listed = jnp.sum(jnp.where((slot == rank) & (flag > 0.5), box, 0.0), axis=0, keepdims=True)
    late_ref[2 * entries + 1 : 2 * entries + 2, :] = listed.astype(jnp.int32)
    total = jnp.sum(few, axis=1, keepdims=True)[:1]
    late_ref[2 * entries + 2 : 2 * entries + 3, :] = jnp.broadcast_to(total, (1, lanes)).astype(jnp.int32)


def pack_kernel(currents_ref, translations_ref, out_ref, block_ref, table_ref, packed_ref, in_sem, out_sem):
    devices, rows, lanes = out_ref.shape
    parts, boxes, _, illum = currents_ref.shape
    own = illum // devices
    pieces = [(c, b) for c in range(parts) for b in range(boxes)]
    last = len(pieces)
    loads = [pltpu.make_async_copy(currents_ref.at[c, b], block_ref.at[n], in_sem.at[n]) for n, (c, b) in enumerate(pieces)]
    loads.append(pltpu.make_async_copy(translations_ref, table_ref, in_sem.at[last]))
    stores = [
        pltpu.make_async_copy(packed_ref.at[:, pl.ds(n * own, own), :], out_ref.at[:, pl.ds(n * own, own), :], out_sem.at[n])
        for n in range(last + 1)
    ]
    for load in [loads[last], *loads[:last]]:
        load.start()
    loads[last].wait()
    table = jnp.concatenate([table_ref[0], table_ref[1]], axis=1)
    packed_ref[:, last * own :, :] = jnp.broadcast_to(table[None], (devices, own, lanes))
    stores[last].start()
    for n in range(last):
        loads[n].wait()
        packed_ref[:, n * own : (n + 1) * own, :] = block_ref[n].T.reshape(devices, own, lanes)
        stores[n].start()
    for store in stores:
        store.wait()


def near_kernel(index_ref, blocks_ref, own_ref, left_ref, right_ref, out_ref, high_ref, low_ref):
    boxes, entries = blocks_ref.shape[1], blocks_ref.shape[2]
    width = own_ref.shape[3]
    for place, ref in enumerate((left_ref, own_ref, right_ref)):
        for b in range(boxes):
            slot = place * boxes + b
            real, imag = split(ref[0, b]), split(ref[1, b])
            for store, x, y in ((high_ref, real[0], imag[0]), (low_ref, real[1], imag[1])):
                store[slot] = jnp.concatenate(
                    [jnp.concatenate([x, y], axis=1), jnp.concatenate([-y, x], axis=1)], axis=0
                )
    for b in range(boxes):

        def step(j, total):
            source = index_ref[b, j]
            block = split(jnp.concatenate([blocks_ref[0, b, j], blocks_ref[1, b, j]], axis=1))
            return total + dot3(block, (high_ref[source], low_ref[source]), NN_FORM)

        total = lax.fori_loop(0, entries, step, jnp.zeros((blocks_ref.shape[3], 2 * width), F32))
        out_ref[0, b] = total[:, :width]
        out_ref[1, b] = total[:, width:]


def radiate(block_ref, weights):
    devices, rows, lanes = block_ref.shape
    half = RE_IM_ROWS // 2
    real = block_ref[:, :half, :].reshape(devices * half, lanes)
    imag = block_ref[:, half : 2 * half, :].reshape(devices * half, lanes)
    return dot3(split(jnp.concatenate([real, imag], axis=1)), weights, NT_FORM)


def complex_rows(ref):
    real, imag = ref[0], ref[1]
    return jnp.concatenate(
        [jnp.concatenate([real, -imag], axis=1), jnp.concatenate([imag, real], axis=1)], axis=0
    )


def own_kernel(own_ref, up0_ref, up1_ref, radiated_ref, table_ref):
    boxes, sub, width = radiated_ref.shape
    radiated_ref[...] = radiate(own_ref, (up0_ref[...], up1_ref[...])).reshape(boxes, sub, width)
    devices, rows, lanes = own_ref.shape
    table = own_ref[:, RE_IM_ROWS:, :].reshape(devices * (rows - RE_IM_ROWS), lanes).T
    half = lanes // 2
    wide = jnp.concatenate([table[:half], table[half:]], axis=1)
    table_ref[...] = jnp.broadcast_to(wide[:, None, :], table_ref.shape)


def add_entries(list_ref, g, numbers, total, radiated_ref, table_ref):
    entries = list_ref.shape[0] // 2 - LIST_ROWS // 2
    half = table_ref.shape[2] // 2
    real, imag = total
    for n in numbers:
        q, t = list_ref[n, g], list_ref[entries + n, g]
        xr, xi = radiated_ref[q, :, :half], radiated_ref[q, :, half:]
        tr, ti = table_ref[t, :, :half], table_ref[t, :, half:]
        real, imag = real + (tr * xr - ti * xi), imag + (tr * xi + ti * xr)
    return real, imag


def add_all(list_ref, numbers, start, out_ref, radiated_ref, table_ref):
    half = table_ref.shape[2] // 2

    def one_box(g, carry):
        total = add_entries(list_ref, g, numbers, start(g), radiated_ref, table_ref)
        out_ref[g, :, :half], out_ref[g, :, half:] = total
        return carry

    lax.fori_loop(0, out_ref.shape[0], one_box, 0, unroll=8)


def mid_kernel(
    lists_ref, own_ref, table_ref, block_ref, up0_ref, up1_ref, out_ref, radiated_ref, list_ref, sem
):
    staged = pltpu.make_async_copy(lists_ref, list_ref, sem)
    staged.start()
    boxes, sub, width = own_ref.shape
    radiated_ref[:boxes] = own_ref[...]
    radiated_ref[boxes : 2 * boxes] = radiate(block_ref, (up0_ref[...], up1_ref[...])).reshape(boxes, sub, width)
    radiated_ref[2 * boxes] = jnp.zeros((sub, width), F32)
    staged.wait()
    nothing = jnp.zeros((sub, width // 2), F32)
    add_all(list_ref, range(FIRST), lambda g: (nothing, nothing), out_ref, radiated_ref, table_ref)


def far_kernel(
    lists_ref, mid_ref, near_ref, table_ref, block_ref, up0_ref, up1_ref, down0_ref, down1_ref, out_ref, radiated_ref,
    incoming_ref, rows_ref, store_sem, list_ref, sem,
):
    staged = pltpu.make_async_copy(lists_ref, list_ref, sem)
    staged.start()
    boxes, sub, width = mid_ref.shape
    half = width // 2
    entries = list_ref.shape[0] // 2 - LIST_ROWS // 2
    radiated_ref[: 2 * boxes] = near_ref[: 2 * boxes]
    radiated_ref[2 * boxes :] = radiate(block_ref, (up0_ref[...], up1_ref[...])).reshape(boxes, sub, width)
    staged.wait()
    rest = range(FIRST, entries)
    add_all(
        list_ref, rest, lambda g: (mid_ref[g, :, :half], mid_ref[g, :, half:]), incoming_ref, radiated_ref, table_ref
    )

    def skipped(place, carry):
        g = list_ref[2 * entries + 1, place]

        def one(n, total):
            return add_entries(list_ref, g, (n,), total, radiated_ref, table_ref)

        both = (incoming_ref[g, :, :half], incoming_ref[g, :, half:])
        both = lax.fori_loop(list_ref[2 * entries, g], FIRST, one, both)
        incoming_ref[g, :, :half], incoming_ref[g, :, half:] = both
        return carry

    lax.fori_loop(0, list_ref[2 * entries + 2, 0], skipped, 0)
    down = down0_ref[...], down1_ref[...]
    devices, rows, lanes = out_ref.shape
    half_rows, some, batch = rows // 2, devices // PARTS, boxes // PARTS
    stores = []
    for n in range(PARTS):
        here = pl.ds(n * some, some)
        far = dot3(split(incoming_ref[n * batch : (n + 1) * batch].reshape(batch * sub, width)), down, NT_FORM)
        rows_ref[here, :half_rows, :] = far[:, :lanes].reshape(some, half_rows, lanes)
        rows_ref[here, half_rows:, :] = far[:, lanes:].reshape(some, half_rows, lanes)
        stores.append(pltpu.make_async_copy(rows_ref.at[here], out_ref.at[here], store_sem.at[n]))
        stores[n].start()
    for store in stores:
        store.wait()


def join_kernel(far_ref, near_ref, out_ref, sum_ref, sem):
    parts, boxes, lanes, illum = out_ref.shape
    own = illum // far_ref.shape[0]
    stores = []
    for n, (c, b) in enumerate((c, b) for c in range(parts) for b in range(boxes)):
        turned = far_ref[:, n * own : (n + 1) * own, :].reshape(illum, lanes).T
        sum_ref[n] = near_ref[c, b] + turned
        stores.append(pltpu.make_async_copy(sum_ref.at[n], out_ref.at[c, b], sem.at[n]))
        stores[n].start()
    for store in stores:
        store.wait()


def call(kernel, outs, kinds, scratch=(), limit=16, micros=1, name=None, out_kind=VMEM):
    specs = [pl.BlockSpec(memory_space=kind) for kind in kinds]

    def run(*args):
        moved = 4 * sum(a.size for a in (*args, *jax.tree.leaves(outs)))
        return pl.pallas_call(
            kernel,
            out_shape=outs,
            in_specs=specs,
            out_specs=jax.tree.map(lambda _: pl.BlockSpec(memory_space=out_kind), outs),
            scratch_shapes=list(scratch),
            compiler_params=pltpu.CompilerParams(vmem_limit_bytes=limit * MIB),
            cost_estimate=pl.CostEstimate(flops=micros * 1_000_000_000, bytes_accessed=moved, transcendentals=0),
            name=name,
        )(*args)

    return run


def shape(*dims, kind=F32):
    return jax.ShapeDtypeStruct(dims, kind)


def body(currents, near_blocks, near_index, aggregate, translations, inter_source, inter_shift, disaggregate):
    devices = lax.axis_size("dir")
    slabs = lax.axis_size("slab")
    parts, box_dev, unknowns, illum = currents.shape
    own = illum // devices
    width = 2 * aggregate.shape[1]
    boxes, entries = inter_source.shape
    ops = translations.shape[1]
    rows = parts * box_dev * own
    ring = [(i, (i + 1) % devices) for i in range(devices)]
    pairs_of = [[(i, i + 1) for i in range(start, slabs - 1, 2)] for start in (0, 1)]
    same, cross = [p + [(j, i) for i, j in p] for p in pairs_of]

    turned = jnp.transpose(translations, (0, 2, 1))
    pieces = parts * box_dev
    blocks = pltpu.VMEM((pieces, unknowns, illum), F32)
    whole = shape(devices, rows + turned.shape[1], unknowns)
    packed = call(
        pack_kernel,
        whole,
        (ANY, ANY),
        scratch=(
            blocks,
            pltpu.VMEM(turned.shape, F32),
            pltpu.VMEM(whole.shape, F32),
            pltpu.SemaphoreType.DMA((pieces + 1,)),
            pltpu.SemaphoreType.DMA((pieces + 1,)),
        ),
        limit=FULL,
        name="pack",
        out_kind=ANY,
    )(currents, turned)
    mine = lax.all_to_all(packed, "dir", 0, 0, tiled=True)
    lists = shape(2 * entries + LIST_ROWS, 128, kind=jnp.int32)
    up, down = shape(width, 2 * unknowns, kind=BF16), shape(2 * unknowns, width, kind=BF16)
    planned = call(plan_kernel, (lists, lists, up, up, down, down), (VMEM,) * 4, name="plan")(
        inter_source.T, inter_shift.T, aggregate, disaggregate
    )
    mine, beside, planned = lax.optimization_barrier((mine, currents, planned))
    early, late, up0, up1, down0, down1 = planned
    sent = mine[:, :rows]
    from_cross = lax.ppermute(sent, "slab", cross)
    from_same = lax.ppermute(sent, "slab", same)
    left = lax.ppermute(beside, "dir", ring)
    right = lax.ppermute(beside, "dir", [(j, i) for i, j in ring])
    field = shape(boxes, own, width)
    radiated, table = call(own_kernel, (field, shape(ops, own, width)), (VMEM,) * 3, micros=0, name="own")(mine, up0, up1)
    staging = (pltpu.SMEM(lists.shape, jnp.int32), pltpu.SemaphoreType.DMA)
    partial, near_fields = call(
        mid_kernel,
        (field, shape(2 * boxes + 1, own, width)),
        (VMEM,) * 6,
        scratch=staging,
        micros=0,
        name="mid",
    )(early, radiated, table, from_same, up0, up1)
    far = call(
        far_kernel,
        shape(devices, rows, unknowns),
        (VMEM,) * 9,
        scratch=(
            pltpu.VMEM((3 * boxes, own, width), F32),
            pltpu.VMEM((boxes, own, width), F32),
            pltpu.VMEM((devices, rows, unknowns), F32),
            pltpu.SemaphoreType.DMA((PARTS,)),
            *staging,
        ),
        micros=0,
        name="far",
        out_kind=ANY,
    )(late, partial, near_fields, table, from_cross, up0, up1, down0, down1)
    back = lax.all_to_all(far, "dir", 0, 0, tiled=True)

    stack = pltpu.VMEM((3 * box_dev, 2 * unknowns, 2 * illum), BF16)
    near = call(
        near_kernel, shape(*currents.shape), (SMEM,) + (VMEM,) * 4, scratch=(stack, stack), micros=20, name="near"
    )(near_index, near_blocks, currents, left, right)
    return call(
        join_kernel,
        shape(*currents.shape),
        (VMEM, VMEM),
        scratch=(blocks, pltpu.SemaphoreType.DMA((pieces,))),
        micros=0,
        name="join",
        out_kind=ANY,
    )(back, near)


def solution(mesh):
    in_specs = (
        P(None, ("slab", "dir"), None, None),
        P(None, ("slab", "dir"), None, None, None),
        P(("slab", "dir"), None),
        P(),
        P(None, None, "dir"),
        P("slab", None),
        P("slab", None),
        P(),
    )
    out_specs = P(None, ("slab", "dir"), None, None)
    return jax.shard_map(body, mesh=mesh, in_specs=in_specs, out_specs=out_specs, check_vma=False)
```
